32 devices in a mesh: dp: 4 (over y, x), seq: 8 (over z, core).
Axes of the slice: x: 2, y: 2, z: 4, core: 2. Of those that a mesh axis runs over, the one named last changes fastest.
Arguments:
- tokens: bfloat16 [8, 512, 2048], P('dp', 'seq'), may hold values from -6 to 6
- cotangent: bfloat16 [8, 512, 2048], P('dp', 'seq'), may hold values from -6 to 6
- prefix_len: int32 [8], P('dp'), may hold values from 0 to 511, as said below
- attn_gain: bfloat16 [2048], P(('dp', 'seq')), may hold values from 0.5 to 1.5
- w_query: bfloat16 [2048, 2048], P(('dp', 'seq')), may hold values from -0.125 to 0.125
- w_key: bfloat16 [2048, 512], P(('dp', 'seq')), may hold values from -0.125 to 0.125
- w_value: bfloat16 [2048, 512], P(('dp', 'seq')), may hold values from -0.125 to 0.125
- w_out: bfloat16 [2048, 2048], P(('dp', 'seq')), may hold values from -2 to 2
- mlp_gain: bfloat16 [2048], P(('dp', 'seq')), may hold values from 0.5 to 1.5
- w_gate: bfloat16 [2048, 8192], P(('dp', 'seq')), may hold values from -0.125 to 0.125
- w_up: bfloat16 [2048, 8192], P(('dp', 'seq')), may hold values from -0.125 to 0.125
- w_down: bfloat16 [8192, 2048], P(('dp', 'seq')), may hold values from -0.0625 to 0.0625
Outputs:
- block_out: bfloat16 [8, 512, 2048], P('dp', 'seq')
- input_grad: float32 [8, 512, 2048], P('dp', 'seq')
- attn_gain_grad: float32 [2048], P(('dp', 'seq'))
- w_query_grad: float32 [2048, 2048], P(('dp', 'seq'))
- w_key_grad: float32 [2048, 512], P(('dp', 'seq'))
- w_value_grad: float32 [2048, 512], P(('dp', 'seq'))
- w_out_grad: float32 [2048, 2048], P(('dp', 'seq'))
- mlp_gain_grad: float32 [2048], P(('dp', 'seq'))
- w_gate_grad: float32 [2048, 8192], P(('dp', 'seq'))
- w_up_grad: float32 [2048, 8192], P(('dp', 'seq'))
- w_down_grad: float32 [8192, 2048], P(('dp', 'seq'))
The draws below stay inside these ranges and needn't reach their ends.
Inputs may be any that keep to these rules, and one draw needn't show every extreme that they name: A sequence's first prefix_len positions see one another both ways; some sequence has 0 and some has 511.
All inputs are finite; a program needn't handle non-finite values.
Results may differ from the reference program's by a relative error of at most 0.018.
Values may be sent and summed in bfloat16 or wider, within the bound.
A program may use at most 1.25 GiB of HBM per device.

```python
import math
import jax
import jax.numpy as jnp
from jax import lax

D = 2048
FF = 8192
HEADS = 32
KV_HEADS = 8
HEAD_DIM = 64
SEQS = 8
LEN = 512


def draw_prefix_len(key, part):
    key_base = jax.random.fold_in(key, 11)
    key_values, key_low, key_high = jax.random.split(key_base, 3)
    values = jax.random.randint(key_values, (SEQS,), 0, LEN)
    low_slot = jax.random.randint(key_low, (), 0, SEQS)
    high_slot = (low_slot + 1 + jax.random.randint(key_high, (), 0, SEQS - 1)) % SEQS
    slot_ids = jnp.arange(SEQS)
    values = jnp.where(slot_ids == low_slot, 0, values)
    values = jnp.where(slot_ids == high_slot, LEN - 1, values)
    return values.astype(jnp.int32)


def level_of(stream_key, extent, pieces, least, top_value):
    factor_of = 1.0
    for position, blocks in pieces:
        draws = jax.random.uniform(jax.random.fold_in(jax.random.fold_in(stream_key, 6), position), (blocks,), jnp.float32, least / len(pieces), top_value / len(pieces))
        factor_of = factor_of * jnp.repeat(jnp.exp(draws), extent[position] // blocks).reshape((-1,) + (1,) * (len(extent) - 1 - position))
    return factor_of


def centred(stream_key, shape, width, most, cuts=(), held_as=jnp.bfloat16):
    drawn = width * jax.random.normal(stream_key, shape, jnp.float32)
    if cuts:
        drawn = drawn * level_of(stream_key, shape, cuts, -0.22, 0.18)
    return jnp.clip(drawn, -most, most).astype(held_as)


def setup_inputs(seed: int = 0) -> dict:
    streams_of = jax.random.split(jax.random.key(seed), 13)
    return {
        "tokens": centred(streams_of[0], (SEQS, LEN, D), 1.0, 6.0, ((0, 4), (1, 8))),
        "cotangent": centred(streams_of[1], (SEQS, LEN, D), 1.0, 6.0, ((0, 4), (1, 8))),
        "prefix_len": draw_prefix_len(jax.random.fold_in(streams_of[12], 71), 0),
        "attn_gain": jnp.clip(1.0 + 0.1 * jax.random.normal(streams_of[3], (D,), jnp.float32), 0.5, 1.5).astype(jnp.bfloat16),
        "w_query": centred(streams_of[4], (D, D), D ** -0.5, 0.125, ((0, 32),)),
        "w_key": centred(streams_of[5], (D, KV_HEADS * HEAD_DIM), D ** -0.5, 0.125, ((0, 32),)),
        "w_value": centred(streams_of[6], (D, KV_HEADS * HEAD_DIM), D ** -0.5, 0.125, ((0, 32),)),
        "w_out": centred(streams_of[7], (D, D), (max(D // 256, 1)) ** -0.5, 2.0, ((0, 32),)),
        "mlp_gain": jnp.clip(1.0 + 0.1 * jax.random.normal(streams_of[8], (D,), jnp.float32), 0.5, 1.5).astype(jnp.bfloat16),
        "w_gate": centred(streams_of[9], (D, FF), D ** -0.5, 0.125, ((0, 32),)),
        "w_up": centred(streams_of[10], (D, FF), D ** -0.5, 0.125, ((0, 32),)),
        "w_down": centred(streams_of[11], (FF, D), FF ** -0.5, 0.0625, ((0, 32),)),
    }


EPSILON = 1e-05
THETA = 500000.0
NEGATIVE = -1e+30
PRECISE = lax.Precision.HIGHEST

@jax.custom_vjp
def low(v):
    return lax.optimization_barrier(v.astype(jnp.bfloat16)).astype(jnp.float32)

@jax.custom_vjp
def low_back(v):
    return v

def low_keep(v):
    return (low(v), None)

def low_pass(kept, grad):
    return (grad,)

def back_keep(v):
    return (v, None)

def back_low(kept, grad):
    return (low(grad),)
low.defvjp(low_keep, low_pass)
low_back.defvjp(back_keep, back_low)

def rope_table(positions, head_size):
    half_size = head_size // 2
    index_half = jnp.arange(half_size, dtype=jnp.float32)
    inverse = jnp.power(THETA, -2.0 * index_half / head_size)
    wavelength = 2.0 * math.pi / inverse
    smooth = (8192.0 / wavelength - 1.0) / 3.0
    blended = (1.0 - smooth) * inverse / 32.0 + smooth * inverse
    inverse = jnp.where(wavelength < 2048.0, inverse, jnp.where(wavelength > 8192.0, inverse / 32.0, blended))
    angles = positions.astype(jnp.float32)[:, None] * inverse[None, :]
    cos_table = jnp.concatenate([jnp.cos(angles), jnp.cos(angles)], axis=1)
    sin_table = jnp.concatenate([jnp.sin(angles), jnp.sin(angles)], axis=1)
    return (cos_table, sin_table)

def rotate(values, cos_table, sin_table):
    rows_here = values.shape[0]
    head_size = cos_table.shape[1]
    half_size = head_size // 2
    split_heads = values.reshape(rows_here, -1, head_size)
    turned = jnp.concatenate([-split_heads[:, :, half_size:], split_heads[:, :, :half_size]], axis=2)
    return (split_heads * cos_table[:, None, :] + turned * sin_table[:, None, :]).reshape(rows_here, -1)

def rms_norm(values, gain_vec):
    scale_rows = lax.rsqrt(lax.optimization_barrier(jnp.mean(values * values, axis=-1, keepdims=True)) + EPSILON)
    return values * scale_rows * gain_vec

def product(activation, weight):
    return jnp.dot(activation, weight, precision=PRECISE, preferred_element_type=jnp.float32)

def attend(query_rot, key_rot, value_low, allowed):
    length = query_rot.shape[0]
    groups = HEADS // KV_HEADS
    query_heads = query_rot.reshape(length, KV_HEADS, groups, HEAD_DIM).transpose(1, 2, 0, 3)
    key_heads = key_rot.reshape(length, KV_HEADS, HEAD_DIM).transpose(1, 0, 2)
    value_heads = value_low.reshape(length, KV_HEADS, HEAD_DIM).transpose(1, 0, 2)
    score_scale = 1.0 / math.sqrt(HEAD_DIM)

    def one_head(operands):
        query_group, key_group, value_group = operands
        scores = low_back(jnp.einsum('gqd,kd->gqk', query_group, key_group, precision=PRECISE) * score_scale)
        scores = jnp.where(allowed[None, :, :], scores, NEGATIVE)
        weights = low(jax.nn.softmax(scores, axis=-1))
        return jnp.einsum('gqk,kd->gqd', weights, value_group, precision=PRECISE)
    outputs = lax.map(jax.checkpoint(one_head), (query_heads, key_heads, value_heads))
    return outputs.transpose(2, 0, 1, 3).reshape(length, HEADS * HEAD_DIM)

def decoder_layer(params, sequence, cos_table, sin_table, allowed):
    attn_gain, w_query, w_key, w_value, w_out, mlp_gain, w_gate, w_up, w_down = params
    normed = low(rms_norm(sequence, attn_gain))
    query_rot = low(rotate(low_back(product(normed, w_query)), cos_table, sin_table))
    key_rot = low(rotate(low_back(product(normed, w_key)), cos_table, sin_table))
    value_low = low(low_back(product(normed, w_value)))
    attn_mixed = low(low_back(attend(query_rot, key_rot, value_low, allowed)))
    hidden_state = sequence + low_back(product(attn_mixed, w_out))
    normed_mlp = low(rms_norm(hidden_state, mlp_gain))
    gate_proj = low_back(product(normed_mlp, w_gate))
    up_proj = low_back(product(normed_mlp, w_up))
    activated = low(jax.nn.silu(gate_proj) * up_proj)
    return hidden_state + low_back(product(activated, w_down))

def reference(tokens, cotangent, prefix_len, attn_gain, w_query, w_key, w_value, w_out, mlp_gain, w_gate, w_up, w_down):
    params = tuple((weight.astype(jnp.float32) for weight in (attn_gain, w_query, w_key, w_value, w_out, mlp_gain, w_gate, w_up, w_down)))
    positions = jnp.arange(LEN, dtype=jnp.int32)
    cos_table, sin_table = rope_table(positions, HEAD_DIM)

    def one_sequence(totals, operands):
        sequence, cot_rows, prefix_one = operands
        allowed = (positions[None, :] <= positions[:, None]) | (positions[None, :] < prefix_one)

        def forward(param_set, seq_values):
            return decoder_layer(param_set, seq_values, cos_table, sin_table, allowed)
        result, pullback = jax.vjp(forward, params, sequence.astype(jnp.float32))
        param_grads, seq_grad = pullback(cot_rows.astype(jnp.float32))
        totals = jax.tree.map(lambda total_one, grad_one: total_one + grad_one, totals, param_grads)
        return (totals, (result.astype(jnp.bfloat16), seq_grad))
    zero_grads = jax.tree.map(jnp.zeros_like, params)
    totals, (outputs, input_grads) = lax.scan(one_sequence, zero_grads, (tokens, cotangent, prefix_len))
    return (outputs, input_grads, totals[0], totals[1], totals[2], totals[3], totals[4], totals[5], totals[6], totals[7], totals[8])
```

```python
import math

import jax
import jax.numpy as jnp
from jax import lax
from jax.sharding import PartitionSpec as P

HEADS = 32
KV_HEADS = 8
HEAD_DIM = 64
EPSILON = 1e-05
THETA = 500000.0
NEGATIVE = -1e30
BF16 = jnp.bfloat16
F32 = jnp.float32


def rope_table(positions, head_size):
    half_size = head_size // 2
    index_half = jnp.arange(half_size, dtype=jnp.float32)
    inverse = jnp.power(THETA, -2.0 * index_half / head_size)
    wavelength = 2.0 * math.pi / inverse
    smooth = (8192.0 / wavelength - 1.0) / 3.0
    blended = (1.0 - smooth) * inverse / 32.0 + smooth * inverse
    inverse = jnp.where(
        wavelength < 2048.0, inverse, jnp.where(wavelength > 8192.0, inverse / 32.0, blended)
    )
    angles = positions.astype(jnp.float32)[:, None] * inverse[None, :]
    cos_table = jnp.concatenate([jnp.cos(angles), jnp.cos(angles)], axis=1)
    sin_table = jnp.concatenate([jnp.sin(angles), jnp.sin(angles)], axis=1)
    return (cos_table, sin_table)


def rotate(values, cos_table, sin_table):
    half = HEAD_DIM // 2
    turned = jnp.concatenate([-values[..., half:], values[..., :half]], axis=-1)
    return values * cos_table + turned * sin_table


def rotate_back(gradient, cos_table, sin_table):
    half = HEAD_DIM // 2
    sined = gradient * sin_table
    turned = jnp.concatenate([sined[..., half:], -sined[..., :half]], axis=-1)
    return gradient * cos_table + turned


def rms_norm(values, gain_vec):
    scale_rows = lax.rsqrt(jnp.mean(values * values, axis=-1, keepdims=True) + EPSILON)
    return values * scale_rows * gain_vec


def swiglu(gate_in, up_in):
    return jax.nn.silu(gate_in) * up_in


def nn(a, b):
    return jnp.dot(a, b, preferred_element_type=F32)


def tn(a, b):
    return lax.dot_general(a, b, (((0,), (0,)), ((), ())), preferred_element_type=F32)


def nt(a, b):
    return lax.dot_general(a, b, (((1,), (1,)), ((), ())), preferred_element_type=F32)


def body(
    tokens, cotangent, prefix_len, attn_gain, w_query, w_key, w_value, w_out, mlp_gain, w_gate, w_up, w_down
):
    n_dp = lax.axis_size("dp")
    n_seq = lax.axis_size("seq")
    both = ("dp", "seq")
    micro, span, width = tokens.shape
    shard = w_query.shape[0]
    ff_block = w_down.shape[0]
    length = span * n_seq
    rows = micro * span
    group_heads = HEADS // n_seq
    repeat = max(1, n_seq // KV_HEADS)
    kv_here = max(1, KV_HEADS // n_seq)
    q_cols = group_heads * HEAD_DIM
    kv_cols = kv_here * HEAD_DIM
    s_index = lax.axis_index("seq")

    def spread(blocks):
        cols = blocks.shape[2]
        mine = lax.all_to_all(blocks, "seq", split_axis=0, concat_axis=0, tiled=True)
        return lax.all_gather(mine.reshape(n_seq * shard, cols), "dp", axis=0, tiled=True)

    def kv_blocks(w):
        w = w.reshape(shard, -1, 1, kv_cols)
        w = jnp.broadcast_to(w, (shard, n_seq // repeat, repeat, kv_cols))
        return w.reshape(shard, n_seq, kv_cols)

    qkv_blocks = jnp.concatenate(
        [w_query.reshape(shard, n_seq, q_cols), kv_blocks(w_key), kv_blocks(w_value)], axis=2
    ).transpose(1, 0, 2)
    wqkv = spread(qkv_blocks)

    def ff_blocks(w):
        return (
            w.reshape(shard, n_dp, n_seq, ff_block)
            .transpose(2, 0, 1, 3)
            .reshape(n_seq, shard, n_dp * ff_block)
        )

    gains = lax.all_gather(jnp.stack([attn_gain, mlp_gain]), both, axis=1, tiled=True).astype(F32)
    gain_attn, gain_mlp = gains[0], gains[1]
    w_out_all = lax.all_gather(w_out, both, axis=0, tiled=True)
    wo = lax.dynamic_slice_in_dim(w_out_all, s_index * q_cols, q_cols, 0)
    wg = spread(ff_blocks(w_gate))
    wu = spread(ff_blocks(w_up))
    wd = lax.all_gather(w_down, "dp", axis=0, tiled=True)

    def gather_rows(values):
        return lax.all_gather(values, "seq", axis=0, tiled=True)

    def scatter_rows(values):
        return lax.psum_scatter(
            values.astype(BF16), "seq", scatter_dimension=0, tiled=True
        ).astype(F32)

    tok = tokens.reshape(rows, width).astype(F32)
    cot = cotangent.reshape(rows, width)
    normed = gather_rows(rms_norm(tok, gain_attn).astype(BF16))
    cot_all = gather_rows(cot)

    def heads(values, count):
        return (
            values.reshape(n_seq, micro, span, count, HEAD_DIM)
            .transpose(1, 3, 0, 2, 4)
            .reshape(micro, count, length, HEAD_DIM)
        )

    def unheads(values):
        count = values.shape[1]
        return (
            values.reshape(micro, count, n_seq, span, HEAD_DIM)
            .transpose(2, 0, 3, 1, 4)
            .reshape(n_seq * rows, count * HEAD_DIM)
        )

    positions = jnp.arange(length, dtype=jnp.int32)
    cos_table, sin_table = rope_table(positions, HEAD_DIM)
    scale = 1.0 / math.sqrt(HEAD_DIM)
    qkv = nn(normed, wqkv)
    query = rotate(heads(qkv[:, :q_cols], group_heads), cos_table, sin_table).astype(BF16)
    key = rotate(heads(qkv[:, q_cols : q_cols + kv_cols], kv_here), cos_table, sin_table).astype(BF16)
    value = heads(qkv[:, q_cols + kv_cols :], kv_here).astype(BF16)
    per = group_heads // kv_here
    query = query.reshape(micro, kv_here, per, length, HEAD_DIM)
    allowed = (positions[None, :] <= positions[:, None])[None] | (
        positions[None, None, :] < prefix_len[:, None, None]
    )
    scores = jnp.einsum("mkgqd,mkjd->mkgqj", query, key, preferred_element_type=F32) * scale
    scores = jnp.where(allowed[:, None, None], scores, NEGATIVE)
    probs = jax.nn.softmax(scores, axis=-1)
    probs_low = probs.astype(BF16)
    mixed_heads = jnp.einsum("mkgqj,mkjd->mkgqd", probs_low, value, preferred_element_type=F32)
    mixed = unheads(mixed_heads.reshape(micro, group_heads, length, HEAD_DIM)).astype(BF16)
    hidden = tok + scatter_rows(nn(mixed, wo))

    normed_mlp = gather_rows(rms_norm(hidden, gain_mlp).astype(BF16))
    gate = nn(normed_mlp, wg)
    up = nn(normed_mlp, wu)
    activated = swiglu(gate, up).astype(BF16)
    block_out = (hidden + scatter_rows(nn(activated, wd))).astype(BF16)

    grad_act = nt(cot_all, wd)
    grad_gate, grad_up = jax.vjp(swiglu, gate, up)[1](grad_act)
    grad_gate = grad_gate.astype(BF16)
    grad_up = grad_up.astype(BF16)
    grad_normed_mlp = scatter_rows(nt(grad_gate, wg) + nt(grad_up, wu))
    grad_hidden_part, grad_mlp_gain = jax.vjp(rms_norm, hidden, gain_mlp)[1](grad_normed_mlp)
    grad_hidden = cot.astype(F32) + grad_hidden_part
    branch = gather_rows(grad_hidden.astype(BF16))

    def collect(grad):
        cols = grad.shape[1]
        mine = lax.psum_scatter(grad.astype(BF16), "dp", scatter_dimension=0, tiled=True)
        return lax.all_to_all(
            mine.reshape(n_seq, shard, cols), "seq", split_axis=0, concat_axis=0, tiled=True
        )

    def ff_unblocks(blocks):
        return (
            blocks.reshape(n_seq, shard, n_dp, ff_block)
            .transpose(1, 2, 0, 3)
            .reshape(shard, n_dp * n_seq * ff_block)
            .astype(F32)
        )

    w_gate_grad = ff_unblocks(collect(tn(normed_mlp, grad_gate)))
    w_up_grad = ff_unblocks(collect(tn(normed_mlp, grad_up)))
    w_down_grad = lax.psum_scatter(
        tn(activated, cot_all).astype(BF16), "dp", scatter_dimension=0, tiled=True
    ).astype(F32)

    grad_mixed = heads(nt(branch, wo), group_heads).astype(BF16)
    grad_mixed = grad_mixed.reshape(micro, kv_here, per, length, HEAD_DIM)
    out_grad = tn(mixed, branch).astype(BF16)
    ratio = n_seq // n_dp
    out_blocks = out_grad.reshape(1, n_dp, shard, width)
    slot = lax.broadcasted_iota(jnp.int32, (ratio, 1, 1, 1), 0)
    out_blocks = jnp.where(slot == s_index % ratio, out_blocks, 0).reshape(n_seq, shard, width)
    out_blocks = lax.all_to_all(out_blocks, "seq", split_axis=0, concat_axis=0, tiled=True)
    out_blocks = out_blocks.reshape(n_dp, ratio, shard, width)
    out_blocks = lax.dynamic_index_in_dim(out_blocks, s_index // n_dp, 1, keepdims=False)
    w_out_grad = lax.psum_scatter(
        out_blocks.reshape(n_dp * shard, width), "dp", scatter_dimension=0, tiled=True
    ).astype(F32)

    grad_probs = jnp.einsum("mkgqd,mkjd->mkgqj", grad_mixed, value, preferred_element_type=F32)
    delta = jnp.sum(probs * grad_probs, axis=-1, keepdims=True)
    grad_scores = (probs * (grad_probs - delta)).astype(BF16)
    grad_query = jnp.einsum("mkgqj,mkjd->mkgqd", grad_scores, key, preferred_element_type=F32) * scale
    grad_key = jnp.einsum("mkgqj,mkgqd->mkjd", grad_scores, query, preferred_element_type=F32) * scale
    grad_value = jnp.einsum("mkgqj,mkgqd->mkjd", probs_low, grad_mixed, preferred_element_type=F32)
    grad_query = grad_query.reshape(micro, group_heads, length, HEAD_DIM)
    grad_qkv = jnp.concatenate(
        [
            unheads(rotate_back(grad_query, cos_table, sin_table)),
            unheads(rotate_back(grad_key, cos_table, sin_table)),
            unheads(grad_value),
        ],
        axis=1,
    ).astype(BF16)
    grad_normed = scatter_rows(nt(grad_qkv, wqkv))
    tokens_part, grad_attn_gain = jax.vjp(rms_norm, tok, gain_attn)[1](grad_normed)
    input_grad = grad_hidden + tokens_part

    qkv_grad = collect(tn(normed, grad_qkv)).transpose(1, 0, 2).astype(F32)
    w_query_grad = qkv_grad[:, :, :q_cols].reshape(shard, -1)

    def kv_grad(values):
        return values.reshape(shard, n_seq // repeat, repeat, kv_cols).sum(axis=2).reshape(shard, -1)

    w_key_grad = kv_grad(qkv_grad[:, :, q_cols : q_cols + kv_cols])
    w_value_grad = kv_grad(qkv_grad[:, :, q_cols + kv_cols :])
    gain_grads = lax.psum_scatter(
        jnp.stack([grad_attn_gain, grad_mlp_gain]), both, scatter_dimension=1, tiled=True
    )
    return (
        block_out.reshape(micro, span, width),
        input_grad.reshape(micro, span, width),
        gain_grads[0],
        w_query_grad,
        w_key_grad,
        w_value_grad,
        w_out_grad,
        gain_grads[1],
        w_gate_grad,
        w_up_grad,
        w_down_grad,
    )


def solution(mesh):
    rows = P("dp", "seq", None)
    vec = P(("dp", "seq"))
    mat = P(("dp", "seq"), None)
    in_specs = (rows, rows, P("dp"), vec, mat, mat, mat, mat, vec, mat, mat, mat)
    out_specs = (rows, rows, vec, mat, mat, mat, mat, vec, mat, mat, mat)
    return jax.shard_map(body, mesh=mesh, in_specs=in_specs, out_specs=out_specs, check_vma=False)
```

```python
import functools
import math

import jax
import jax.numpy as jnp
from jax import lax
from jax.experimental import pallas as pl
from jax.experimental.pallas import tpu as pltpu
from jax.sharding import PartitionSpec as P

HEADS = 32
KV_HEADS = 8
HEAD_DIM = 64
EPSILON = 1e-05
THETA = 500000.0
NEGATIVE = -1e30
BF16 = jnp.bfloat16
F32 = jnp.float32
MESH = pl.DeviceIdType.MESH
TILE = 256
QUERY_TILE = 256
VMEM_LIMIT = 60 << 20


def rope_table(positions, head_size):
    half_size = head_size // 2
    index_half = jnp.arange(half_size, dtype=jnp.float32)
    inverse = jnp.power(THETA, -2.0 * index_half / head_size)
    wavelength = 2.0 * math.pi / inverse
    smooth = (8192.0 / wavelength - 1.0) / 3.0
    blended = (1.0 - smooth) * inverse / 32.0 + smooth * inverse
    inverse = jnp.where(
        wavelength < 2048.0, inverse, jnp.where(wavelength > 8192.0, inverse / 32.0, blended)
    )
    angles = positions.astype(jnp.float32)[:, None] * inverse[None, :]
    cos_table = jnp.concatenate([jnp.cos(angles), jnp.cos(angles)], axis=1)
    sin_table = jnp.concatenate([jnp.sin(angles), jnp.sin(angles)], axis=1)
    return (cos_table, sin_table)


def nn(a, b):
    return jnp.dot(a, b, preferred_element_type=F32)


def tn(a, b):
    return lax.dot_general(a, b, (((0,), (0,)), ((), ())), preferred_element_type=F32)


def nt(a, b):
    return lax.dot_general(a, b, (((1,), (1,)), ((), ())), preferred_element_type=F32)


class Line:
    def __init__(self, n_seq):
        self.n_line = n_seq // 2
        self.last = self.n_line - 1
        self.s = lax.axis_index("seq")
        self.c = lax.rem(self.s, 2)
        self.l = lax.div(self.s, 2)
        self.sibling = self.s + 1 - 2 * self.c
        self.right = jnp.minimum(self.s + 2, n_seq - 2 + self.c)
        self.left = jnp.maximum(self.s - 2, self.c)
        self.has_right = self.l < self.last
        self.has_left = self.l > 0

    def greet(self):
        barrier = pltpu.get_barrier_semaphore()
        pl.semaphore_signal(barrier, 1, device_id={"seq": self.sibling}, device_id_type=MESH)

        @pl.when(self.has_right)
        def _():
            pl.semaphore_signal(barrier, 1, device_id={"seq": self.right}, device_id_type=MESH)

        @pl.when(self.has_left)
        def _():
            pl.semaphore_signal(barrier, 1, device_id={"seq": self.left}, device_id_type=MESH)

        pl.semaphore_wait(barrier, jnp.where(self.has_right & self.has_left, 3, 2))

    def order(self, j):
        near = jnp.minimum(self.l, self.last - self.l)
        half = lax.div(j + 1, 2)
        both = jnp.where(lax.rem(j, 2) == 1, self.l - half, self.l + half)
        far = jnp.where(self.l <= self.last - self.l, j, self.last - j)
        return jnp.where(j <= 2 * near, both, far)


def remote(src, dst, send, recv, seq):
    return pltpu.make_async_remote_copy(
        src_ref=src, dst_ref=dst, send_sem=send, recv_sem=recv, device_id={"seq": seq}, device_id_type=MESH
    )


class Gather:
    def __init__(self, line, full, send_z, send_c, recv):
        self.line, self.full, self.send_z, self.send_c, self.recv = line, full, send_z, send_c, recv

    @staticmethod
    def sems(n_seq):
        n_line = n_seq // 2
        return [
            pltpu.SemaphoreType.DMA((n_line + 1,)),
            pltpu.SemaphoreType.DMA((n_line,)),
            pltpu.SemaphoreType.DMA((n_seq,)),
        ]

    def copy(self, index, send, seq):
        return remote(self.full.at[index], self.full.at[index], send, self.recv.at[index], seq)

    def begin(self):
        n = self.line
        pl.when(n.has_right)(lambda: self.copy(n.s, self.send_z.at[n.l], n.right).start())
        pl.when(n.has_left)(lambda: self.copy(n.s, self.send_z.at[n.n_line], n.left).start())
        self.copy(n.s, self.send_c.at[n.l], n.sibling).start()

    def visit(self, chip):
        n = self.line
        mine = 2 * chip + n.c

        @pl.when(chip != n.l)
        def _():
            self.copy(mine, self.send_c.at[chip], n.sibling).wait_recv()
            pl.when((chip < n.l) & n.has_right)(
                lambda: self.copy(mine, self.send_z.at[chip], n.right).start()
            )
            pl.when((chip > n.l) & n.has_left)(
                lambda: self.copy(mine, self.send_z.at[chip], n.left).start()
            )
            self.copy(mine, self.send_c.at[chip], n.sibling).start()

        self.copy(2 * chip + 1 - n.c, self.send_c.at[chip], n.sibling).wait_recv()

    def end(self):
        n = self.line

        @pl.loop(0, n.n_line)
        def _(chip):
            mine = 2 * chip + n.c
            self.copy(mine, self.send_c.at[chip], n.sibling).wait_send()
            pl.when((chip <= n.l) & n.has_right)(
                lambda: self.copy(mine, self.send_z.at[chip], n.right).wait_send()
            )
            pl.when((chip > n.l) & n.has_left)(
                lambda: self.copy(mine, self.send_z.at[chip], n.left).wait_send()
            )

        pl.when(n.has_left)(lambda: self.copy(n.s, self.send_z.at[n.n_line], n.left).wait_send())


class Scatter:
    def __init__(self, line, part, sib, rcv, send_z, send_c, recv_z, recv_c):
        self.line, self.part, self.sib, self.rcv = line, part, sib, rcv
        self.send_z, self.send_c, self.recv_z, self.recv_c = send_z, send_c, recv_z, recv_c

    @staticmethod
    def sems(n_seq):
        n_line = n_seq // 2
        return [
            pltpu.SemaphoreType.DMA((n_line,)),
            pltpu.SemaphoreType.DMA((n_line,)),
            pltpu.SemaphoreType.DMA((n_line + 1,)),
            pltpu.SemaphoreType.DMA((n_line,)),
        ]

    @staticmethod
    def buffers(n_seq, rows, width):
        n_line = n_seq // 2
        return [
            pltpu.VMEM((n_line, rows, width), BF16),
            pltpu.VMEM((n_line + 1, rows, width), BF16),
        ]

    def across(self, chip):
        n = self.line
        return remote(
            self.part.at[2 * chip + 1 - n.c],
            self.sib.at[chip],
            self.send_c.at[chip],
            self.recv_c.at[chip],
            n.sibling,
        )

    def hop(self, chip, slot, seq):
        n = self.line
        return remote(
            self.part.at[2 * chip + n.c],
            self.rcv.at[slot],
            self.send_z.at[chip],
            self.recv_z.at[slot],
            seq,
        )

    def begin(self):
        n = self.line

        @pl.loop(0, n.n_line)
        def _(j):
            half = lax.div(j, 2)
            self.across(jnp.where(lax.rem(j, 2) == 0, n.last - half, half)).start()

    def add(self, chip, source):
        mine = 2 * chip + self.line.c
        self.part[mine] = (self.part[mine].astype(F32) + source.astype(F32)).astype(BF16)

    def step(self, time):
        n = self.line

        @pl.when(n.l <= time)
        def _():
            chip = n.last - time + n.l
            self.across(chip).wait_recv()
            self.add(chip, self.sib[chip])

            @pl.when(n.has_left)
            def _():
                self.hop(chip, chip, n.right).wait_recv()
                self.add(chip, self.rcv[chip])

            self.hop(chip, chip, n.right).start()

        @pl.when(n.last - n.l <= time)
        def _():
            chip = time - n.last + n.l
            self.across(chip).wait_recv()
            self.add(chip, self.sib[chip])

            @pl.when(n.has_right)
            def _():
                self.hop(chip, chip, n.left).wait_recv()
                self.add(chip, self.rcv[chip])

            self.hop(chip, jnp.where(chip == n.l - 1, n.n_line, chip), n.left).start()

    def finish(self, out):
        n = self.line
        mine = 2 * n.l + n.c
        self.across(n.l).wait_recv()
        out[...] = self.part[mine].astype(F32) + self.sib[n.l].astype(F32)

        @pl.when(n.has_left)
        def _():
            self.hop(n.l, n.l, n.right).wait_recv()
            out[...] += self.rcv[n.l].astype(F32)

        @pl.when(n.has_right)
        def _():
            self.hop(n.l, n.n_line, n.left).wait_recv()
            out[...] += self.rcv[n.n_line].astype(F32)

        @pl.loop(0, n.n_line)
        def _(chip):
            self.across(chip).wait_send()
            pl.when(chip > n.l)(lambda: self.hop(chip, chip, n.right).wait_send())
            pl.when(chip < n.l)(lambda: self.hop(chip, chip, n.left).wait_send())


def spread_work(units, slots, index):
    return (units * index // slots, units * (index + 1) // slots)


class Spread:
    def __init__(self, line, n_dp, blocks, dst, own_sem, send_z, send_xy, recv):
        self.line, self.n_dp, self.blocks, self.dst = line, n_dp, blocks, dst
        self.own_sem, self.send_z, self.send_xy, self.recv = own_sem, send_z, send_xy, recv
        self.n_seq = 2 * line.n_line
        self.d = lax.axis_index("dp")

    @staticmethod
    def sems(n_seq, n_dp):
        return [
            pltpu.SemaphoreType.DMA((1,)),
            pltpu.SemaphoreType.DMA((n_seq,)),
            pltpu.SemaphoreType.DMA((n_seq, n_dp)),
            pltpu.SemaphoreType.DMA((n_dp, n_seq)),
        ]

    def hop(self, t):
        n = self.line
        return pltpu.make_async_remote_copy(
            src_ref=self.blocks.at[t],
            dst_ref=self.dst.at[self.d, n.s],
            send_sem=self.send_z.at[t],
            recv_sem=self.recv.at[self.d, n.s],
            device_id={"seq": t},
            device_id_type=MESH,
        )

    def own(self):
        n = self.line
        return pltpu.make_async_copy(self.blocks.at[n.s], self.dst.at[self.d, n.s], self.own_sem.at[0])

    def over(self, source, k, own=False):
        return pltpu.make_async_remote_copy(
            src_ref=self.blocks.at[self.line.s] if own else self.dst.at[self.d, source],
            dst_ref=self.dst.at[self.d, source],
            send_sem=self.send_xy.at[source, k],
            recv_sem=self.recv.at[self.d, source],
            device_id={"dp": lax.rem(self.d + k, self.n_dp)},
            device_id_type=MESH,
        )

    def landed(self, d, source):
        return pltpu.make_async_remote_copy(
            src_ref=self.dst.at[d, source],
            dst_ref=self.dst.at[d, source],
            send_sem=self.send_z.at[0],
            recv_sem=self.recv.at[d, source],
            device_id={"dp": d},
            device_id_type=MESH,
        )

    def begin(self):
        n = self.line

        @pl.loop(1, self.n_seq)
        def _(j):
            self.hop(lax.rem(n.s + j, self.n_seq)).start()

        self.own().start()

    def forward_own(self):
        for k in range(1, self.n_dp):
            self.over(self.line.s, k, True).start()

    def forward(self, first, end):
        n = self.line

        @pl.loop(first, end)
        def _(j):
            source = lax.rem(n.s - j + self.n_seq, self.n_seq)
            self.landed(self.d, source).wait_recv()
            for k in range(1, self.n_dp):
                self.over(source, k).start()

    def arrive(self):
        for k in range(1, self.n_dp):
            owner = lax.rem(self.d + k, self.n_dp)

            @pl.loop(0, self.n_seq)
            def _(source):
                self.landed(owner, source).wait_recv()

        self.own().wait()

    def end(self):
        n = self.line

        @pl.loop(0, self.n_seq)
        def _(j):
            pl.when(j != n.s)(lambda: self.hop(j).wait_send())
            for k in range(1, self.n_dp):
                self.over(j, k).wait_send()


class Copies:
    def __init__(self, n_dp, own, dst, own_sem, send, recv):
        self.n_dp, self.own_ref, self.dst = n_dp, own, dst
        self.own_sem, self.send, self.recv = own_sem, send, recv
        self.d = lax.axis_index("dp")

    @staticmethod
    def sems(n_dp):
        return [
            pltpu.SemaphoreType.DMA((1,)),
            pltpu.SemaphoreType.DMA((n_dp,)),
            pltpu.SemaphoreType.DMA((n_dp,)),
        ]

    def copy(self, k, slot):
        return pltpu.make_async_remote_copy(
            src_ref=self.own_ref,
            dst_ref=self.dst.at[slot],
            send_sem=self.send.at[k],
            recv_sem=self.recv.at[slot],
            device_id={"dp": lax.rem(self.d + k, self.n_dp)},
            device_id_type=MESH,
        )

    def begin(self):
        for k in range(1, self.n_dp):
            self.copy(k, self.d).start()
        pltpu.make_async_copy(self.own_ref, self.dst.at[self.d], self.own_sem.at[0]).start()

    def end(self):
        for k in range(1, self.n_dp):
            self.copy(k, lax.rem(self.d + k, self.n_dp)).wait()
        pltpu.make_async_copy(self.own_ref, self.dst.at[self.d], self.own_sem.at[0]).wait()


class OutRows:
    def __init__(self, line, n_dp, own, dst, own_sem, send_z, send_xy, recv):
        self.line, self.n_dp, self.own_ref, self.dst = line, n_dp, own, dst
        self.own_sem, self.send_z, self.send_xy, self.recv = own_sem, send_z, send_xy, recv
        self.n_seq = 2 * line.n_line
        self.ratio = self.n_seq // n_dp
        self.d = lax.axis_index("dp")
        block = self.d * self.n_seq + line.s
        self.target = lax.div(block, n_dp)
        self.slot = lax.rem(block, n_dp)
        self.source_d = lax.div(line.s, self.ratio)
        self.source_s = lax.rem(line.s, self.ratio) * n_dp

    @staticmethod
    def sems(n_dp):
        return [
            pltpu.SemaphoreType.DMA((1,)),
            pltpu.SemaphoreType.DMA((1,)),
            pltpu.SemaphoreType.DMA((n_dp, n_dp)),
            pltpu.SemaphoreType.DMA((n_dp,)),
        ]

    def hop(self):
        return pltpu.make_async_remote_copy(
            src_ref=self.own_ref,
            dst_ref=self.dst.at[self.slot],
            send_sem=self.send_z.at[0],
            recv_sem=self.recv.at[self.slot],
            device_id={"seq": self.target},
            device_id_type=MESH,
        )

    def own(self):
        return pltpu.make_async_copy(self.own_ref, self.dst.at[self.slot], self.own_sem.at[0])

    def over(self, slot, k):
        return pltpu.make_async_remote_copy(
            src_ref=self.dst.at[slot],
            dst_ref=self.dst.at[slot],
            send_sem=self.send_xy.at[slot, k],
            recv_sem=self.recv.at[slot],
            device_id={"dp": lax.rem(self.d + k, self.n_dp)},
            device_id_type=MESH,
        )

    def begin(self):
        stays = self.target == self.line.s
        pl.when(stays)(lambda: self.own().start())
        pl.when(jnp.logical_not(stays))(lambda: self.hop().start())

    def forward(self):
        @pl.when(self.source_d == self.d)
        def _():
            for slot in range(self.n_dp):
                mine = self.source_s + slot == self.line.s
                pl.when(mine)(lambda: self.own().wait())
                pl.when(jnp.logical_not(mine))(lambda: self.over(slot, 1).wait_recv())
                for k in range(1, self.n_dp):
                    self.over(slot, k).start()

    def arrive(self):
        @pl.when(self.source_d != self.d)
        def _():
            for slot in range(self.n_dp):
                self.over(slot, 1).wait_recv()

    def end(self):
        pl.when(self.target != self.line.s)(lambda: self.hop().wait_send())

        @pl.when(self.source_d == self.d)
        def _():
            for slot in range(self.n_dp):
                for k in range(1, self.n_dp):
                    self.over(slot, k).wait_send()


def greet_all(line, n_dp):
    barrier = pltpu.get_barrier_semaphore()
    n_seq = 2 * line.n_line
    d = lax.axis_index("dp")
    for j in range(1, n_seq):
        pl.semaphore_signal(barrier, 1, device_id={"seq": lax.rem(line.s + j, n_seq)}, device_id_type=MESH)
    for k in range(1, n_dp):
        pl.semaphore_signal(barrier, 1, device_id={"dp": lax.rem(d + k, n_dp)}, device_id_type=MESH)
    pl.semaphore_wait(barrier, n_seq + n_dp - 2)


def turn(values, lanes_low):
    half = HEAD_DIM // 2
    width = values.shape[-1]
    return jnp.where(
        lanes_low, pltpu.roll(values, width - half, values.ndim - 1), pltpu.roll(values, half, values.ndim - 1)
    )


def low_lanes(shape):
    return lax.rem(lax.broadcasted_iota(jnp.int32, shape, len(shape) - 1), HEAD_DIM) < HEAD_DIM // 2


def head_lanes(kv, h, q_cols):
    wide = jnp.concatenate([kv] * (q_cols // (2 * HEAD_DIM)), axis=1).astype(F32)
    swapped = pltpu.roll(wide, HEAD_DIM, 1)
    here = lax.div(lax.broadcasted_iota(jnp.int32, wide.shape, 1), HEAD_DIM) == h
    even = lax.rem(h, 2) == 0
    key = jnp.where(here, jnp.where(even, wide, swapped), 0.0).astype(BF16)
    value = jnp.where(here, jnp.where(even, swapped, wide), 0.0).astype(BF16)
    return key, value


def attention_kernel(
    n_seq, n_dp, prefix_ref, tok_ref, cot_ref, cos_ref, sin_ref, qkvb_hbm, gub_hbm, wo_own, wd_own,
    hidden_ref, nmlp_ref, q_ref, kv_ref, mixed_ref, normed_hbm, cot_hbm, wqkv_hbm, wo_hbm, wgu_hbm, wd_hbm,
    full, cot, wqkv, wo, acc, part, sib, rcv, save_sem, *sems,
):
    n = Line(n_seq)
    rows, width = tok_ref.shape
    micro, length, q_cols = q_ref.shape
    span = rows // micro
    cols_all = wqkv.shape[3]
    pair = 2 * rows
    tok = tok_ref[...].astype(F32)
    full[n.s] = (tok * lax.rsqrt(jnp.mean(tok * tok, axis=1, keepdims=True) + EPSILON)).astype(BF16)
    cot[n.s] = cot_ref[...]

    gather = Gather(n, full, *sems[0:3])
    gather_cot = Gather(n, cot, *sems[3:6])
    scatter = Scatter(n, part, sib, rcv, *sems[6:10])
    qkv_w = Spread(n, n_dp, qkvb_hbm, wqkv, *sems[10:14])
    gu_w = Spread(n, n_dp, gub_hbm, wgu_hbm, *sems[14:18])
    out_w = OutRows(n, n_dp, wo_own, wo, *sems[18:22])
    down_w = Copies(n_dp, wd_own, wd_hbm, *sems[22:25])

    greet_all(n, n_dp)
    qkv_w.begin()
    gather.begin()
    out_w.begin()
    qkv_w.forward_own()
    qkv_w.forward(1, n_seq)
    out_w.forward()
    down_w.begin()
    for j in range(n.n_line):
        gather.visit(n.order(j))
    gu_w.begin()
    gu_w.forward_own()
    qkv_w.arrive()

    saves = [
        pltpu.make_async_copy(full, normed_hbm, save_sem.at[0]),
        pltpu.make_async_copy(wqkv, wqkv_hbm, save_sem.at[1]),
    ]
    for save in saves:
        save.start()

    low = low_lanes((span, cols_all))

    @pl.loop(0, n.n_line)
    def _(chip):
        two = pl.ds(pl.multiple_of(2 * chip, 2), 2)
        value = nn(full[two].reshape(pair, width), wqkv[...].reshape(width, cols_all))
        for core in range(2):
            at = pl.ds(pl.multiple_of((2 * chip + core) * span, span), span)
            cos, sin = cos_ref[at, :], sin_ref[at, :]
            for m in range(micro):
                block = value[(core * micro + m) * span : (core * micro + m + 1) * span]
                turned = (block * cos + turn(block, low) * sin).astype(BF16)
                q_ref[m, at, :] = turned[:, :q_cols]
                kv_ref[m, at, :] = turned[:, q_cols:]

    scale = 1.0 / math.sqrt(HEAD_DIM)
    q_tile = min(length, QUERY_TILE)

    @pl.loop(0, micro)
    def _(m):
        prefix = prefix_ref[m]

        @pl.loop(0, q_cols // HEAD_DIM)
        def _(h):
            key, val = head_lanes(kv_ref[m], h, q_cols)

            @pl.loop(0, length // q_tile)
            def _(i):
                at = pl.ds(pl.multiple_of(i * q_tile, q_tile), q_tile)
                scores = nt(q_ref[m, at, :], key) * scale
                query_pos = i * q_tile + lax.broadcasted_iota(jnp.int32, scores.shape, 0)
                key_pos = lax.broadcasted_iota(jnp.int32, scores.shape, 1)
                scores = jnp.where((key_pos <= query_pos) | (key_pos < prefix), scores, NEGATIVE)
                weights = jnp.exp(scores - jnp.max(scores, axis=1, keepdims=True))
                total = jnp.sum(weights, axis=1, keepdims=True)
                mixed = nn((weights / total).astype(BF16), val)

                @pl.when(h == 0)
                def _():
                    acc[at, :] = mixed

                @pl.when(h > 0)
                def _():
                    acc[at, :] += mixed

        mixed_ref[m] = acc[...].astype(BF16)

    out_w.arrive()
    pltpu.make_async_copy(wo, wo_hbm, save_sem.at[2]).start()
    for m in range(micro):

        @pl.loop(0, width // TILE)
        def _(w):
            cols = pl.ds(pl.multiple_of(w * TILE, TILE), TILE)
            value = nn(mixed_ref[m], wo[:, :, cols].reshape(q_cols, TILE))
            part[:, m * span : (m + 1) * span, cols] = value.astype(BF16).reshape(n_seq, span, TILE)

    scatter.begin()
    gather_cot.begin()
    gather_cot.visit(n.l)
    for time in range(n.last):
        scatter.step(time)
        gather_cot.visit(n.order(time + 1))
        first, end = spread_work(n_seq - 1, n.last, time)
        gu_w.forward(first + 1, end + 1)
    pltpu.make_async_copy(cot, cot_hbm, save_sem.at[3]).start()
    scatter.finish(hidden_ref)
    hidden = hidden_ref[...] + tok_ref[...].astype(F32)
    hidden_ref[...] = hidden
    nmlp_ref[...] = (hidden * lax.rsqrt(jnp.mean(hidden * hidden, axis=1, keepdims=True) + EPSILON)).astype(BF16)
    gu_w.arrive()
    down_w.end()
    for save in saves:
        save.wait()
    pltpu.make_async_copy(wo, wo_hbm, save_sem.at[2]).wait()
    pltpu.make_async_copy(cot, cot_hbm, save_sem.at[3]).wait()
    gather.end()
    gather_cot.end()
    qkv_w.end()
    gu_w.end()
    out_w.end()


def attention_call(prefix, tok, cot, cos, sin, qkvb, gub, wo_own, wd_own, n_seq, n_dp):
    rows, width = tok.shape
    micro = prefix.shape[0]
    length = cos.shape[0]
    shard, qkv_cols = qkvb.shape[1:]
    gu_cols = gub.shape[2]
    q_cols = width // n_seq
    ff_block = wd_own.shape[0]
    every = n_seq * rows
    any_spec = pl.BlockSpec(memory_space=pl.ANY)
    vmem = pl.BlockSpec(memory_space=pltpu.VMEM)
    outs = [
        ((rows, width), F32, vmem),
        ((rows, width), BF16, vmem),
        ((micro, length, q_cols), BF16, vmem),
        ((micro, length, 2 * HEAD_DIM), BF16, vmem),
        ((micro, length, q_cols), BF16, vmem),
        ((n_seq, rows, width), BF16, any_spec),
        ((n_seq, rows, width), BF16, any_spec),
        ((n_dp, n_seq, shard, qkv_cols), BF16, any_spec),
        ((n_dp, shard, width), BF16, any_spec),
        ((n_dp, n_seq, shard, gu_cols), BF16, any_spec),
        ((n_dp, ff_block, width), BF16, any_spec),
    ]
    return pl.pallas_call(
        functools.partial(attention_kernel, n_seq, n_dp),
        out_shape=tuple(jax.ShapeDtypeStruct(s, t) for s, t, _ in outs),
        in_specs=[pl.BlockSpec(memory_space=pltpu.SMEM)] + [vmem] * 4 + [any_spec] * 4,
        out_specs=tuple(spec for _, _, spec in outs),
        scratch_shapes=[
            pltpu.VMEM((n_seq, rows, width), BF16),
            pltpu.VMEM((n_seq, rows, width), BF16),
            pltpu.VMEM((n_dp, n_seq, shard, qkv_cols), BF16),
            pltpu.VMEM((n_dp, shard, width), BF16),
            pltpu.VMEM((length, q_cols), F32),
            pltpu.VMEM((n_seq, rows, width), BF16),
            *Scatter.buffers(n_seq, rows, width),
            pltpu.SemaphoreType.DMA((4,)),
            *Gather.sems(n_seq),
            *Gather.sems(n_seq),
            *Scatter.sems(n_seq),
            *Spread.sems(n_seq, n_dp),
            *Spread.sems(n_seq, n_dp),
            *OutRows.sems(n_dp),
            *Copies.sems(n_dp),
        ],
        compiler_params=pltpu.CompilerParams(
            collective_id=2, has_side_effects=True, vmem_limit_bytes=VMEM_LIMIT
        ),
        cost_estimate=pl.CostEstimate(flops=10**10, bytes_accessed=40 << 20, transcendentals=0),
        name="attention",
    )(prefix, tok, cot, cos, sin, qkvb, gub, wo_own, wd_own)


def mlp_kernel(
    n_seq, x_ref, cot_hbm, wgu_hbm, wd_hbm,
    gnm_ref, pout_hbm, dwg_hbm, dwu_hbm, dwd_hbm,
    full, cot, wgu, wd, act, gg, gu, part, sib, rcv, stage_gu, stage_rows, load_sem, gu_sem, rows_sem, *sems,
):
    n = Line(n_seq)
    rows, width = x_ref.shape
    ff = wd.shape[0]
    pair = 2 * rows
    loads = [
        pltpu.make_async_copy(src, dst, load_sem.at[i])
        for i, (src, dst) in enumerate(
            [(wgu_hbm, wgu), (cot_hbm, cot), (wd_hbm, wd)]
        )
    ]
    for load in loads:
        load.start()
    full[n.s] = x_ref[...]
    n.greet()
    gather = Gather(n, full, *sems[:3])
    scatter = Scatter(n, part, sib, rcv, *sems[3:7])
    gather.begin()
    for load in loads:
        load.wait()

    @pl.loop(0, n.n_line)
    def _(j):
        chip = n.order(j)
        gather.visit(chip)
        at = pl.ds(pl.multiple_of(chip * pair, pair), pair)
        two = pl.ds(pl.multiple_of(2 * chip, 2), 2)

        @pl.loop(0, ff // TILE)
        def _(f):
            cols = pl.ds(pl.multiple_of(f * TILE, TILE), TILE)
            x = full[two].reshape(pair, width)
            gate = nn(x, wgu[:, cols])
            up = nn(x, wgu[:, pl.ds(pl.multiple_of(ff + f * TILE, TILE), TILE)])
            grad = nt(cot[two].reshape(pair, width), wd[cols, :])
            sig = jax.nn.sigmoid(gate)
            silu = gate * sig
            act[at, cols] = (silu * up).astype(BF16)
            gg[at, cols] = (grad * up * (sig + silu * (1.0 - sig))).astype(BF16)
            gu[at, cols] = (grad * silu).astype(BF16)

        @pl.loop(0, width // TILE)
        def _(w):
            cols = pl.ds(pl.multiple_of(w * TILE, TILE), TILE)
            value = nt(gg[at, :], wgu[cols, :ff]) + nt(gu[at, :], wgu[cols, ff:])
            part[two, :, cols] = value.astype(BF16).reshape(2, rows, TILE)

    scatter.begin()

    def gate_up_grads(first, end):
        @pl.loop(first, end)
        def _(w):
            slot = lax.rem(w, 2)
            cols = pl.ds(pl.multiple_of(w * TILE, TILE), TILE)
            x = full[:, :, cols].reshape(n_seq * rows, TILE)
            for i, (src, dst) in enumerate([(gg, dwg_hbm), (gu, dwu_hbm)]):
                copy = pltpu.make_async_copy(
                    stage_gu.at[slot, i], dst.at[cols, :], gu_sem.at[slot, i]
                )
                pl.when(w >= 2)(lambda: copy.wait())
                stage_gu[slot, i] = tn(x, src[...]).astype(BF16)
                copy.start()

    def down_grads(first, end):
        @pl.loop(first, end)
        def _(f):
            slot = lax.rem(f, 2)
            cols = pl.ds(pl.multiple_of(f * TILE, TILE), TILE)
            copy = pltpu.make_async_copy(stage_rows.at[slot], dwd_hbm.at[cols, :], rows_sem.at[slot])
            pl.when(f >= 2)(lambda: copy.wait())
            for w in range(0, width, 2 * TILE):
                span = cot[:, :, w : w + 2 * TILE].reshape(n_seq * rows, 2 * TILE)
                stage_rows[slot, :, w : w + 2 * TILE] = tn(act[:, cols], span).astype(BF16)
            copy.start()

    def out_parts(first, end):
        @pl.loop(first, end)
        def _(chip):
            slot = lax.rem(chip, 2)
            at = pl.ds(pl.multiple_of(chip * pair, pair), pair)
            two = pl.ds(pl.multiple_of(2 * chip, 2), 2)
            copies = [
                pltpu.make_async_copy(
                    stage_rows.at[slot, pl.ds(i * rows, rows)], pout_hbm.at[2 * chip + i], rows_sem.at[slot + 2 + 2 * i]
                )
                for i in range(2)
            ]

            @pl.when(chip >= 2)
            def _():
                for copy in copies:
                    copy.wait()

            for w in range(0, width, 2 * TILE):
                stage_rows[slot, :pair, w : w + 2 * TILE] = nn(act[at, :], wd[:, w : w + 2 * TILE]).astype(BF16)
            for copy in copies:
                copy.start()

    def drain_down():
        for slot in range(2):
            pltpu.make_async_copy(stage_rows.at[slot], dwd_hbm.at[pl.ds(0, TILE), :], rows_sem.at[slot]).wait()

    def drain_out():
        for slot in range(2):
            for i in range(2):
                pltpu.make_async_copy(
                    stage_rows.at[slot, pl.ds(i * rows, rows)], pout_hbm.at[i], rows_sem.at[slot + 2 + 2 * i]
                ).wait()

    def drain_gate_up():
        for slot in range(2):
            for i, dst in enumerate([dwg_hbm, dwu_hbm]):
                pltpu.make_async_copy(stage_gu.at[slot, i], dst.at[pl.ds(0, TILE), :], gu_sem.at[slot, i]).wait()

    last = n.last
    for time in range(last):
        scatter.step(time)
        gate_up_grads(*spread_work(width // TILE, last, time))
        if time == last - 2:
            down_grads(0, ff // TILE)
            drain_down()
        if time == last - 1:
            out_parts(0, n.n_line)
            drain_out()
    drain_gate_up()
    scatter.finish(gnm_ref)
    gather.end()


def mlp_call(x, cot, wgu, wd, n_seq):
    rows, width = x.shape
    ff = wd.shape[0]
    every = n_seq * rows
    any_spec = pl.BlockSpec(memory_space=pl.ANY)
    vmem = pl.BlockSpec(memory_space=pltpu.VMEM)
    return pl.pallas_call(
        functools.partial(mlp_kernel, n_seq),
        out_shape=(
            jax.ShapeDtypeStruct((rows, width), F32),
            jax.ShapeDtypeStruct((n_seq, rows, width), BF16),
            jax.ShapeDtypeStruct((width, ff), BF16),
            jax.ShapeDtypeStruct((width, ff), BF16),
            jax.ShapeDtypeStruct((ff, width), BF16),
        ),
        in_specs=[vmem] + [any_spec] * 3,
        out_specs=(vmem,) + (any_spec,) * 4,
        scratch_shapes=[
            pltpu.VMEM((n_seq, rows, width), BF16),
            pltpu.VMEM((n_seq, rows, width), BF16),
            pltpu.VMEM((width, 2 * ff), BF16),
            pltpu.VMEM((ff, width), BF16),
            pltpu.VMEM((every, ff), BF16),
            pltpu.VMEM((every, ff), BF16),
            pltpu.VMEM((every, ff), BF16),
            pltpu.VMEM((n_seq, rows, width), BF16),
            *Scatter.buffers(n_seq, rows, width),
            pltpu.VMEM((2, 2, TILE, ff), BF16),
            pltpu.VMEM((2, TILE, width), BF16),
            pltpu.SemaphoreType.DMA((3,)),
            pltpu.SemaphoreType.DMA((2, 2)),
            pltpu.SemaphoreType.DMA((6,)),
            *Gather.sems(n_seq),
            *Scatter.sems(n_seq),
        ],
        compiler_params=pltpu.CompilerParams(
            collective_id=1, has_side_effects=True, vmem_limit_bytes=VMEM_LIMIT
        ),
        cost_estimate=pl.CostEstimate(flops=18 * every * width * ff, bytes_accessed=40 << 20, transcendentals=0),
        name="mlp",
    )(x, cot, wgu, wd)


def backward_kernel(
    n_seq, prefix_ref, branch_ref, q_ref, kv_ref, mixed_ref, cos_ref, sin_ref, pout_hbm, normed_hbm, wqkv_hbm, wo_hbm,
    ge_ref, sum_ref, dqkv_ref, dwo_ref,
    full, normed, wqkv, wo, gm, acc_q, acc_k, acc_v, gqkv, part, sib, rcv, sib_o, rcv_o, load_sem, *sems,
):
    n = Line(n_seq)
    rows, width = branch_ref.shape
    micro, length, q_cols = q_ref.shape
    span = rows // micro
    pair = 2 * rows
    loads = [
        pltpu.make_async_copy(src, dst, load_sem.at[i])
        for i, (src, dst) in enumerate(
            [(pout_hbm, part), (wo_hbm, wo), (normed_hbm, normed), (wqkv_hbm, wqkv)]
        )
    ]
    for load in loads:
        load.start()
    full[n.s] = branch_ref[...]
    gather = Gather(n, full, *sems[0:3])
    scatter = Scatter(n, part, sib, rcv, *sems[3:7])
    scatter_out = Scatter(n, part, sib_o, rcv_o, *sems[7:11])
    n.greet()
    gather.begin()
    loads[0].wait()
    scatter_out.begin()
    loads[1].wait()

    for j in range(n.n_line):
        chip = n.order(j)
        gather.visit(chip)
        two = pl.ds(pl.multiple_of(2 * chip, 2), 2)
        value = nt(full[two].reshape(pair, width), wo[...].reshape(q_cols, width)).astype(BF16)
        for core in range(2):
            at = pl.ds(pl.multiple_of((2 * chip + core) * span, span), span)
            for m in range(micro):
                gm[m, at, :] = value[(core * micro + m) * span : (core * micro + m + 1) * span]
        if j < n.last:
            scatter_out.step(j)

    scale = 1.0 / math.sqrt(HEAD_DIM)
    q_tile = min(length, QUERY_TILE)
    low = low_lanes((length, q_cols + 2 * HEAD_DIM))
    loads[2].wait()
    loads[3].wait()

    @pl.loop(0, micro)
    def _(m):
        prefix = prefix_ref[m]
        for ref in (acc_q, acc_k, acc_v):
            ref[...] = jnp.zeros_like(ref)

        @pl.loop(0, q_cols // HEAD_DIM)
        def _(h):
            key, val = head_lanes(kv_ref[m], h, q_cols)
            here = lax.div(lax.broadcasted_iota(jnp.int32, (length, q_cols), 1), HEAD_DIM) == h

            @pl.loop(0, length // q_tile)
            def _(i):
                at = pl.ds(pl.multiple_of(i * q_tile, q_tile), q_tile)
                query, grad = q_ref[m, at, :], gm[m, at, :]
                scores = nt(key, query) * scale
                key_pos = lax.broadcasted_iota(jnp.int32, scores.shape, 0)
                query_pos = i * q_tile + lax.broadcasted_iota(jnp.int32, scores.shape, 1)
                scores = jnp.where((key_pos <= query_pos) | (key_pos < prefix), scores, NEGATIVE)
                weights = jnp.exp(scores - jnp.max(scores, axis=0, keepdims=True))
                probs = weights / jnp.sum(weights, axis=0, keepdims=True)
                grad_probs = nt(val, grad)
                delta = jnp.sum(probs * grad_probs, axis=0, keepdims=True)
                grad_scores = (probs * (grad_probs - delta)).astype(BF16)
                acc_q[at, :] += tn(grad_scores, key)
                acc_k[...] += jnp.where(here, nn(grad_scores, query), 0.0)
                acc_v[...] += jnp.where(here, nn(probs.astype(BF16), grad), 0.0)

        def fold(ref):
            total = ref[:, : 2 * HEAD_DIM]
            for w in range(2 * HEAD_DIM, q_cols, 2 * HEAD_DIM):
                total = total + ref[:, w : w + 2 * HEAD_DIM]
            return total + pltpu.roll(total, HEAD_DIM, 1)

        first = lax.broadcasted_iota(jnp.int32, (length, 2 * HEAD_DIM), 1) < HEAD_DIM
        grads = jnp.concatenate([acc_q[...] * scale, jnp.where(first, fold(acc_k) * scale, fold(acc_v))], axis=1)
        gqkv[m] = (grads * cos_ref[...] - turn(grads, low) * sin_ref[...]).astype(BF16)

    scatter_out.finish(sum_ref)
    for m in range(micro):

        @pl.loop(0, width // TILE)
        def _(w):
            at = pl.ds(pl.multiple_of(w * TILE, TILE), TILE)
            value = nt(gqkv[m], wqkv[at, :])
            part[:, m * span : (m + 1) * span, at] = value.astype(BF16).reshape(n_seq, span, TILE)

    scatter.begin()

    def weight_grads(first, end):
        @pl.loop(first, end)
        def _(w):
            cols = pl.ds(pl.multiple_of(w * TILE, TILE), TILE)
            d_out = jnp.zeros((q_cols, TILE), F32)
            d_qkv = jnp.zeros((TILE, q_cols + 2 * HEAD_DIM), F32)
            for m in range(micro):
                mine = slice(m * span, (m + 1) * span)
                d_out = d_out + tn(mixed_ref[m], full[:, mine, cols].reshape(length, TILE))
                d_qkv = d_qkv + tn(normed[:, mine, cols].reshape(length, TILE), gqkv[m])
            dwo_ref[:, cols] = d_out.astype(BF16)
            dqkv_ref[cols, :] = d_qkv.astype(BF16)

    for time in range(n.last):
        scatter.step(time)
        weight_grads(*spread_work(width // TILE, n.last, time))
    scatter.finish(ge_ref)
    gather.end()


def backward_call(prefix, branch, q, kv, mixed, cos, sin, pout, normed, wqkv, wo, n_seq):
    rows, width = branch.shape
    micro, length, q_cols = q.shape
    qkv_cols = q_cols + 2 * HEAD_DIM
    any_spec = pl.BlockSpec(memory_space=pl.ANY)
    vmem = pl.BlockSpec(memory_space=pltpu.VMEM)
    line_rows = pltpu.VMEM((n_seq, rows, width), BF16)
    return pl.pallas_call(
        functools.partial(backward_kernel, n_seq),
        out_shape=(
            jax.ShapeDtypeStruct((rows, width), F32),
            jax.ShapeDtypeStruct((rows, width), F32),
            jax.ShapeDtypeStruct((width, qkv_cols), BF16),
            jax.ShapeDtypeStruct((q_cols, width), BF16),
        ),
        in_specs=[pl.BlockSpec(memory_space=pltpu.SMEM)] + [vmem] * 6 + [any_spec] * 4,
        out_specs=(vmem,) * 4,
        scratch_shapes=[
            line_rows,
            line_rows,
            pltpu.VMEM((width, qkv_cols), BF16),
            pltpu.VMEM(wo.shape, BF16),
            pltpu.VMEM((micro, length, q_cols), BF16),
            pltpu.VMEM((length, q_cols), F32),
            pltpu.VMEM((length, q_cols), F32),
            pltpu.VMEM((length, q_cols), F32),
            pltpu.VMEM((micro, length, qkv_cols), BF16),
            line_rows,
            *Scatter.buffers(n_seq, rows, width),
            *Scatter.buffers(n_seq, rows, width),
            pltpu.SemaphoreType.DMA((4,)),
            *Gather.sems(n_seq),
            *Scatter.sems(n_seq),
            *Scatter.sems(n_seq),
        ],
        compiler_params=pltpu.CompilerParams(
            collective_id=3, has_side_effects=True, vmem_limit_bytes=VMEM_LIMIT
        ),
        cost_estimate=pl.CostEstimate(flops=10**10, bytes_accessed=40 << 20, transcendentals=0),
        name="backward",
    )(prefix, branch, q, kv, mixed, cos, sin, pout, normed, wqkv, wo)


def body(
    tokens, cotangent, prefix_len, attn_gain, w_query, w_key, w_value, w_out, mlp_gain, w_gate, w_up, w_down
):
    n_dp = lax.axis_size("dp")
    n_seq = lax.axis_size("seq")
    both = ("dp", "seq")
    micro, span, width = tokens.shape
    shard = w_query.shape[0]
    ff_block = w_down.shape[0]
    length = span * n_seq
    rows = micro * span
    repeat = n_seq // KV_HEADS
    q_cols = HEADS // n_seq * HEAD_DIM

    gain_attn, gain_mlp = attn_gain.astype(F32), mlp_gain.astype(F32)

    def kv_blocks(w):
        w = w.reshape(shard, KV_HEADS, 1, HEAD_DIM)
        return jnp.broadcast_to(w, (shard, KV_HEADS, repeat, HEAD_DIM)).reshape(shard, n_seq, HEAD_DIM)

    def scaled(blocks, gain):
        return (blocks.astype(F32) * gain[:, None, None]).astype(BF16).transpose(1, 0, 2)

    qkv_blocks = scaled(
        jnp.concatenate([w_query.reshape(shard, n_seq, q_cols), kv_blocks(w_key), kv_blocks(w_value)], axis=2),
        gain_attn,
    )

    def ff_blocks(w):
        w = w.reshape(shard, n_dp, n_seq, ff_block).transpose(0, 2, 1, 3)
        return w.reshape(shard, n_seq, n_dp * ff_block)

    gu_blocks = scaled(jnp.concatenate([ff_blocks(w_gate), ff_blocks(w_up)], axis=2), gain_mlp)

    cos_one, sin_one = rope_table(jnp.arange(length, dtype=jnp.int32), HEAD_DIM)
    half = HEAD_DIM // 2
    sin_one = jnp.concatenate([-sin_one[:, :half], sin_one[:, half:]], axis=1)
    count = q_cols // HEAD_DIM + 1
    cos = jnp.concatenate([jnp.tile(cos_one, (1, count)), jnp.ones((length, HEAD_DIM), F32)], axis=1)
    sin = jnp.concatenate([jnp.tile(sin_one, (1, count)), jnp.zeros((length, HEAD_DIM), F32)], axis=1)

    tok = tokens.reshape(rows, width)
    cot = cotangent.reshape(rows, width)
    hidden, normed_mlp, q, kv, mixed, normed_all, cot_all, wqkv, wo, wgu, wd = attention_call(
        prefix_len, tok, cot, cos, sin, qkv_blocks, gu_blocks, w_out, w_down, n_seq, n_dp
    )
    ge_mlp, out_part, dwg, dwu, dwd = mlp_call(
        normed_mlp, cot_all, wgu.reshape(width, -1), wd.reshape(-1, width), n_seq
    )

    def norm_back(u, ge):
        r = lax.rsqrt(jnp.mean(u * u, axis=1, keepdims=True) + EPSILON)
        return r * ge - u * (r * r * r * jnp.mean(u * ge, axis=1, keepdims=True)), jnp.sum(ge * u * r, axis=0)

    back, gain_mlp_part = norm_back(hidden, ge_mlp)
    grad_hidden = cot.astype(F32) + back
    ge_attn, out_sum, dqkv, dwo = backward_call(
        prefix_len, grad_hidden.astype(BF16), q, kv, mixed, cos, sin, out_part, normed_all,
        wqkv.reshape(width, -1), wo.reshape(-1, width), n_seq,
    )
    block_out = (hidden + out_sum).astype(BF16)
    back, gain_attn_part = norm_back(tok.astype(F32), ge_attn)
    input_grad = grad_hidden + back

    def collect(grad):
        cols = grad.shape[1]
        mine = lax.psum_scatter(grad, "dp", scatter_dimension=0, tiled=True)
        return lax.all_to_all(
            mine.reshape(n_seq, shard, cols), "seq", split_axis=0, concat_axis=0, tiled=True
        ).astype(F32)

    def ff_unblocks(blocks):
        blocks = blocks * gain_mlp[None, :, None]
        blocks = blocks.reshape(n_seq, shard, n_dp, ff_block).transpose(1, 2, 0, 3)
        return blocks.reshape(shard, n_dp * n_seq * ff_block)

    w_gate_grad = ff_unblocks(collect(dwg))
    w_up_grad = ff_unblocks(collect(dwu))
    w_down_grad = lax.psum_scatter(dwd, "dp", scatter_dimension=0, tiled=True).astype(F32)

    s_index = lax.axis_index("seq")
    ratio = n_seq // n_dp
    out_blocks = dwo.reshape(1, n_dp, shard, width)
    slot = lax.broadcasted_iota(jnp.int32, (ratio, 1, 1, 1), 0)
    out_blocks = jnp.where(slot == s_index % ratio, out_blocks, 0).reshape(n_seq, shard, width)
    out_blocks = lax.all_to_all(out_blocks, "seq", split_axis=0, concat_axis=0, tiled=True)
    out_blocks = out_blocks.reshape(n_dp, ratio, shard, width)
    out_blocks = lax.dynamic_index_in_dim(out_blocks, s_index // n_dp, 1, keepdims=False)
    w_out_grad = lax.psum_scatter(
        out_blocks.reshape(n_dp * shard, width), "dp", scatter_dimension=0, tiled=True
    ).astype(F32)

    qkv_grad = collect(dqkv).transpose(1, 0, 2) * gain_attn[:, None, None]
    w_query_grad = qkv_grad[:, :, :q_cols].reshape(shard, -1)

    def kv_grad(values):
        return values.reshape(shard, KV_HEADS, repeat, HEAD_DIM).sum(axis=2).reshape(shard, -1)

    w_key_grad = kv_grad(qkv_grad[:, :, q_cols : q_cols + HEAD_DIM])
    w_value_grad = kv_grad(qkv_grad[:, :, q_cols + HEAD_DIM :])
    gain_parts = jnp.stack([gain_attn_part, gain_mlp_part], axis=1).reshape(n_dp * n_seq, shard, 2)
    gain_grads = lax.all_to_all(gain_parts, both, split_axis=0, concat_axis=0, tiled=True).sum(axis=0)
    return (
        block_out.reshape(micro, span, width),
        input_grad.reshape(micro, span, width),
        gain_grads[:, 0] / gain_attn,
        w_query_grad,
        w_key_grad,
        w_value_grad,
        w_out_grad,
        gain_grads[:, 1] / gain_mlp,
        w_gate_grad,
        w_up_grad,
        w_down_grad,
    )


def solution(mesh):
    rows = P("dp", "seq", None)
    vec = P(("dp", "seq"))
    mat = P(("dp", "seq"), None)
    in_specs = (rows, rows, P("dp"), vec, mat, mat, mat, mat, vec, mat, mat, mat)
    out_specs = (rows, rows, vec, mat, mat, mat, mat, vec, mat, mat, mat)
    return jax.shard_map(body, mesh=mesh, in_specs=in_specs, out_specs=out_specs, check_vma=False)
```

```python
import functools
import math

import jax
import jax.numpy as jnp
from jax import lax
from jax.experimental import pallas as pl
from jax.experimental.pallas import tpu as pltpu
from jax.sharding import PartitionSpec as P

HEADS = 32
KV_HEADS = 8
HEAD_DIM = 64
EPSILON = 1e-05
THETA = 500000.0
NEGATIVE = -1e30
BF16 = jnp.bfloat16
F32 = jnp.float32
MESH = pl.DeviceIdType.MESH
TILE = 256
QUERY_TILE = 256
VMEM_LIMIT = 60 << 20


def rope_table(positions, head_size):
    half_size = head_size // 2
    index_half = jnp.arange(half_size, dtype=jnp.float32)
    inverse = jnp.power(THETA, -2.0 * index_half / head_size)
    wavelength = 2.0 * math.pi / inverse
    smooth = (8192.0 / wavelength - 1.0) / 3.0
    blended = (1.0 - smooth) * inverse / 32.0 + smooth * inverse
    inverse = jnp.where(
        wavelength < 2048.0, inverse, jnp.where(wavelength > 8192.0, inverse / 32.0, blended)
    )
    angles = positions.astype(jnp.float32)[:, None] * inverse[None, :]
    cos_table = jnp.concatenate([jnp.cos(angles), jnp.cos(angles)], axis=1)
    sin_table = jnp.concatenate([jnp.sin(angles), jnp.sin(angles)], axis=1)
    return (cos_table, sin_table)


def nn(a, b):
    return jnp.dot(a, b, preferred_element_type=F32)


def tn(a, b):
    return lax.dot_general(a, b, (((0,), (0,)), ((), ())), preferred_element_type=F32)


def nt(a, b):
    return lax.dot_general(a, b, (((1,), (1,)), ((), ())), preferred_element_type=F32)


class Line:
    def __init__(self, n_seq):
        self.n_line = n_seq // 2
        self.last = self.n_line - 1
        self.s = lax.axis_index("seq")
        self.c = lax.rem(self.s, 2)
        self.l = lax.div(self.s, 2)
        self.sibling = self.s + 1 - 2 * self.c
        self.right = jnp.minimum(self.s + 2, n_seq - 2 + self.c)
        self.left = jnp.maximum(self.s - 2, self.c)
        self.has_right = self.l < self.last
        self.has_left = self.l > 0

    def greet(self, n_dp):
        barrier = pltpu.get_barrier_semaphore()
        d = lax.axis_index("dp")
        for k in range(1, n_dp):
            pl.semaphore_signal(barrier, 1, device_id={"dp": lax.rem(d + k, n_dp)}, device_id_type=MESH)
        pl.semaphore_signal(barrier, 1, device_id={"seq": self.sibling}, device_id_type=MESH)

        @pl.when(self.has_right)
        def _():
            pl.semaphore_signal(barrier, 1, device_id={"seq": self.right}, device_id_type=MESH)

        @pl.when(self.has_left)
        def _():
            pl.semaphore_signal(barrier, 1, device_id={"seq": self.left}, device_id_type=MESH)

        pl.semaphore_wait(barrier, n_dp - 1 + jnp.where(self.has_right & self.has_left, 3, 2))

    def order(self, j):
        near = jnp.minimum(self.l, self.last - self.l)
        half = lax.div(j + 1, 2)
        both = jnp.where(lax.rem(j, 2) == 1, self.l - half, self.l + half)
        far = jnp.where(self.l <= self.last - self.l, j, self.last - j)
        return jnp.where(j <= 2 * near, both, far)


def remote(src, dst, send, recv, seq):
    return pltpu.make_async_remote_copy(
        src_ref=src, dst_ref=dst, send_sem=send, recv_sem=recv, device_id={"seq": seq}, device_id_type=MESH
    )


class Gather:
    def __init__(self, line, full, send_z, send_c, recv):
        self.line, self.full, self.send_z, self.send_c, self.recv = line, full, send_z, send_c, recv

    @staticmethod
    def sems(n_seq):
        n_line = n_seq // 2
        return [
            pltpu.SemaphoreType.DMA((n_line + 1,)),
            pltpu.SemaphoreType.DMA((n_line,)),
            pltpu.SemaphoreType.DMA((n_seq,)),
        ]

    def copy(self, index, send, seq):
        return remote(self.full.at[index], self.full.at[index], send, self.recv.at[index], seq)

    def begin(self):
        n = self.line
        pl.when(n.has_right)(lambda: self.copy(n.s, self.send_z.at[n.l], n.right).start())
        pl.when(n.has_left)(lambda: self.copy(n.s, self.send_z.at[n.n_line], n.left).start())
        self.copy(n.s, self.send_c.at[n.l], n.sibling).start()

    def visit(self, chip):
        n = self.line
        mine = 2 * chip + n.c

        @pl.when(chip != n.l)
        def _():
            self.copy(mine, self.send_c.at[chip], n.sibling).wait_recv()
            pl.when((chip < n.l) & n.has_right)(
                lambda: self.copy(mine, self.send_z.at[chip], n.right).start()
            )
            pl.when((chip > n.l) & n.has_left)(
                lambda: self.copy(mine, self.send_z.at[chip], n.left).start()
            )
            self.copy(mine, self.send_c.at[chip], n.sibling).start()

        self.copy(2 * chip + 1 - n.c, self.send_c.at[chip], n.sibling).wait_recv()

    def end(self):
        n = self.line

        @pl.loop(0, n.n_line)
        def _(chip):
            mine = 2 * chip + n.c
            self.copy(mine, self.send_c.at[chip], n.sibling).wait_send()
            pl.when((chip <= n.l) & n.has_right)(
                lambda: self.copy(mine, self.send_z.at[chip], n.right).wait_send()
            )
            pl.when((chip > n.l) & n.has_left)(
                lambda: self.copy(mine, self.send_z.at[chip], n.left).wait_send()
            )

        pl.when(n.has_left)(lambda: self.copy(n.s, self.send_z.at[n.n_line], n.left).wait_send())


class Scatter:
    def __init__(self, line, part, sib, rcv, send_z, send_c, recv_z, recv_c):
        self.line, self.part, self.sib, self.rcv = line, part, sib, rcv
        self.send_z, self.send_c, self.recv_z, self.recv_c = send_z, send_c, recv_z, recv_c

    @staticmethod
    def sems(n_seq):
        n_line = n_seq // 2
        return [
            pltpu.SemaphoreType.DMA((n_line,)),
            pltpu.SemaphoreType.DMA((n_line,)),
            pltpu.SemaphoreType.DMA((n_line + 1,)),
            pltpu.SemaphoreType.DMA((n_line,)),
        ]

    @staticmethod
    def buffers(n_seq, rows, width):
        n_line = n_seq // 2
        return [
            pltpu.VMEM((n_line, rows, width), BF16),
            pltpu.VMEM((n_line + 1, rows, width), BF16),
        ]

    def across(self, chip):
        n = self.line
        return remote(
            self.part.at[2 * chip + 1 - n.c],
            self.sib.at[chip],
            self.send_c.at[chip],
            self.recv_c.at[chip],
            n.sibling,
        )

    def hop(self, chip, slot, seq):
        n = self.line
        return remote(
            self.part.at[2 * chip + n.c],
            self.rcv.at[slot],
            self.send_z.at[chip],
            self.recv_z.at[slot],
            seq,
        )

    def begin(self):
        n = self.line

        @pl.loop(0, n.n_line)
        def _(j):
            half = lax.div(j, 2)
            self.across(jnp.where(lax.rem(j, 2) == 0, n.last - half, half)).start()

    def add(self, chip, source):
        mine = 2 * chip + self.line.c
        self.part[mine] = (self.part[mine].astype(F32) + source.astype(F32)).astype(BF16)

    def step(self, time):
        n = self.line

        @pl.when(n.l <= time)
        def _():
            chip = n.last - time + n.l
            self.across(chip).wait_recv()
            self.add(chip, self.sib[chip])

            @pl.when(n.has_left)
            def _():
                self.hop(chip, chip, n.right).wait_recv()
                self.add(chip, self.rcv[chip])

            self.hop(chip, chip, n.right).start()

        @pl.when(n.last - n.l <= time)
        def _():
            chip = time - n.last + n.l
            self.across(chip).wait_recv()
            self.add(chip, self.sib[chip])

            @pl.when(n.has_right)
            def _():
                self.hop(chip, chip, n.left).wait_recv()
                self.add(chip, self.rcv[chip])

            self.hop(chip, jnp.where(chip == n.l - 1, n.n_line, chip), n.left).start()

    def finish(self, out):
        n = self.line
        mine = 2 * n.l + n.c
        self.across(n.l).wait_recv()
        out[...] = self.part[mine].astype(F32) + self.sib[n.l].astype(F32)

        @pl.when(n.has_left)
        def _():
            self.hop(n.l, n.l, n.right).wait_recv()
            out[...] += self.rcv[n.l].astype(F32)

        @pl.when(n.has_right)
        def _():
            self.hop(n.l, n.n_line, n.left).wait_recv()
            out[...] += self.rcv[n.n_line].astype(F32)

        @pl.loop(0, n.n_line)
        def _(chip):
            self.across(chip).wait_send()
            pl.when(chip > n.l)(lambda: self.hop(chip, chip, n.right).wait_send())
            pl.when(chip < n.l)(lambda: self.hop(chip, chip, n.left).wait_send())


def spread_work(units, slots, index):
    return (units * index // slots, units * (index + 1) // slots)


class Spread:
    def __init__(self, line, n_dp, blocks, dst, own_sem, send_z, send_xy, recv):
        self.line, self.n_dp, self.blocks, self.dst = line, n_dp, blocks, dst
        self.own_sem, self.send_z, self.send_xy, self.recv = own_sem, send_z, send_xy, recv
        self.n_seq = 2 * line.n_line
        self.d = lax.axis_index("dp")

    @staticmethod
    def sems(n_seq, n_dp):
        return [
            pltpu.SemaphoreType.DMA((1,)),
            pltpu.SemaphoreType.DMA((n_seq,)),
            pltpu.SemaphoreType.DMA((n_seq, n_dp)),
            pltpu.SemaphoreType.DMA((n_dp, n_seq)),
        ]

    def hop(self, t):
        n = self.line
        return pltpu.make_async_remote_copy(
            src_ref=self.blocks.at[t],
            dst_ref=self.dst.at[self.d, n.s],
            send_sem=self.send_z.at[t],
            recv_sem=self.recv.at[self.d, n.s],
            device_id={"seq": t},
            device_id_type=MESH,
        )

    def own(self):
        n = self.line
        return pltpu.make_async_copy(self.blocks.at[n.s], self.dst.at[self.d, n.s], self.own_sem.at[0])

    def over(self, source, k, own=False):
        return pltpu.make_async_remote_copy(
            src_ref=self.blocks.at[self.line.s] if own else self.dst.at[self.d, source],
            dst_ref=self.dst.at[self.d, source],
            send_sem=self.send_xy.at[source, k],
            recv_sem=self.recv.at[self.d, source],
            device_id={"dp": lax.rem(self.d + k, self.n_dp)},
            device_id_type=MESH,
        )

    def landed(self, d, source):
        return pltpu.make_async_remote_copy(
            src_ref=self.dst.at[d, source],
            dst_ref=self.dst.at[d, source],
            send_sem=self.send_z.at[0],
            recv_sem=self.recv.at[d, source],
            device_id={"dp": d},
            device_id_type=MESH,
        )

    def begin(self):
        n = self.line

        @pl.loop(1, self.n_seq)
        def _(j):
            self.hop(lax.rem(n.s + j, self.n_seq)).start()

        self.own().start()

    def forward_own(self):
        for k in range(1, self.n_dp):
            self.over(self.line.s, k, True).start()

    def forward(self, first, end):
        n = self.line

        @pl.loop(first, end)
        def _(j):
            source = lax.rem(n.s - j + self.n_seq, self.n_seq)
            self.landed(self.d, source).wait_recv()
            for k in range(1, self.n_dp):
                self.over(source, k).start()

    def arrive(self):
        for k in range(1, self.n_dp):
            owner = lax.rem(self.d + k, self.n_dp)

            @pl.loop(0, self.n_seq)
            def _(source):
                self.landed(owner, source).wait_recv()

        self.own().wait()

    def end(self):
        n = self.line

        @pl.loop(0, self.n_seq)
        def _(j):
            pl.when(j != n.s)(lambda: self.hop(j).wait_send())
            for k in range(1, self.n_dp):
                self.over(j, k).wait_send()


class Copies:
    def __init__(self, n_dp, own, dst, own_sem, send, recv):
        self.n_dp, self.own_ref, self.dst = n_dp, own, dst
        self.own_sem, self.send, self.recv = own_sem, send, recv
        self.d = lax.axis_index("dp")

    @staticmethod
    def sems(n_dp):
        return [
            pltpu.SemaphoreType.DMA((1,)),
            pltpu.SemaphoreType.DMA((n_dp,)),
            pltpu.SemaphoreType.DMA((n_dp,)),
        ]

    def copy(self, k, slot):
        return pltpu.make_async_remote_copy(
            src_ref=self.own_ref,
            dst_ref=self.dst.at[slot],
            send_sem=self.send.at[k],
            recv_sem=self.recv.at[slot],
            device_id={"dp": lax.rem(self.d + k, self.n_dp)},
            device_id_type=MESH,
        )

    def begin(self):
        for k in range(1, self.n_dp):
            self.copy(k, self.d).start()
        pltpu.make_async_copy(self.own_ref, self.dst.at[self.d], self.own_sem.at[0]).start()

    def end(self):
        for k in range(1, self.n_dp):
            self.copy(k, lax.rem(self.d + k, self.n_dp)).wait()
        pltpu.make_async_copy(self.own_ref, self.dst.at[self.d], self.own_sem.at[0]).wait()


class Relay:
    def __init__(self, line, n_dp):
        n_seq = 2 * line.n_line
        self.n_dp = n_dp
        self.d = lax.axis_index("dp")
        block = self.d * n_seq + line.s
        self.slot, self.target = lax.rem(block, n_dp), lax.div(block, n_dp)
        block = line.s * n_dp + self.d
        self.owner_d, self.owner_s = lax.div(block, n_seq), lax.rem(block, n_seq)
        self.stays = (self.slot == self.d) & (self.target == line.s)
        self.moves = jnp.logical_not(self.stays)

    def to_relay(self, src, dst, send, recv):
        return pltpu.make_async_remote_copy(
            src_ref=src, dst_ref=dst, send_sem=send, recv_sem=recv,
            device_id=(self.slot, self.target), device_id_type=MESH,
        )

    def to_owner(self, src, dst, send, recv):
        return pltpu.make_async_remote_copy(
            src_ref=src, dst_ref=dst, send_sem=send, recv_sem=recv,
            device_id=(self.owner_d, self.owner_s), device_id_type=MESH,
        )

    def over(self, k, src, dst, send, recv):
        return pltpu.make_async_remote_copy(
            src_ref=src, dst_ref=dst, send_sem=send, recv_sem=recv,
            device_id={"dp": lax.rem(self.d + k, self.n_dp)}, device_id_type=MESH,
        )


class OutRows(Relay):
    def __init__(self, line, n_dp, own, dst, own_sem, send_z, send_xy, recv):
        super().__init__(line, n_dp)
        self.own_ref, self.dst = own, dst
        self.own_sem, self.send_z, self.send_xy, self.recv = own_sem, send_z, send_xy, recv

    @staticmethod
    def sems(n_dp):
        return [
            pltpu.SemaphoreType.DMA((1,)),
            pltpu.SemaphoreType.DMA((1,)),
            pltpu.SemaphoreType.DMA((n_dp,)),
            pltpu.SemaphoreType.DMA((n_dp,)),
        ]

    def hop(self):
        return self.to_relay(self.own_ref, self.dst.at[self.slot], self.send_z.at[0], self.recv.at[self.slot])

    def own(self):
        return pltpu.make_async_copy(self.own_ref, self.dst.at[self.slot], self.own_sem.at[0])

    def copy(self, k):
        return self.over(k, self.dst.at[self.d], self.dst.at[self.d], self.send_xy.at[k], self.recv.at[self.d])

    def landed(self, slot):
        return self.over(1, self.dst.at[slot], self.dst.at[slot], self.send_xy.at[1], self.recv.at[slot])

    def begin(self):
        pl.when(self.stays)(lambda: self.own().start())
        pl.when(self.moves)(lambda: self.hop().start())

    def forward(self):
        pl.when(self.stays)(lambda: self.own().wait())
        pl.when(self.moves)(lambda: self.landed(self.d).wait_recv())
        for k in range(1, self.n_dp):
            self.copy(k).start()

    def arrive(self):
        for k in range(1, self.n_dp):
            self.landed(lax.rem(self.d + k, self.n_dp)).wait_recv()

    def end(self):
        pl.when(self.moves)(lambda: self.hop().wait_send())
        for k in range(1, self.n_dp):
            self.copy(k).wait_send()


class OutSum(Relay):
    def __init__(self, line, n_dp, src, land, final, own_sem, send_xy, recv_xy, send_z, recv_z):
        super().__init__(line, n_dp)
        self.src, self.land, self.final = src, land, final
        self.own_sem, self.send_xy, self.recv_xy, self.send_z, self.recv_z = own_sem, send_xy, recv_xy, send_z, recv_z

    @staticmethod
    def sems(n_dp):
        return [
            pltpu.SemaphoreType.DMA((1,)),
            pltpu.SemaphoreType.DMA((n_dp,)),
            pltpu.SemaphoreType.DMA((n_dp,)),
            pltpu.SemaphoreType.DMA((1,)),
            pltpu.SemaphoreType.DMA((1,)),
        ]

    def copy(self, k):
        return self.over(
            k, self.src.at[lax.rem(self.d + k, self.n_dp)], self.land.at[self.d], self.send_xy.at[k], self.recv_xy.at[self.d]
        )

    def landed(self, owner):
        return self.over(1, self.land.at[owner], self.land.at[owner], self.send_xy.at[1], self.recv_xy.at[owner])

    def own(self):
        return pltpu.make_async_copy(self.src.at[self.d], self.land.at[self.d], self.own_sem.at[0])

    def hop(self):
        return self.to_owner(self.land.at[self.d], self.final, self.send_z.at[0], self.recv_z.at[0])

    def begin(self):
        self.own().start()
        for k in range(1, self.n_dp):
            self.copy(k).start()

    def reduce(self):
        self.own().wait()
        for k in range(1, self.n_dp):
            self.landed(lax.rem(self.d + k, self.n_dp)).wait_recv()
        total = self.land[0].astype(F32)
        for owner in range(1, self.n_dp):
            total = total + self.land[owner].astype(F32)
        total = total.astype(BF16)

        @pl.when(self.stays)
        def _():
            self.final[...] = total

        @pl.when(self.moves)
        def _():
            self.land[self.d] = total
            self.hop().start()

    def end(self):
        pl.when(self.moves)(lambda: self.hop().wait())
        for k in range(1, self.n_dp):
            self.copy(k).wait_send()


class Collect:
    def __init__(self, line, n_dp, src, land, final, own_sem, send_xy, recv_xy, send_z, recv_z):
        self.line, self.n_dp, self.n_seq = line, n_dp, 2 * line.n_line
        self.src, self.land, self.final = src, land, final
        self.own_sem, self.send_xy, self.recv_xy, self.send_z, self.recv_z = own_sem, send_xy, recv_xy, send_z, recv_z
        self.d = lax.axis_index("dp")

    @staticmethod
    def sems(n_seq, n_dp):
        return [
            pltpu.SemaphoreType.DMA((1,)),
            pltpu.SemaphoreType.DMA((n_seq, n_dp)),
            pltpu.SemaphoreType.DMA((n_dp, n_seq)),
            pltpu.SemaphoreType.DMA((n_seq,)),
            pltpu.SemaphoreType.DMA((n_seq,)),
        ]

    def over(self, t, k):
        peer = lax.rem(self.d + k, self.n_dp)
        return pltpu.make_async_remote_copy(
            src_ref=self.src.at[peer, t],
            dst_ref=self.land.at[self.d, t],
            send_sem=self.send_xy.at[t, k],
            recv_sem=self.recv_xy.at[self.d, t],
            device_id={"dp": peer},
            device_id_type=MESH,
        )

    def landed(self, owner, t):
        return pltpu.make_async_remote_copy(
            src_ref=self.land.at[owner, t],
            dst_ref=self.land.at[owner, t],
            send_sem=self.send_xy.at[t, 1],
            recv_sem=self.recv_xy.at[owner, t],
            device_id={"dp": owner},
            device_id_type=MESH,
        )

    def own(self):
        return pltpu.make_async_copy(self.src.at[self.d], self.land.at[self.d], self.own_sem.at[0])

    def hop(self, t, slot):
        return pltpu.make_async_remote_copy(
            src_ref=self.land.at[self.d, t],
            dst_ref=self.final.at[slot],
            send_sem=self.send_z.at[t],
            recv_sem=self.recv_z.at[slot],
            device_id={"seq": t},
            device_id_type=MESH,
        )

    def place(self, j):
        return lax.rem(self.line.s + 1 + j, self.n_seq)

    def begin(self):
        self.own().start()

        @pl.loop(0, self.n_seq)
        def _(j):
            for k in range(1, self.n_dp):
                self.over(self.place(j), k).start()

    def reduce(self, first, end):
        if first == 0:
            self.own().wait()

        @pl.loop(first, end)
        def _(j):
            t = self.place(j)
            for k in range(1, self.n_dp):
                self.landed(lax.rem(self.d + k, self.n_dp), t).wait_recv()
            total = self.land[0, t].astype(F32)
            for owner in range(1, self.n_dp):
                total = total + self.land[owner, t].astype(F32)
            total = total.astype(BF16)

            @pl.when(t == self.line.s)
            def _():
                self.final[t] = total

            @pl.when(t != self.line.s)
            def _():
                self.land[self.d, t] = total
                self.hop(t, self.line.s).start()

    def end(self):
        @pl.loop(0, self.n_seq)
        def _(t):
            pl.when(t != self.line.s)(lambda: self.hop(t, t).wait())
            for k in range(1, self.n_dp):
                self.over(t, k).wait_send()


class RowSum:
    def __init__(self, n_dp, src, land, own_sem, send, recv):
        self.n_dp, self.src, self.land = n_dp, src, land
        self.own_sem, self.send, self.recv = own_sem, send, recv
        self.d = lax.axis_index("dp")

    sems = Copies.sems

    def copy(self, k, slot):
        peer = lax.rem(self.d + k, self.n_dp)
        return pltpu.make_async_remote_copy(
            src_ref=self.src.at[peer],
            dst_ref=self.land.at[slot],
            send_sem=self.send.at[k],
            recv_sem=self.recv.at[slot],
            device_id={"dp": peer},
            device_id_type=MESH,
        )

    def own(self):
        return pltpu.make_async_copy(self.src.at[self.d], self.land.at[self.d], self.own_sem.at[0])

    def begin(self):
        self.own().start()
        for k in range(1, self.n_dp):
            self.copy(k, self.d).start()

    def finish(self, out):
        self.own().wait()
        for k in range(1, self.n_dp):
            self.copy(k, lax.rem(self.d + k, self.n_dp)).wait()
        total = self.land[0].astype(F32)
        for owner in range(1, self.n_dp):
            total = total + self.land[owner].astype(F32)
        out[...] = total


def greet_all(line, n_dp, relay):
    barrier = pltpu.get_barrier_semaphore()
    n_seq = 2 * line.n_line
    d = lax.axis_index("dp")
    for j in range(1, n_seq):
        pl.semaphore_signal(barrier, 1, device_id={"seq": lax.rem(line.s + j, n_seq)}, device_id_type=MESH)
    for k in range(1, n_dp):
        pl.semaphore_signal(barrier, 1, device_id={"dp": lax.rem(d + k, n_dp)}, device_id_type=MESH)

    @pl.when(relay.moves)
    def _():
        for device in ((relay.slot, relay.target), (relay.owner_d, relay.owner_s)):
            pl.semaphore_signal(barrier, 1, device_id=device, device_id_type=MESH)

    pl.semaphore_wait(barrier, n_seq + n_dp - 2 + jnp.where(relay.moves, 2, 0))


def turn(values, lanes_low):
    half = HEAD_DIM // 2
    width = values.shape[-1]
    return jnp.where(
        lanes_low, pltpu.roll(values, width - half, values.ndim - 1), pltpu.roll(values, half, values.ndim - 1)
    )


def low_lanes(shape):
    return lax.rem(lax.broadcasted_iota(jnp.int32, shape, len(shape) - 1), HEAD_DIM) < HEAD_DIM // 2


def head_lanes(kv, h, q_cols):
    wide = jnp.concatenate([kv] * (q_cols // (2 * HEAD_DIM)), axis=1).astype(F32)
    swapped = pltpu.roll(wide, HEAD_DIM, 1)
    here = lax.div(lax.broadcasted_iota(jnp.int32, wide.shape, 1), HEAD_DIM) == h
    even = lax.rem(h, 2) == 0
    key = jnp.where(here, jnp.where(even, wide, swapped), 0.0).astype(BF16)
    value = jnp.where(here, jnp.where(even, swapped, wide), 0.0).astype(BF16)
    return key, value


def attention_kernel(
    n_seq, n_dp, prefix_ref, tok_ref, cot_ref, cos_ref, sin_ref, qkvb_hbm, gub_hbm, wo_own, wd_own,
    hidden_ref, nmlp_ref, q_ref, kv_ref, mixed_ref, normed_hbm, cot_hbm, wqkv_hbm, wo_hbm, wgu_hbm, wd_hbm,
    full, cot, wqkv, wo, acc, part, sib, rcv, save_sem, *sems,
):
    n = Line(n_seq)
    rows, width = tok_ref.shape
    micro, length, q_cols = q_ref.shape
    span = rows // micro
    cols_all = wqkv.shape[3]
    pair = 2 * rows
    tok = tok_ref[...].astype(F32)
    full[n.s] = (tok * lax.rsqrt(jnp.mean(tok * tok, axis=1, keepdims=True) + EPSILON)).astype(BF16)
    cot[n.s] = cot_ref[...]

    gather = Gather(n, full, *sems[0:3])
    gather_cot = Gather(n, cot, *sems[3:6])
    scatter = Scatter(n, part, sib, rcv, *sems[6:10])
    qkv_w = Spread(n, n_dp, qkvb_hbm, wqkv, *sems[10:14])
    gu_w = Spread(n, n_dp, gub_hbm, wgu_hbm, *sems[14:18])
    out_w = OutRows(n, n_dp, wo_own, wo, *sems[18:22])
    down_w = Copies(n_dp, wd_own, wd_hbm, *sems[22:25])

    greet_all(n, n_dp, out_w)
    qkv_w.begin()
    gather.begin()
    out_w.begin()
    qkv_w.forward_own()
    qkv_w.forward(1, n_seq)
    out_w.forward()
    down_w.begin()
    for j in range(n.n_line):
        gather.visit(n.order(j))
    gu_w.begin()
    gu_w.forward_own()
    qkv_w.arrive()

    saves = [
        pltpu.make_async_copy(full, normed_hbm, save_sem.at[0]),
        pltpu.make_async_copy(wqkv, wqkv_hbm, save_sem.at[1]),
    ]
    for save in saves:
        save.start()

    low = low_lanes((span, cols_all))

    @pl.loop(0, n.n_line)
    def _(chip):
        two = pl.ds(pl.multiple_of(2 * chip, 2), 2)
        value = nn(full[two].reshape(pair, width), wqkv[...].reshape(width, cols_all))
        for core in range(2):
            at = pl.ds(pl.multiple_of((2 * chip + core) * span, span), span)
            cos, sin = cos_ref[at, :], sin_ref[at, :]
            for m in range(micro):
                block = value[(core * micro + m) * span : (core * micro + m + 1) * span]
                turned = (block * cos + turn(block, low) * sin).astype(BF16)
                q_ref[m, at, :] = turned[:, :q_cols]
                kv_ref[m, at, :] = turned[:, q_cols:]

    scale = 1.0 / math.sqrt(HEAD_DIM)
    q_tile = min(length, QUERY_TILE)

    @pl.loop(0, micro)
    def _(m):
        prefix = prefix_ref[m]

        @pl.loop(0, q_cols // HEAD_DIM)
        def _(h):
            key, val = head_lanes(kv_ref[m], h, q_cols)

            @pl.loop(0, length // q_tile)
            def _(i):
                at = pl.ds(pl.multiple_of(i * q_tile, q_tile), q_tile)
                scores = nt(q_ref[m, at, :], key) * scale
                query_pos = i * q_tile + lax.broadcasted_iota(jnp.int32, scores.shape, 0)
                key_pos = lax.broadcasted_iota(jnp.int32, scores.shape, 1)
                scores = jnp.where((key_pos <= query_pos) | (key_pos < prefix), scores, NEGATIVE)
                weights = jnp.exp(scores - jnp.max(scores, axis=1, keepdims=True))
                total = jnp.sum(weights, axis=1, keepdims=True)
                mixed = nn((weights / total).astype(BF16), val)

                @pl.when(h == 0)
                def _():
                    acc[at, :] = mixed

                @pl.when(h > 0)
                def _():
                    acc[at, :] += mixed

        mixed_ref[m] = acc[...].astype(BF16)

    out_w.arrive()
    pltpu.make_async_copy(wo, wo_hbm, save_sem.at[2]).start()
    for m in range(micro):

        @pl.loop(0, width // TILE)
        def _(w):
            cols = pl.ds(pl.multiple_of(w * TILE, TILE), TILE)
            value = nn(mixed_ref[m], wo[:, :, cols].reshape(q_cols, TILE))
            part[:, m * span : (m + 1) * span, cols] = value.astype(BF16).reshape(n_seq, span, TILE)

    scatter.begin()
    gather_cot.begin()
    gather_cot.visit(n.l)
    for time in range(n.last):
        scatter.step(time)
        gather_cot.visit(n.order(time + 1))
        first, end = spread_work(n_seq - 1, n.last, time)
        gu_w.forward(first + 1, end + 1)
    pltpu.make_async_copy(cot, cot_hbm, save_sem.at[3]).start()
    scatter.finish(hidden_ref)
    hidden = hidden_ref[...] + tok_ref[...].astype(F32)
    hidden_ref[...] = hidden
    nmlp_ref[...] = (hidden * lax.rsqrt(jnp.mean(hidden * hidden, axis=1, keepdims=True) + EPSILON)).astype(BF16)
    gu_w.arrive()
    down_w.end()
    for save in saves:
        save.wait()
    pltpu.make_async_copy(wo, wo_hbm, save_sem.at[2]).wait()
    pltpu.make_async_copy(cot, cot_hbm, save_sem.at[3]).wait()
    gather.end()
    gather_cot.end()
    qkv_w.end()
    gu_w.end()
    out_w.end()


def attention_call(prefix, tok, cot, cos, sin, qkvb, gub, wo_own, wd_own, n_seq, n_dp):
    rows, width = tok.shape
    micro = prefix.shape[0]
    length = cos.shape[0]
    shard, qkv_cols = qkvb.shape[1:]
    gu_cols = gub.shape[2]
    q_cols = width // n_seq
    ff_block = wd_own.shape[0]
    every = n_seq * rows
    any_spec = pl.BlockSpec(memory_space=pl.ANY)
    vmem = pl.BlockSpec(memory_space=pltpu.VMEM)
    outs = [
        ((rows, width), F32, vmem),
        ((rows, width), BF16, vmem),
        ((micro, length, q_cols), BF16, vmem),
        ((micro, length, 2 * HEAD_DIM), BF16, vmem),
        ((micro, length, q_cols), BF16, vmem),
        ((n_seq, rows, width), BF16, any_spec),
        ((n_seq, rows, width), BF16, any_spec),
        ((n_dp, n_seq, shard, qkv_cols), BF16, any_spec),
        ((n_dp, shard, width), BF16, any_spec),
        ((n_dp, n_seq, shard, gu_cols), BF16, any_spec),
        ((n_dp, ff_block, width), BF16, any_spec),
    ]
    return pl.pallas_call(
        functools.partial(attention_kernel, n_seq, n_dp),
        out_shape=tuple(jax.ShapeDtypeStruct(s, t) for s, t, _ in outs),
        in_specs=[pl.BlockSpec(memory_space=pltpu.SMEM)] + [vmem] * 4 + [any_spec] * 4,
        out_specs=tuple(spec for _, _, spec in outs),
        scratch_shapes=[
            pltpu.VMEM((n_seq, rows, width), BF16),
            pltpu.VMEM((n_seq, rows, width), BF16),
            pltpu.VMEM((n_dp, n_seq, shard, qkv_cols), BF16),
            pltpu.VMEM((n_dp, shard, width), BF16),
            pltpu.VMEM((length, q_cols), F32),
            pltpu.VMEM((n_seq, rows, width), BF16),
            *Scatter.buffers(n_seq, rows, width),
            pltpu.SemaphoreType.DMA((4,)),
            *Gather.sems(n_seq),
            *Gather.sems(n_seq),
            *Scatter.sems(n_seq),
            *Spread.sems(n_seq, n_dp),
            *Spread.sems(n_seq, n_dp),
            *OutRows.sems(n_dp),
            *Copies.sems(n_dp),
        ],
        compiler_params=pltpu.CompilerParams(
            collective_id=2, has_side_effects=True, vmem_limit_bytes=VMEM_LIMIT
        ),
        cost_estimate=pl.CostEstimate(flops=10**10, bytes_accessed=40 << 20, transcendentals=0),
        name="attention",
    )(prefix, tok, cot, cos, sin, qkvb, gub, wo_own, wd_own)


def mlp_kernel(
    n_seq, n_dp, x_ref, cot_hbm, wgu_hbm, wd_hbm,
    gnm_ref, pout_hbm, dgu_hbm, dwd_ref,
    full, cot, wgu, wd, act, gg, gu, part, sib, rcv, dwd, land, stage_gu, stage_rows, load_sem, gu_sem, rows_sem, *sems,
):
    n = Line(n_seq)
    rows, width = x_ref.shape
    ff = wd.shape[0]
    pair = 2 * rows
    loads = [
        pltpu.make_async_copy(src, dst, load_sem.at[i])
        for i, (src, dst) in enumerate(
            [(wgu_hbm, wgu), (cot_hbm, cot), (wd_hbm, wd)]
        )
    ]
    for load in loads:
        load.start()
    full[n.s] = x_ref[...]
    n.greet(n_dp)
    gather = Gather(n, full, *sems[:3])
    scatter = Scatter(n, part, sib, rcv, *sems[3:7])
    down = RowSum(n_dp, dwd, land, *sems[7:10])
    gather.begin()
    for load in loads:
        load.wait()

    @pl.loop(0, n.n_line)
    def _(j):
        chip = n.order(j)
        gather.visit(chip)
        at = pl.ds(pl.multiple_of(chip * pair, pair), pair)
        two = pl.ds(pl.multiple_of(2 * chip, 2), 2)

        @pl.loop(0, ff // TILE)
        def _(f):
            cols = pl.ds(pl.multiple_of(f * TILE, TILE), TILE)
            x = full[two].reshape(pair, width)
            gate = nn(x, wgu[:, cols])
            up = nn(x, wgu[:, pl.ds(pl.multiple_of(ff + f * TILE, TILE), TILE)])
            grad = nt(cot[two].reshape(pair, width), wd[cols, :])
            sig = jax.nn.sigmoid(gate)
            silu = gate * sig
            act[at, cols] = (silu * up).astype(BF16)
            gg[at, cols] = (grad * up * (sig + silu * (1.0 - sig))).astype(BF16)
            gu[at, cols] = (grad * silu).astype(BF16)

        @pl.loop(0, width // TILE)
        def _(w):
            cols = pl.ds(pl.multiple_of(w * TILE, TILE), TILE)
            value = nt(gg[at, :], wgu[cols, :ff]) + nt(gu[at, :], wgu[cols, ff:])
            part[two, :, cols] = value.astype(BF16).reshape(2, rows, TILE)

    scatter.begin()

    owners = TILE // dwd.shape[1]

    @pl.loop(0, ff // TILE)
    def _(f):
        cols = pl.ds(pl.multiple_of(f * TILE, TILE), TILE)
        at = pl.ds(f * owners, owners)
        for w in range(0, width, 2 * TILE):
            span = cot[:, :, w : w + 2 * TILE].reshape(n_seq * rows, 2 * TILE)
            value = tn(act[:, cols], span).astype(BF16)
            dwd[at, :, w : w + 2 * TILE] = value.reshape(owners, dwd.shape[1], 2 * TILE)

    down.begin()

    def gate_up_grads(first, end):
        @pl.loop(first, end)
        def _(w):
            slot = lax.rem(w, 2)
            cols = pl.ds(pl.multiple_of(w * TILE, TILE), TILE)
            x = full[:, :, cols].reshape(n_seq * rows, TILE)
            copy = pltpu.make_async_copy(stage_gu.at[slot], dgu_hbm.at[cols, :], gu_sem.at[slot])
            pl.when(w >= 2)(lambda: copy.wait())
            stage_gu[slot, :, :ff] = tn(x, gg[...]).astype(BF16)
            stage_gu[slot, :, ff:] = tn(x, gu[...]).astype(BF16)
            copy.start()

    def out_parts(first, end):
        @pl.loop(first, end)
        def _(chip):
            slot = lax.rem(chip, 2)
            at = pl.ds(pl.multiple_of(chip * pair, pair), pair)
            two = pl.ds(pl.multiple_of(2 * chip, 2), 2)
            copies = [
                pltpu.make_async_copy(
                    stage_rows.at[slot, pl.ds(i * rows, rows)], pout_hbm.at[2 * chip + i], rows_sem.at[slot + 2 * i]
                )
                for i in range(2)
            ]

            @pl.when(chip >= 2)
            def _():
                for copy in copies:
                    copy.wait()

            for w in range(0, width, 2 * TILE):
                stage_rows[slot, :pair, w : w + 2 * TILE] = nn(act[at, :], wd[:, w : w + 2 * TILE]).astype(BF16)
            for copy in copies:
                copy.start()

    def drain_out():
        for slot in range(2):
            for i in range(2):
                pltpu.make_async_copy(
                    stage_rows.at[slot, pl.ds(i * rows, rows)], pout_hbm.at[i], rows_sem.at[slot + 2 * i]
                ).wait()

    for time in range(n.last):
        scatter.step(time)
        gate_up_grads(*spread_work(width // TILE, n.last, time))
        if time == n.last - 1:
            out_parts(0, n.n_line)
            drain_out()
    for slot in range(2):
        pltpu.make_async_copy(stage_gu.at[slot], dgu_hbm.at[pl.ds(0, TILE), :], gu_sem.at[slot]).wait()
    scatter.finish(gnm_ref)
    down.finish(dwd_ref)
    gather.end()


def mlp_call(x, cot, wgu, wd, n_seq, n_dp):
    rows, width = x.shape
    ff = wd.shape[0]
    every = n_seq * rows
    any_spec = pl.BlockSpec(memory_space=pl.ANY)
    vmem = pl.BlockSpec(memory_space=pltpu.VMEM)
    return pl.pallas_call(
        functools.partial(mlp_kernel, n_seq, n_dp),
        out_shape=(
            jax.ShapeDtypeStruct((rows, width), F32),
            jax.ShapeDtypeStruct((n_seq, rows, width), BF16),
            jax.ShapeDtypeStruct((width, 2 * ff), BF16),
            jax.ShapeDtypeStruct((ff // n_dp, width), F32),
        ),
        in_specs=[vmem] + [any_spec] * 3,
        out_specs=(vmem, any_spec, any_spec, vmem),
        scratch_shapes=[
            pltpu.VMEM((n_seq, rows, width), BF16),
            pltpu.VMEM((n_seq, rows, width), BF16),
            pltpu.VMEM((width, 2 * ff), BF16),
            pltpu.VMEM((ff, width), BF16),
            pltpu.VMEM((every, ff), BF16),
            pltpu.VMEM((every, ff), BF16),
            pltpu.VMEM((every, ff), BF16),
            pltpu.VMEM((n_seq, rows, width), BF16),
            *Scatter.buffers(n_seq, rows, width),
            pltpu.VMEM((n_dp, ff // n_dp, width), BF16),
            pltpu.VMEM((n_dp, ff // n_dp, width), BF16),
            pltpu.VMEM((2, TILE, 2 * ff), BF16),
            pltpu.VMEM((2, TILE, width), BF16),
            pltpu.SemaphoreType.DMA((3,)),
            pltpu.SemaphoreType.DMA((2,)),
            pltpu.SemaphoreType.DMA((4,)),
            *Gather.sems(n_seq),
            *Scatter.sems(n_seq),
            *RowSum.sems(n_dp),
        ],
        compiler_params=pltpu.CompilerParams(
            collective_id=1, has_side_effects=True, vmem_limit_bytes=VMEM_LIMIT
        ),
        cost_estimate=pl.CostEstimate(flops=18 * every * width * ff, bytes_accessed=40 << 20, transcendentals=0),
        name="mlp",
    )(x, cot, wgu, wd)


def backward_kernel(
    n_seq, n_dp, prefix_ref, branch_ref, q_ref, kv_ref, mixed_ref, cos_ref, sin_ref, gains_ref,
    pout_hbm, normed_hbm, wqkv_hbm, wo_hbm, dgu_hbm,
    ge_ref, sum_ref, dqkv_out, dwo_out, dgate_ref, dup_ref,
    full, tiles, wqkv, wo, gm, acc_q, acc_k, acc_v, gqkv, part, sib, rcv, sib_o, rcv_o,
    land_gu, final_gu, dqkv, land_qkv, final_qkv, dwo, land_o, final_o, load_sem, tile_sem, *sems,
):
    n = Line(n_seq)
    rows, width = branch_ref.shape
    micro, length, q_cols = q_ref.shape
    span = rows // micro
    pair = 2 * rows
    loads = [
        pltpu.make_async_copy(src, dst, load_sem.at[i])
        for i, (src, dst) in enumerate(
            [(pout_hbm, part), (wo_hbm, wo), (wqkv_hbm, wqkv)]
        )
    ]
    for load in loads:
        load.start()
    full[n.s] = branch_ref[...]
    gather = Gather(n, full, *sems[0:3])
    scatter = Scatter(n, part, sib, rcv, *sems[3:7])
    scatter_out = Scatter(n, part, sib_o, rcv_o, *sems[7:11])
    gu_sum = Collect(n, n_dp, dgu_hbm, land_gu, final_gu, *sems[11:16])
    qkv_sum = Collect(n, n_dp, dqkv, land_qkv, final_qkv, *sems[16:21])
    out_sum = OutSum(n, n_dp, dwo, land_o, final_o, *sems[21:26])
    greet_all(n, n_dp, out_sum)
    gather.begin()
    loads[0].wait()
    scatter_out.begin()
    gu_sum.begin()
    loads[1].wait()
    early = n_seq // 2

    for j in range(n.n_line):
        chip = n.order(j)
        gather.visit(chip)
        two = pl.ds(pl.multiple_of(2 * chip, 2), 2)
        value = nt(full[two].reshape(pair, width), wo[...].reshape(q_cols, width)).astype(BF16)
        for core in range(2):
            at = pl.ds(pl.multiple_of((2 * chip + core) * span, span), span)
            for m in range(micro):
                gm[m, at, :] = value[(core * micro + m) * span : (core * micro + m + 1) * span]
        if j < n.last:
            scatter_out.step(j)
        if j > 0:
            gu_sum.reduce(*spread_work(early, n.last, j - 1))

    scale = 1.0 / math.sqrt(HEAD_DIM)
    q_tile = min(length, QUERY_TILE)
    low = low_lanes((length, q_cols + 2 * HEAD_DIM))
    loads[2].wait()

    @pl.loop(0, micro)
    def _(m):
        prefix = prefix_ref[m]
        for ref in (acc_q, acc_k, acc_v):
            ref[...] = jnp.zeros_like(ref)

        @pl.loop(0, q_cols // HEAD_DIM)
        def _(h):
            key, val = head_lanes(kv_ref[m], h, q_cols)
            here = lax.div(lax.broadcasted_iota(jnp.int32, (length, q_cols), 1), HEAD_DIM) == h

            @pl.loop(0, length // q_tile)
            def _(i):
                at = pl.ds(pl.multiple_of(i * q_tile, q_tile), q_tile)
                query, grad = q_ref[m, at, :], gm[m, at, :]
                scores = nt(key, query) * scale
                key_pos = lax.broadcasted_iota(jnp.int32, scores.shape, 0)
                query_pos = i * q_tile + lax.broadcasted_iota(jnp.int32, scores.shape, 1)
                scores = jnp.where((key_pos <= query_pos) | (key_pos < prefix), scores, NEGATIVE)
                weights = jnp.exp(scores - jnp.max(scores, axis=0, keepdims=True))
                probs = weights / jnp.sum(weights, axis=0, keepdims=True)
                grad_probs = nt(val, grad)
                delta = jnp.sum(probs * grad_probs, axis=0, keepdims=True)
                grad_scores = (probs * (grad_probs - delta)).astype(BF16)
                acc_q[at, :] += tn(grad_scores, key)
                acc_k[...] += jnp.where(here, nn(grad_scores, query), 0.0)
                acc_v[...] += jnp.where(here, nn(probs.astype(BF16), grad), 0.0)

        def fold(ref):
            total = ref[:, : 2 * HEAD_DIM]
            for w in range(2 * HEAD_DIM, q_cols, 2 * HEAD_DIM):
                total = total + ref[:, w : w + 2 * HEAD_DIM]
            return total + pltpu.roll(total, HEAD_DIM, 1)

        first = lax.broadcasted_iota(jnp.int32, (length, 2 * HEAD_DIM), 1) < HEAD_DIM
        grads = jnp.concatenate([acc_q[...] * scale, jnp.where(first, fold(acc_k) * scale, fold(acc_v))], axis=1)
        gqkv[m] = (grads * cos_ref[...] - turn(grads, low) * sin_ref[...]).astype(BF16)

    scatter_out.finish(sum_ref)
    for m in range(micro):

        @pl.loop(0, width // TILE)
        def _(w):
            at = pl.ds(pl.multiple_of(w * TILE, TILE), TILE)
            value = nt(gqkv[m], wqkv[at, :])
            part[:, m * span : (m + 1) * span, at] = value.astype(BF16).reshape(n_seq, span, TILE)

    scatter.begin()

    shard = dwo.shape[1]

    @pl.loop(0, width // TILE)
    def _(w):
        cols = pl.ds(pl.multiple_of(w * TILE, TILE), TILE)
        d_out = jnp.zeros((q_cols, TILE), F32)
        for m in range(micro):
            d_out = d_out + tn(mixed_ref[m], full[:, m * span : (m + 1) * span, cols].reshape(length, TILE))
        dwo[:, :, cols] = d_out.astype(BF16).reshape(n_dp, shard, TILE)

    out_sum.begin()

    half = n_seq // 2
    depth = half * shard

    def fetch(w):
        cols = pl.ds(pl.multiple_of(w * depth, depth), depth)
        slot = lax.rem(w, 2)
        return pltpu.make_async_copy(normed_hbm.at[:, :, cols], tiles.at[slot], tile_sem.at[slot])

    fetch(jnp.int32(0)).start()

    @pl.loop(0, n_dp * 2)
    def _(w):
        pl.when(w + 1 < n_dp * 2)(lambda: fetch(w + 1).start())
        fetch(w).wait()
        slot = lax.rem(w, 2)
        d_qkv = jnp.zeros((depth, q_cols + 2 * HEAD_DIM), F32)
        for m in range(micro):
            d_qkv = d_qkv + tn(tiles[slot, :, m * span : (m + 1) * span, :].reshape(length, depth), gqkv[m])
        at = pl.ds(pl.multiple_of(lax.rem(w, 2) * half, half), half)
        dqkv[lax.div(w, 2), at] = d_qkv.astype(BF16).reshape(half, shard, q_cols + 2 * HEAD_DIM)

    qkv_sum.begin()
    for time in range(n.last):
        scatter.step(time)
        first, end = spread_work(n_seq - early, n.last, time)
        gu_sum.reduce(early + first, early + end)
    out_sum.reduce()
    qkv_sum.reduce(0, n_seq)
    scatter.finish(ge_ref)
    gu_sum.end()
    ff_block = dgate_ref.shape[1] // (n_dp * n_seq)
    gain = gains_ref[:, 2 * HEAD_DIM : 2 * HEAD_DIM + 1]
    for t in range(n_seq):
        for i, ref in enumerate((dgate_ref, dup_ref)):
            for owner in range(n_dp):
                cols = slice((owner * n_seq + t) * ff_block, (owner * n_seq + t + 1) * ff_block)
                first = (i * n_dp + owner) * ff_block
                ref[:, cols] = final_gu[t, :, first : first + ff_block].astype(F32) * gain
    qkv_sum.end()
    dqkv_out[...] = final_qkv[...].astype(F32) * gains_ref[:, :1][None]
    out_sum.end()
    dwo_out[...] = final_o[...].astype(F32)
    gather.end()


def backward_call(prefix, branch, q, kv, mixed, cos, sin, gains, pout, normed, wqkv, wo, dgu):
    rows, width = branch.shape
    n_dp, n_seq, shard, gu_cols = dgu.shape
    ff = gu_cols // 2 * n_seq
    micro, length, q_cols = q.shape
    qkv_cols = q_cols + 2 * HEAD_DIM
    any_spec = pl.BlockSpec(memory_space=pl.ANY)
    vmem = pl.BlockSpec(memory_space=pltpu.VMEM)
    line_rows = pltpu.VMEM((n_seq, rows, width), BF16)
    return pl.pallas_call(
        functools.partial(backward_kernel, n_seq, n_dp),
        out_shape=(
            jax.ShapeDtypeStruct((rows, width), F32),
            jax.ShapeDtypeStruct((rows, width), F32),
            jax.ShapeDtypeStruct((n_seq, shard, qkv_cols), F32),
            jax.ShapeDtypeStruct((shard, width), F32),
            jax.ShapeDtypeStruct((shard, ff), F32),
            jax.ShapeDtypeStruct((shard, ff), F32),
        ),
        in_specs=[pl.BlockSpec(memory_space=pltpu.SMEM)] + [vmem] * 7 + [any_spec] * 5,
        out_specs=(vmem,) * 6,
        scratch_shapes=[
            line_rows,
            pltpu.VMEM((2, n_seq, rows, n_seq // 2 * shard), BF16),
            pltpu.VMEM((width, qkv_cols), BF16),
            pltpu.VMEM(wo.shape, BF16),
            pltpu.VMEM((micro, length, q_cols), BF16),
            pltpu.VMEM((length, q_cols), F32),
            pltpu.VMEM((length, q_cols), F32),
            pltpu.VMEM((length, q_cols), F32),
            pltpu.VMEM((micro, length, qkv_cols), BF16),
            line_rows,
            *Scatter.buffers(n_seq, rows, width),
            *Scatter.buffers(n_seq, rows, width),
            pltpu.VMEM((n_dp, n_seq, shard, gu_cols), BF16),
            pltpu.VMEM((n_seq, shard, gu_cols), BF16),
            pltpu.VMEM((n_dp, n_seq, shard, qkv_cols), BF16),
            pltpu.VMEM((n_dp, n_seq, shard, qkv_cols), BF16),
            pltpu.VMEM((n_seq, shard, qkv_cols), BF16),
            pltpu.VMEM((n_dp, shard, width), BF16),
            pltpu.VMEM((n_dp, shard, width), BF16),
            pltpu.VMEM((shard, width), BF16),
            pltpu.SemaphoreType.DMA((3,)),
            pltpu.SemaphoreType.DMA((2,)),
            *Gather.sems(n_seq),
            *Scatter.sems(n_seq),
            *Scatter.sems(n_seq),
            *Collect.sems(n_seq, n_dp),
            *Collect.sems(n_seq, n_dp),
            *OutSum.sems(n_dp),
        ],
        compiler_params=pltpu.CompilerParams(
            collective_id=3, has_side_effects=True, vmem_limit_bytes=VMEM_LIMIT
        ),
        cost_estimate=pl.CostEstimate(flops=10**10, bytes_accessed=40 << 20, transcendentals=0),
        name="backward",
    )(prefix, branch, q, kv, mixed, cos, sin, gains, pout, normed, wqkv, wo, dgu)


def body(
    tokens, cotangent, prefix_len, attn_gain, w_query, w_key, w_value, w_out, mlp_gain, w_gate, w_up, w_down
):
    n_dp = lax.axis_size("dp")
    n_seq = lax.axis_size("seq")
    both = ("dp", "seq")
    micro, span, width = tokens.shape
    shard = w_query.shape[0]
    ff_block = w_down.shape[0]
    length = span * n_seq
    rows = micro * span
    repeat = n_seq // KV_HEADS
    q_cols = HEADS // n_seq * HEAD_DIM

    gain_attn, gain_mlp = attn_gain.astype(F32), mlp_gain.astype(F32)

    def kv_blocks(w):
        w = w.reshape(shard, KV_HEADS, 1, HEAD_DIM)
        return jnp.broadcast_to(w, (shard, KV_HEADS, repeat, HEAD_DIM)).reshape(shard, n_seq, HEAD_DIM)

    def scaled(blocks, gain):
        return (blocks.astype(F32) * gain[:, None, None]).astype(BF16).transpose(1, 0, 2)

    qkv_blocks = scaled(
        jnp.concatenate([w_query.reshape(shard, n_seq, q_cols), kv_blocks(w_key), kv_blocks(w_value)], axis=2),
        gain_attn,
    )

    def ff_blocks(w):
        w = w.reshape(shard, n_dp, n_seq, ff_block).transpose(0, 2, 1, 3)
        return w.reshape(shard, n_seq, n_dp * ff_block)

    gu_blocks = scaled(jnp.concatenate([ff_blocks(w_gate), ff_blocks(w_up)], axis=2), gain_mlp)

    cos_one, sin_one = rope_table(jnp.arange(length, dtype=jnp.int32), HEAD_DIM)
    half = HEAD_DIM // 2
    sin_one = jnp.concatenate([-sin_one[:, :half], sin_one[:, half:]], axis=1)
    count = q_cols // HEAD_DIM + 1
    cos = jnp.concatenate([jnp.tile(cos_one, (1, count)), jnp.ones((length, HEAD_DIM), F32)], axis=1)
    sin = jnp.concatenate([jnp.tile(sin_one, (1, count)), jnp.zeros((length, HEAD_DIM), F32)], axis=1)

    tok = tokens.reshape(rows, width)
    cot = cotangent.reshape(rows, width)
    hidden, normed_mlp, q, kv, mixed, normed_all, cot_all, wqkv, wo, wgu, wd = attention_call(
        prefix_len, tok, cot, cos, sin, qkv_blocks, gu_blocks, w_out, w_down, n_seq, n_dp
    )
    ge_mlp, out_part, dgu, w_down_grad = mlp_call(
        normed_mlp, cot_all, wgu.reshape(width, -1), wd.reshape(-1, width), n_seq, n_dp
    )

    def norm_back(u, ge):
        r = lax.rsqrt(jnp.mean(u * u, axis=1, keepdims=True) + EPSILON)
        return r * ge - u * (r * r * r * jnp.mean(u * ge, axis=1, keepdims=True)), jnp.sum(ge * u * r, axis=0)

    back, gain_mlp_part = norm_back(hidden, ge_mlp)
    grad_hidden = cot.astype(F32) + back
    gains = jnp.concatenate(
        [jnp.broadcast_to(g[:, None], (shard, 2 * HEAD_DIM)) for g in (gain_attn, gain_mlp)], axis=1
    )
    ge_attn, out_sum, qkv_grad, w_out_grad, w_gate_grad, w_up_grad = backward_call(
        prefix_len, grad_hidden.astype(BF16), q, kv, mixed, cos, sin, gains, out_part, normed_all,
        wqkv.reshape(width, -1), wo.reshape(-1, width), dgu.reshape(n_dp, n_seq, shard, -1),
    )
    block_out = (hidden + out_sum).astype(BF16)
    back, gain_attn_part = norm_back(tok.astype(F32), ge_attn)
    input_grad = grad_hidden + back

    qkv_grad = qkv_grad.transpose(1, 0, 2)
    w_query_grad = qkv_grad[:, :, :q_cols].reshape(shard, -1)

    def kv_grad(values):
        return values.reshape(shard, KV_HEADS, repeat, HEAD_DIM).sum(axis=2).reshape(shard, -1)

    w_key_grad = kv_grad(qkv_grad[:, :, q_cols : q_cols + HEAD_DIM])
    w_value_grad = kv_grad(qkv_grad[:, :, q_cols + HEAD_DIM :])
    gain_parts = jnp.stack([gain_attn_part, gain_mlp_part], axis=1).reshape(n_dp * n_seq, shard, 2)
    gain_grads = lax.all_to_all(gain_parts, both, split_axis=0, concat_axis=0, tiled=True).sum(axis=0)
    return (
        block_out.reshape(micro, span, width),
        input_grad.reshape(micro, span, width),
        gain_grads[:, 0] / gain_attn,
        w_query_grad,
        w_key_grad,
        w_value_grad,
        w_out_grad,
        gain_grads[:, 1] / gain_mlp,
        w_gate_grad,
        w_up_grad,
        w_down_grad,
    )


def solution(mesh):
    rows = P("dp", "seq", None)
    vec = P(("dp", "seq"))
    mat = P(("dp", "seq"), None)
    in_specs = (rows, rows, P("dp"), vec, mat, mat, mat, mat, vec, mat, mat, mat)
    out_specs = (rows, rows, vec, mat, mat, mat, mat, vec, mat, mat, mat)
    return jax.shard_map(body, mesh=mesh, in_specs=in_specs, out_specs=out_specs, check_vma=False)
```

```python
import functools
import math

import jax
import jax.numpy as jnp
import numpy as np
from jax import lax
from jax.experimental import pallas as pl
from jax.experimental.pallas import tpu as pltpu
from jax.sharding import PartitionSpec as P

HEADS = 32
KV_HEADS = 8
HEAD_DIM = 64
EPSILON = 1e-05
THETA = 500000.0
NEGATIVE = -1e30
BF16 = jnp.bfloat16
F32 = jnp.float32
MESH = pl.DeviceIdType.MESH
TILE = 256
QUERY_TILE = 256
AHEAD = 4
VMEM_LIMIT = 61 << 20


def rope_tables(length, q_cols):
    half = HEAD_DIM // 2
    f32 = np.float32
    index_half = np.arange(half, dtype=f32)
    inverse = np.power(f32(THETA), f32(-2.0) * index_half / f32(HEAD_DIM)).astype(f32)
    wavelength = (f32(2.0 * math.pi) / inverse).astype(f32)
    smooth = ((f32(8192.0) / wavelength - f32(1.0)) / f32(3.0)).astype(f32)
    blended = ((f32(1.0) - smooth) * inverse / f32(32.0) + smooth * inverse).astype(f32)
    inverse = np.where(
        wavelength < 2048.0, inverse, np.where(wavelength > 8192.0, inverse / f32(32.0), blended)
    ).astype(f32)
    angles = (np.arange(length, dtype=f32)[:, None] * inverse[None, :]).astype(f32)
    cos, sin = np.cos(angles).astype(f32), np.sin(angles).astype(f32)
    count = q_cols // HEAD_DIM + 1
    ones, zeros = np.ones((length, HEAD_DIM), f32), np.zeros((length, HEAD_DIM), f32)
    cos = np.concatenate([cos, cos] * count + [ones], axis=1)
    sin = np.concatenate([-sin, sin] * count + [zeros], axis=1)
    return jnp.asarray(cos), jnp.asarray(sin)


def nn(a, b):
    return jnp.dot(a, b, preferred_element_type=F32)


def tn(a, b):
    return lax.dot_general(a, b, (((0,), (0,)), ((), ())), preferred_element_type=F32)


def nt(a, b):
    return lax.dot_general(a, b, (((1,), (1,)), ((), ())), preferred_element_type=F32)


class Line:
    def __init__(self, n_seq):
        self.n_line = n_seq // 2
        self.last = self.n_line - 1
        self.s = lax.axis_index("seq")
        self.c = lax.rem(self.s, 2)
        self.l = lax.div(self.s, 2)
        self.sibling = self.s + 1 - 2 * self.c
        self.right = jnp.minimum(self.s + 2, n_seq - 2 + self.c)
        self.left = jnp.maximum(self.s - 2, self.c)
        self.has_right = self.l < self.last
        self.has_left = self.l > 0

    def greet(self, n_dp):
        barrier = pltpu.get_barrier_semaphore()
        d = lax.axis_index("dp")
        for k in range(1, n_dp):
            pl.semaphore_signal(barrier, 1, device_id={"dp": lax.rem(d + k, n_dp)}, device_id_type=MESH)
        pl.semaphore_signal(barrier, 1, device_id={"seq": self.sibling}, device_id_type=MESH)

        @pl.when(self.has_right)
        def _():
            pl.semaphore_signal(barrier, 1, device_id={"seq": self.right}, device_id_type=MESH)

        @pl.when(self.has_left)
        def _():
            pl.semaphore_signal(barrier, 1, device_id={"seq": self.left}, device_id_type=MESH)

        pl.semaphore_wait(barrier, n_dp - 1 + jnp.where(self.has_right & self.has_left, 3, 2))

    def order(self, j):
        near = jnp.minimum(self.l, self.last - self.l)
        half = lax.div(j + 1, 2)
        both = jnp.where(lax.rem(j, 2) == 1, self.l - half, self.l + half)
        far = jnp.where(self.l <= self.last - self.l, j, self.last - j)
        return jnp.where(j <= 2 * near, both, far)


def remote(src, dst, send, recv, seq):
    return pltpu.make_async_remote_copy(
        src_ref=src, dst_ref=dst, send_sem=send, recv_sem=recv, device_id={"seq": seq}, device_id_type=MESH
    )


class Gather:
    def __init__(self, line, full, send_z, send_c, recv, m=None):
        self.m = m
        self.line, self.full, self.send_z, self.send_c, self.recv = line, full, send_z, send_c, recv

    @staticmethod
    def sems(n_seq):
        n_line = n_seq // 2
        return [
            pltpu.SemaphoreType.DMA((n_line + 1,)),
            pltpu.SemaphoreType.DMA((n_line,)),
            pltpu.SemaphoreType.DMA((n_seq,)),
        ]

    def copy(self, index, send, seq):
        chunk = self.full.at[index] if self.m is None else self.full.at[self.m, index]
        return remote(chunk, chunk, send, self.recv.at[index], seq)

    def begin(self):
        n = self.line
        pl.when(n.has_right)(lambda: self.copy(n.s, self.send_z.at[n.l], n.right).start())
        pl.when(n.has_left)(lambda: self.copy(n.s, self.send_z.at[n.n_line], n.left).start())
        self.copy(n.s, self.send_c.at[n.l], n.sibling).start()

    def visit(self, chip):
        n = self.line
        mine = 2 * chip + n.c

        @pl.when(chip != n.l)
        def _():
            self.copy(mine, self.send_c.at[chip], n.sibling).wait_recv()
            pl.when((chip < n.l) & n.has_right)(
                lambda: self.copy(mine, self.send_z.at[chip], n.right).start()
            )
            pl.when((chip > n.l) & n.has_left)(
                lambda: self.copy(mine, self.send_z.at[chip], n.left).start()
            )
            self.copy(mine, self.send_c.at[chip], n.sibling).start()

        self.copy(2 * chip + 1 - n.c, self.send_c.at[chip], n.sibling).wait_recv()

    def end(self):
        n = self.line

        @pl.loop(0, n.n_line)
        def _(chip):
            mine = 2 * chip + n.c
            self.copy(mine, self.send_c.at[chip], n.sibling).wait_send()
            pl.when((chip <= n.l) & n.has_right)(
                lambda: self.copy(mine, self.send_z.at[chip], n.right).wait_send()
            )
            pl.when((chip > n.l) & n.has_left)(
                lambda: self.copy(mine, self.send_z.at[chip], n.left).wait_send()
            )

        pl.when(n.has_left)(lambda: self.copy(n.s, self.send_z.at[n.n_line], n.left).wait_send())


class Scatter:
    def __init__(self, line, part, sib, rcv, send_z, send_c, recv_z, recv_c, m=None):
        self.line, self.m = line, m
        self.part, self.sib, self.rcv = part, sib, rcv
        self.send_z, self.send_c, self.recv_z, self.recv_c = send_z, send_c, recv_z, recv_c

    @staticmethod
    def sems(n_seq):
        n_line = n_seq // 2
        return [
            pltpu.SemaphoreType.DMA((n_line,)),
            pltpu.SemaphoreType.DMA((n_line,)),
            pltpu.SemaphoreType.DMA((n_line + 1,)),
            pltpu.SemaphoreType.DMA((n_line,)),
        ]

    @staticmethod
    def buffers(n_seq, rows, width, *lead):
        n_line = n_seq // 2
        return [
            pltpu.VMEM((*lead, n_line, rows, width), BF16),
            pltpu.VMEM((*lead, n_line + 1, rows, width), BF16),
        ]

    def at(self, index):
        return index if self.m is None else (self.m, index)

    def across(self, chip):
        n = self.line
        return remote(
            self.part.at[self.at(2 * chip + 1 - n.c)],
            self.sib.at[self.at(chip)],
            self.send_c.at[chip],
            self.recv_c.at[chip],
            n.sibling,
        )

    def hop(self, chip, slot, seq):
        n = self.line
        return remote(
            self.part.at[self.at(2 * chip + n.c)],
            self.rcv.at[self.at(slot)],
            self.send_z.at[chip],
            self.recv_z.at[slot],
            seq,
        )

    def begin(self):
        n = self.line

        @pl.loop(0, n.n_line)
        def _(j):
            half = lax.div(j, 2)
            self.across(jnp.where(lax.rem(j, 2) == 0, n.last - half, half)).start()

    def add(self, chip, source):
        mine = self.at(2 * chip + self.line.c)
        self.part[mine] = (self.part[mine].astype(F32) + source.astype(F32)).astype(BF16)

    def step(self, time):
        n = self.line

        @pl.when(n.l <= time)
        def _():
            chip = n.last - time + n.l
            self.across(chip).wait_recv()
            self.add(chip, self.sib[self.at(chip)])

            @pl.when(n.has_left)
            def _():
                self.hop(chip, chip, n.right).wait_recv()
                self.add(chip, self.rcv[self.at(chip)])

            self.hop(chip, chip, n.right).start()

        @pl.when(n.last - n.l <= time)
        def _():
            chip = time - n.last + n.l
            self.across(chip).wait_recv()
            self.add(chip, self.sib[self.at(chip)])

            @pl.when(n.has_right)
            def _():
                self.hop(chip, chip, n.left).wait_recv()
                self.add(chip, self.rcv[self.at(chip)])

            self.hop(chip, jnp.where(chip == n.l - 1, n.n_line, chip), n.left).start()

    def finish(self, out, add=False):
        n = self.line
        mine = 2 * n.l + n.c
        self.across(n.l).wait_recv()
        value = self.part[self.at(mine)].astype(F32) + self.sib[self.at(n.l)].astype(F32)
        out[...] = out[...] + value if add else value

        @pl.when(n.has_left)
        def _():
            self.hop(n.l, n.l, n.right).wait_recv()
            out[...] += self.rcv[self.at(n.l)].astype(F32)

        @pl.when(n.has_right)
        def _():
            self.hop(n.l, n.n_line, n.left).wait_recv()
            out[...] += self.rcv[self.at(n.n_line)].astype(F32)

        @pl.loop(0, n.n_line)
        def _(chip):
            self.across(chip).wait_send()
            pl.when(chip > n.l)(lambda: self.hop(chip, chip, n.right).wait_send())
            pl.when(chip < n.l)(lambda: self.hop(chip, chip, n.left).wait_send())


def norm_back(u, ge):
    r = lax.rsqrt(jnp.mean(u * u, axis=1, keepdims=True) + EPSILON)
    return r * ge - u * (r * r * r * jnp.mean(u * ge, axis=1, keepdims=True))


def spread_work(units, slots, index):
    return (units * index // slots, units * (index + 1) // slots)


class Square:
    def __init__(self):
        self.d = lax.axis_index("dp")
        self.first = self.d + 1 - 2 * lax.rem(self.d, 2)
        self.second = lax.rem(self.d + 2, 4)
        self.across = 3 - self.d


class Spread:
    def __init__(self, line, n_dp, relay, blocks, dst, own_sem, send_z, send_xy, recv, recv_half):
        self.line, self.n_dp, self.blocks, self.dst = line, n_dp, blocks, dst
        self.relay = relay and n_dp == 4
        self.own_sem, self.send_z, self.send_xy, self.recv, self.recv_half = own_sem, send_z, send_xy, recv, recv_half
        self.n_seq = 2 * line.n_line
        self.d = lax.axis_index("dp")
        self.square = Square()
        self.half = blocks.shape[1] // 2

    @staticmethod
    def sems(n_seq, n_dp):
        return [
            pltpu.SemaphoreType.DMA((1,)),
            pltpu.SemaphoreType.DMA((n_seq,)),
            pltpu.SemaphoreType.DMA((n_seq, n_dp)),
            pltpu.SemaphoreType.DMA((n_dp, n_seq)),
            pltpu.SemaphoreType.DMA((n_seq,)),
        ]

    def source(self, j):
        return lax.rem(self.line.s - j + self.n_seq, self.n_seq)

    def hop(self, t):
        n = self.line
        return pltpu.make_async_remote_copy(
            src_ref=self.blocks.at[t],
            dst_ref=self.dst.at[self.d, n.s],
            send_sem=self.send_z.at[t],
            recv_sem=self.recv.at[self.d, n.s],
            device_id={"seq": t},
            device_id_type=MESH,
        )

    def own(self):
        n = self.line
        return pltpu.make_async_copy(self.blocks.at[n.s], self.dst.at[self.d, n.s], self.own_sem.at[0])

    def to_dp(self, src, dst, send, recv, peer):
        return pltpu.make_async_remote_copy(
            src_ref=src, dst_ref=dst, send_sem=send, recv_sem=recv, device_id={"dp": peer}, device_id_type=MESH
        )

    def over(self, source, own=False):
        src = self.blocks.at[self.line.s] if own else self.dst.at[self.d, source]
        peers = [lax.rem(self.d + k, self.n_dp) for k in range(1, self.n_dp)]
        if self.relay:
            peers = [self.square.first, self.square.second]
        return [
            self.to_dp(src, self.dst.at[self.d, source], self.send_xy.at[source, k + 1], self.recv.at[self.d, source], peer)
            for k, peer in enumerate(peers)
        ]

    def landed(self, d, source):
        block = self.dst.at[d, source]
        return self.to_dp(block, block, self.send_z.at[0], self.recv.at[d, source], d)

    def halves(self, source):
        low, high = pl.ds(0, self.half), pl.ds(self.half, self.half)
        one = self.dst.at[self.square.first, source, low]
        two = self.dst.at[self.square.second, source, high]
        return (
            self.to_dp(one, one, self.send_xy.at[source, 3], self.recv.at[self.square.first, source], self.square.second),
            self.to_dp(two, two, self.send_xy.at[source, 0], self.recv_half.at[source], self.square.first),
        )

    def pass_on(self, j):
        if not self.relay:
            return

        @pl.when(j < self.n_seq)
        def _():
            source = self.source(j)
            one, two = self.halves(source)
            self.landed(self.square.first, source).wait_recv()
            one.start()
            self.landed(self.square.second, source).wait_recv()
            two.start()

    def begin(self, end):
        n = self.line

        @pl.loop(1, end)
        def _(j):
            self.hop(lax.rem(n.s + j, self.n_seq)).start()

        self.own().start()

    def forward_one(self, j, ahead):
        n = self.line

        @pl.when(j < self.n_seq)
        def _():
            pl.when(j + ahead < self.n_seq)(lambda: self.hop(lax.rem(n.s + j + ahead, self.n_seq)).start())
            source = self.source(j)
            self.landed(self.d, source).wait_recv()
            for copy in self.over(source):
                copy.start()

    def forward_own(self):
        for copy in self.over(self.line.s, True):
            copy.start()

    def arrive(self):
        @pl.loop(0, self.n_seq)
        def _(source):
            if self.relay:
                low, high = pl.ds(0, self.half), pl.ds(self.half, self.half)
                one = self.dst.at[self.square.across, source, low]
                two = self.dst.at[self.square.across, source, high]
                self.to_dp(one, one, self.send_z.at[0], self.recv.at[self.square.across, source], self.d).wait_recv()
                self.to_dp(two, two, self.send_z.at[0], self.recv_half.at[source], self.d).wait_recv()
            else:
                for k in range(1, self.n_dp):
                    self.landed(lax.rem(self.d + k, self.n_dp), source).wait_recv()

        self.own().wait()

    def end(self):
        n = self.line

        @pl.loop(0, self.n_seq)
        def _(j):
            pl.when(j != n.s)(lambda: self.hop(j).wait_send())
            for copy in self.over(j):
                copy.wait_send()
            if self.relay:
                for copy in self.halves(j):
                    copy.wait_send()


class Copies:
    def __init__(self, n_dp, own, dst, own_sem, send, recv):
        self.n_dp, self.own_ref, self.dst = n_dp, own, dst
        self.own_sem, self.send, self.recv = own_sem, send, recv
        self.d = lax.axis_index("dp")
        self.relay = n_dp == 4
        self.square = Square()
        self.half = own.shape[0] // 2

    @staticmethod
    def sems(n_dp):
        return [
            pltpu.SemaphoreType.DMA((1,)),
            pltpu.SemaphoreType.DMA((n_dp,)),
            pltpu.SemaphoreType.DMA((n_dp + 1,)),
        ]

    def copy(self, src, slot, part, send, recv, peer):
        return pltpu.make_async_remote_copy(
            src_ref=src,
            dst_ref=self.dst.at[slot] if part is None else self.dst.at[slot, part],
            send_sem=self.send.at[send],
            recv_sem=self.recv.at[recv],
            device_id={"dp": peer},
            device_id_type=MESH,
        )

    def direct(self):
        peers = [lax.rem(self.d + k, self.n_dp) for k in range(1, self.n_dp)]
        if self.relay:
            peers = [self.square.first, self.square.second]
        return [self.copy(self.own_ref, self.d, None, k + 1, self.d, peer) for k, peer in enumerate(peers)]

    def landed(self, slot):
        return self.copy(self.dst.at[slot], slot, None, 0, slot, slot)

    def halves(self):
        q = self.square
        low, high = pl.ds(0, self.half), pl.ds(self.half, self.half)
        return (
            self.copy(self.dst.at[q.first, low], q.first, low, 3, q.first, q.second),
            self.copy(self.dst.at[q.second, high], q.second, high, 0, self.n_dp, q.first),
        )

    def own(self):
        return pltpu.make_async_copy(self.own_ref, self.dst.at[self.d], self.own_sem.at[0])

    def begin(self):
        for copy in self.direct():
            copy.start()
        self.own().start()

    def pass_on(self):
        if not self.relay:
            return
        one, two = self.halves()
        self.landed(self.square.first).wait_recv()
        one.start()
        self.landed(self.square.second).wait_recv()
        two.start()

    def end(self):
        for copy in self.direct():
            copy.wait_send()
        if self.relay:
            low, high = pl.ds(0, self.half), pl.ds(self.half, self.half)
            across = self.square.across
            self.copy(self.dst.at[across, low], across, low, 0, across, across).wait_recv()
            self.copy(self.dst.at[across, high], across, high, 0, self.n_dp, across).wait_recv()
            for copy in self.halves():
                copy.wait_send()
        else:
            for k in range(1, self.n_dp):
                self.landed(lax.rem(self.d + k, self.n_dp)).wait_recv()
        self.own().wait()


class Relay:
    def __init__(self, line, n_dp):
        n_seq = 2 * line.n_line
        self.n_dp = n_dp
        self.d = lax.axis_index("dp")
        block = self.d * n_seq + line.s
        self.slot, self.target = lax.rem(block, n_dp), lax.div(block, n_dp)
        block = line.s * n_dp + self.d
        self.owner_d, self.owner_s = lax.div(block, n_seq), lax.rem(block, n_seq)
        self.stays = (self.slot == self.d) & (self.target == line.s)
        self.moves = jnp.logical_not(self.stays)

    def to_relay(self, src, dst, send, recv):
        return pltpu.make_async_remote_copy(
            src_ref=src, dst_ref=dst, send_sem=send, recv_sem=recv,
            device_id=(self.slot, self.target), device_id_type=MESH,
        )

    def to_owner(self, src, dst, send, recv):
        return pltpu.make_async_remote_copy(
            src_ref=src, dst_ref=dst, send_sem=send, recv_sem=recv,
            device_id=(self.owner_d, self.owner_s), device_id_type=MESH,
        )

    def over(self, k, src, dst, send, recv):
        return pltpu.make_async_remote_copy(
            src_ref=src, dst_ref=dst, send_sem=send, recv_sem=recv,
            device_id={"dp": lax.rem(self.d + k, self.n_dp)}, device_id_type=MESH,
        )


class OutRows(Relay):
    def __init__(self, line, n_dp, own, dst, own_sem, send_z, send_xy, recv):
        super().__init__(line, n_dp)
        self.own_ref, self.dst = own, dst
        self.own_sem, self.send_z, self.send_xy, self.recv = own_sem, send_z, send_xy, recv

    @staticmethod
    def sems(n_dp):
        return [
            pltpu.SemaphoreType.DMA((1,)),
            pltpu.SemaphoreType.DMA((1,)),
            pltpu.SemaphoreType.DMA((n_dp,)),
            pltpu.SemaphoreType.DMA((n_dp,)),
        ]

    def hop(self):
        return self.to_relay(self.own_ref, self.dst.at[self.slot], self.send_z.at[0], self.recv.at[self.slot])

    def own(self):
        return pltpu.make_async_copy(self.own_ref, self.dst.at[self.slot], self.own_sem.at[0])

    def copy(self, k):
        return self.over(k, self.dst.at[self.d], self.dst.at[self.d], self.send_xy.at[k], self.recv.at[self.d])

    def landed(self, slot):
        return self.over(1, self.dst.at[slot], self.dst.at[slot], self.send_xy.at[1], self.recv.at[slot])

    def begin(self):
        pl.when(self.stays)(lambda: self.own().start())
        pl.when(self.moves)(lambda: self.hop().start())

    def forward(self):
        pl.when(self.stays)(lambda: self.own().wait())
        pl.when(self.moves)(lambda: self.landed(self.d).wait_recv())
        for k in range(1, self.n_dp):
            self.copy(k).start()

    def arrive(self):
        for k in range(1, self.n_dp):
            self.landed(lax.rem(self.d + k, self.n_dp)).wait_recv()

    def end(self):
        pl.when(self.moves)(lambda: self.hop().wait_send())
        for k in range(1, self.n_dp):
            self.copy(k).wait_send()


class OutSum(Relay):
    def __init__(self, line, n_dp, src, land, final, own_sem, send_xy, recv_xy, send_z, recv_z):
        super().__init__(line, n_dp)
        self.src, self.land, self.final = src, land, final
        self.own_sem, self.send_xy, self.recv_xy, self.send_z, self.recv_z = own_sem, send_xy, recv_xy, send_z, recv_z

    @staticmethod
    def sems(n_dp):
        return [
            pltpu.SemaphoreType.DMA((1,)),
            pltpu.SemaphoreType.DMA((n_dp,)),
            pltpu.SemaphoreType.DMA((n_dp,)),
            pltpu.SemaphoreType.DMA((1,)),
            pltpu.SemaphoreType.DMA((1,)),
        ]

    def copy(self, k):
        return self.over(
            k, self.src.at[lax.rem(self.d + k, self.n_dp)], self.land.at[self.d], self.send_xy.at[k], self.recv_xy.at[self.d]
        )

    def landed(self, owner):
        return self.over(1, self.land.at[owner], self.land.at[owner], self.send_xy.at[1], self.recv_xy.at[owner])

    def own(self):
        return pltpu.make_async_copy(self.src.at[self.d], self.land.at[self.d], self.own_sem.at[0])

    def hop(self):
        return self.to_owner(self.land.at[self.d], self.final, self.send_z.at[0], self.recv_z.at[0])

    def begin(self):
        self.own().start()
        for k in range(1, self.n_dp):
            self.copy(k).start()

    def reduce(self):
        self.own().wait()
        for k in range(1, self.n_dp):
            self.landed(lax.rem(self.d + k, self.n_dp)).wait_recv()
        total = self.land[0].astype(F32)
        for owner in range(1, self.n_dp):
            total = total + self.land[owner].astype(F32)
        total = total.astype(BF16)

        @pl.when(self.stays)
        def _():
            self.final[...] = total

        @pl.when(self.moves)
        def _():
            self.land[self.d] = total
            self.hop().start()

    def end(self):
        pl.when(self.moves)(lambda: self.hop().wait())
        for k in range(1, self.n_dp):
            self.copy(k).wait_send()


class Collect:
    def __init__(self, line, n_dp, src, land, final, own_sem, send_xy, recv_xy, send_z, recv_z):
        self.line, self.n_dp, self.n_seq = line, n_dp, 2 * line.n_line
        self.src, self.land, self.final = src, land, final
        self.own_sem, self.send_xy, self.recv_xy, self.send_z, self.recv_z = own_sem, send_xy, recv_xy, send_z, recv_z
        self.d = lax.axis_index("dp")

    @staticmethod
    def sems(n_seq, n_dp):
        return [
            pltpu.SemaphoreType.DMA((1,)),
            pltpu.SemaphoreType.DMA((n_seq, n_dp)),
            pltpu.SemaphoreType.DMA((n_dp, n_seq)),
            pltpu.SemaphoreType.DMA((n_seq,)),
            pltpu.SemaphoreType.DMA((n_seq,)),
        ]

    def over(self, t, k):
        peer = lax.rem(self.d + k, self.n_dp)
        return pltpu.make_async_remote_copy(
            src_ref=self.src.at[peer, t],
            dst_ref=self.land.at[self.d, t],
            send_sem=self.send_xy.at[t, k],
            recv_sem=self.recv_xy.at[self.d, t],
            device_id={"dp": peer},
            device_id_type=MESH,
        )

    def landed(self, owner, t):
        return pltpu.make_async_remote_copy(
            src_ref=self.land.at[owner, t],
            dst_ref=self.land.at[owner, t],
            send_sem=self.send_xy.at[t, 1],
            recv_sem=self.recv_xy.at[owner, t],
            device_id={"dp": owner},
            device_id_type=MESH,
        )

    def own(self):
        return pltpu.make_async_copy(self.src.at[self.d], self.land.at[self.d], self.own_sem.at[0])

    def hop(self, t, slot):
        return pltpu.make_async_remote_copy(
            src_ref=self.land.at[self.d, t],
            dst_ref=self.final.at[slot],
            send_sem=self.send_z.at[t],
            recv_sem=self.recv_z.at[slot],
            device_id={"seq": t},
            device_id_type=MESH,
        )

    def place(self, j):
        return lax.rem(self.line.s + 1 + j, self.n_seq)

    def begin(self, ahead):
        self.ahead = ahead
        self.own().start()

        @pl.loop(0, ahead)
        def _(j):
            self.send(j)

    def send(self, j):
        for k in range(1, self.n_dp):
            self.over(self.place(j), k).start()

    def reduce(self, first, end):
        if first == 0:
            self.own().wait()

        @pl.loop(first, end)
        def _(j):
            t = self.place(j)
            pl.when(j + self.ahead < self.n_seq)(lambda: self.send(j + self.ahead))
            for k in range(1, self.n_dp):
                self.landed(lax.rem(self.d + k, self.n_dp), t).wait_recv()
            total = self.land[0, t].astype(F32)
            for owner in range(1, self.n_dp):
                total = total + self.land[owner, t].astype(F32)
            total = total.astype(BF16)

            @pl.when(t == self.line.s)
            def _():
                self.final[t] = total

            @pl.when(t != self.line.s)
            def _():
                self.land[self.d, t] = total
                self.hop(t, self.line.s).start()

    def end(self):
        @pl.loop(0, self.n_seq)
        def _(t):
            pl.when(t != self.line.s)(lambda: self.hop(t, t).wait())
            for k in range(1, self.n_dp):
                self.over(t, k).wait_send()


class RowSum:
    def __init__(self, n_dp, src, land, own_sem, send, recv):
        self.n_dp, self.src, self.land = n_dp, src, land
        self.own_sem, self.send, self.recv = own_sem, send, recv
        self.d = lax.axis_index("dp")

    @staticmethod
    def sems(n_dp):
        return [
            pltpu.SemaphoreType.DMA((1,)),
            pltpu.SemaphoreType.DMA((n_dp,)),
            pltpu.SemaphoreType.DMA((n_dp,)),
        ]

    def copy(self, k, slot):
        peer = lax.rem(self.d + k, self.n_dp)
        return pltpu.make_async_remote_copy(
            src_ref=self.src.at[peer],
            dst_ref=self.land.at[slot],
            send_sem=self.send.at[k],
            recv_sem=self.recv.at[slot],
            device_id={"dp": peer},
            device_id_type=MESH,
        )

    def own(self):
        return pltpu.make_async_copy(self.src.at[self.d], self.land.at[self.d], self.own_sem.at[0])

    def begin(self):
        self.own().start()
        for k in range(1, self.n_dp):
            self.copy(k, self.d).start()

    def finish(self, out):
        self.own().wait()
        for k in range(1, self.n_dp):
            self.copy(k, lax.rem(self.d + k, self.n_dp)).wait()
        total = self.land[0].astype(F32)
        for owner in range(1, self.n_dp):
            total = total + self.land[owner].astype(F32)
        out[...] = total


def greet_all(line, n_dp, relay):
    barrier = pltpu.get_barrier_semaphore()
    n_seq = 2 * line.n_line
    d = lax.axis_index("dp")
    for j in range(1, n_seq):
        pl.semaphore_signal(barrier, 1, device_id={"seq": lax.rem(line.s + j, n_seq)}, device_id_type=MESH)
    for k in range(1, n_dp):
        pl.semaphore_signal(barrier, 1, device_id={"dp": lax.rem(d + k, n_dp)}, device_id_type=MESH)

    if relay is None:
        pl.semaphore_wait(barrier, n_seq + n_dp - 2)
        return

    @pl.when(relay.moves)
    def _():
        for device in ((relay.slot, relay.target), (relay.owner_d, relay.owner_s)):
            pl.semaphore_signal(barrier, 1, device_id=device, device_id_type=MESH)

    pl.semaphore_wait(barrier, n_seq + n_dp - 2 + jnp.where(relay.moves, 2, 0))


def turn(values, lanes_low):
    half = HEAD_DIM // 2
    width = values.shape[-1]
    return jnp.where(
        lanes_low, pltpu.roll(values, width - half, values.ndim - 1), pltpu.roll(values, half, values.ndim - 1)
    )


def low_lanes(shape):
    return lax.rem(lax.broadcasted_iota(jnp.int32, shape, len(shape) - 1), HEAD_DIM) < HEAD_DIM // 2


def head_lanes(kv, h, q_cols):
    wide = jnp.concatenate([kv] * (q_cols // (2 * HEAD_DIM)), axis=1).astype(F32)
    swapped = pltpu.roll(wide, HEAD_DIM, 1)
    here = lax.div(lax.broadcasted_iota(jnp.int32, wide.shape, 1), HEAD_DIM) == h
    key, value = (wide, swapped) if h % 2 == 0 else (swapped, wide)
    key = jnp.where(here, key * (1.0 / math.sqrt(HEAD_DIM)), 0.0).astype(BF16)
    return key, jnp.where(here, value, 0.0).astype(BF16)


def hidden_keys(first, second, prefix, query_axis):
    query, key = (first, second) if query_axis == 0 else (second, first)
    return jnp.where((key <= query) | (key < prefix), 0.0, NEGATIVE)


def bias_shape(length):
    return (length, length) if length <= 2 * QUERY_TILE else (8, 128)


def fill_bias(bias, prefix, query_axis, length):
    if bias.shape[0] != length:
        return
    tile = min(length, QUERY_TILE)

    @pl.loop(0, length // tile)
    def _(i):
        at = pl.ds(pl.multiple_of(i * tile, tile), tile)
        first = i * tile + lax.broadcasted_iota(jnp.int32, (tile, length), 0)
        second = lax.broadcasted_iota(jnp.int32, (tile, length), 1)
        bias[at, :] = hidden_keys(first, second, prefix, query_axis)


def bias_tile(bias, prefix, query_axis, length, tile, i):
    at = pl.ds(pl.multiple_of(i * tile, tile), tile)
    if bias.shape[0] == length:
        return bias[at, :] if query_axis == 0 else bias[:, at]
    shape = (tile, length) if query_axis == 0 else (length, tile)
    first = lax.broadcasted_iota(jnp.int32, shape, 0)
    second = lax.broadcasted_iota(jnp.int32, shape, 1)
    if query_axis == 0:
        first = first + i * tile
    else:
        second = second + i * tile
    return hidden_keys(first, second, prefix, query_axis)


def attention_kernel(
    n_seq, n_dp, prefix_ref, tok_ref, cot_ref, cos_ref, sin_ref, gains_ref,
    w_query_ref, w_key_ref, w_value_ref, w_gate_ref, w_up_ref, wo_own, wd_own,
    hidden_ref, nmlp_ref, q_ref, kv_ref, mixed_ref, normed_hbm, cot_hbm, wqkv_hbm, wo_hbm, wgu_hbm, wd_hbm,
    full, cot, wqkv, wo, acc, part, sib, rcv, qkvb, gub, bias, save_sem, *sems,
):
    n = Line(n_seq)
    rows, width = tok_ref.shape
    micro, length, q_cols = q_ref.shape
    span = rows // micro
    cols_all = wqkv.shape[3]
    pair = 2 * rows
    tok = tok_ref[...].astype(F32)
    normed = (tok * lax.rsqrt(jnp.mean(tok * tok, axis=1, keepdims=True) + EPSILON)).astype(BF16)
    for m in range(micro):
        full[m, n.s] = normed[m * span : (m + 1) * span]
    cot[n.s] = cot_ref[...]

    sems = list(sems)
    take = lambda count: [sems.pop(0) for _ in range(count)]
    gathers = [Gather(n, full, *take(3), m=m) for m in range(micro)]
    scatters = [Scatter(n, part, sib, rcv, *take(4), m=m) for m in range(micro)]
    gather_cot = Gather(n, cot, *take(3))
    qkv_w = Spread(n, n_dp, False, qkvb, wqkv, *take(5))
    gu_w = Spread(n, n_dp, True, gub, wgu_hbm, *take(5))
    out_w = OutRows(n, n_dp, wo_own, wo, *take(4))
    down_w = Copies(n_dp, wd_own, wd_hbm, *take(3))

    repeat = n_seq // KV_HEADS
    ff_block = wd_own.shape[0]
    gain_attn = gains_ref[:, :1]
    gain_mlp = gains_ref[:, 2 * HEAD_DIM : 2 * HEAD_DIM + 1]
    for t in range(n_seq):
        head = slice(t // repeat * HEAD_DIM, (t // repeat + 1) * HEAD_DIM)
        qkvb[t, :, :q_cols] = (w_query_ref[:, t * q_cols : (t + 1) * q_cols].astype(F32) * gain_attn).astype(BF16)
        key_value = jnp.concatenate([w_key_ref[:, head], w_value_ref[:, head]], axis=1)
        qkvb[t, :, q_cols:] = (key_value.astype(F32) * gain_attn).astype(BF16)

    greet_all(n, n_dp, out_w)
    qkv_w.begin(n_seq)
    gathers[0].begin()
    out_w.begin()
    qkv_w.forward_own()
    for i, ref in enumerate((w_gate_ref, w_up_ref)):
        for owner in range(n_dp):
            for t in range(n_seq):
                cols = slice((owner * n_seq + t) * ff_block, (owner * n_seq + t + 1) * ff_block)
                first = (i * n_dp + owner) * ff_block
                gub[t, :, first : first + ff_block] = (ref[:, cols].astype(F32) * gain_mlp).astype(BF16)

    @pl.loop(1, n_seq)
    def _(j):
        qkv_w.forward_one(j, n_seq)

    out_w.forward()
    gathers[1].begin()
    down_w.begin()
    gu_w.forward_own()
    for j in range(n.n_line):
        gathers[0].visit(n.order(j))
    qkv_w.arrive()
    pltpu.make_async_copy(wqkv, wqkv_hbm, save_sem.at[1]).start()
    gu_w.begin(1 + AHEAD)

    low = low_lanes((span, cols_all))
    half_line = length // span // 2
    heads = q_cols // HEAD_DIM
    q_tile = min(length, QUERY_TILE)
    steps = n.last

    def project(m):
        @pl.loop(0, 2)
        def _(i):
            some = pl.ds(pl.multiple_of(i * half_line, half_line), half_line)
            value = nn(full[m, some].reshape(half_line * span, width), wqkv[...].reshape(width, cols_all))
            for k in range(half_line):
                at = pl.ds(pl.multiple_of((i * half_line + k) * span, span), span)
                block = value[k * span : (k + 1) * span]
                turned = (block * cos_ref[at, :] + turn(block, low) * sin_ref[at, :]).astype(BF16)
                q_ref[m, at, :] = turned[:, :q_cols]
                kv_ref[m, at, :] = turned[:, q_cols:]

    def attend(m, h):
        key, val = head_lanes(kv_ref[m], h, q_cols)

        @pl.loop(0, length // q_tile)
        def _(i):
            at = pl.ds(pl.multiple_of(i * q_tile, q_tile), q_tile)
            scores = nt(q_ref[m, at, :], key) + bias_tile(bias, prefix_ref[m], 0, length, q_tile, i)
            weights = jnp.exp(scores - jnp.max(scores, axis=1, keepdims=True))
            inverse = 1.0 / jnp.sum(weights, axis=1, keepdims=True)
            mixed = nn((weights * inverse).astype(BF16), val)
            if h == 0:
                acc[at, :] = mixed
            else:
                acc[at, :] += mixed

    sent = passed = 0
    for m in range(micro):
        project(m)
        fill_bias(bias, prefix_ref[m], 0, length)
        for h in range(heads):
            if m + 1 < micro:
                for j in range(*spread_work(n.n_line, heads, h)):
                    gathers[m + 1].visit(n.order(j))
            if m > 0:
                if h == 0:
                    down_w.pass_on()
                for time in range(*spread_work(steps, heads, h)):
                    scatters[m - 1].step(time)
                    sent += 1
                    gu_w.forward_one(sent, AHEAD)
            attend(m, h)
        mixed_ref[m] = acc[...].astype(BF16)
        if m == 0:
            out_w.arrive()
            pltpu.make_async_copy(wo, wo_hbm, save_sem.at[2]).start()

        @pl.loop(0, width // TILE)
        def _(w):
            cols = pl.ds(pl.multiple_of(w * TILE, TILE), TILE)
            value = nn(mixed_ref[m], wo[:, :, cols].reshape(q_cols, TILE))
            part[m, :, :, cols] = value.astype(BF16).reshape(n_seq, span, TILE)

        scatters[m].begin()
        if m == 0:
            gather_cot.begin()

    pltpu.make_async_copy(full, normed_hbm, save_sem.at[0]).start()
    gather_cot.visit(n.l)
    rest = n_seq - 1 - sent
    for time in range(n.last):
        scatters[-1].step(time)
        for j in range(*spread_work(rest, n.last, time)):
            gu_w.forward_one(sent + 1 + j, AHEAD)
        gather_cot.visit(n.order(time + 1))
        for j in range(*spread_work(n_seq, n.last, time)):
            gu_w.pass_on(j)
    pltpu.make_async_copy(cot, cot_hbm, save_sem.at[3]).start()
    for m in range(micro):
        at = slice(m * span, (m + 1) * span)
        scatters[m].finish(hidden_ref.at[at])
    hidden = hidden_ref[...] + tok_ref[...].astype(F32)
    hidden_ref[...] = hidden
    nmlp_ref[...] = (hidden * lax.rsqrt(jnp.mean(hidden * hidden, axis=1, keepdims=True) + EPSILON)).astype(BF16)
    gu_w.arrive()
    down_w.end()
    pltpu.make_async_copy(full, normed_hbm, save_sem.at[0]).wait()
    pltpu.make_async_copy(wqkv, wqkv_hbm, save_sem.at[1]).wait()
    pltpu.make_async_copy(wo, wo_hbm, save_sem.at[2]).wait()
    pltpu.make_async_copy(cot, cot_hbm, save_sem.at[3]).wait()
    for gather in gathers:
        gather.end()
    gather_cot.end()
    qkv_w.end()
    gu_w.end()
    out_w.end()


def attention_call(prefix, tok, cot, cos, sin, gains, w_query, w_key, w_value, w_gate, w_up, wo_own, wd_own, n_seq, n_dp):
    rows, width = tok.shape
    micro = prefix.shape[0]
    length = cos.shape[0]
    shard = wo_own.shape[0]
    q_cols = width // n_seq
    qkv_cols = q_cols + 2 * HEAD_DIM
    ff_block = wd_own.shape[0]
    gu_cols = 2 * n_dp * ff_block
    every = n_seq * rows
    any_spec = pl.BlockSpec(memory_space=pl.ANY)
    vmem = pl.BlockSpec(memory_space=pltpu.VMEM)
    outs = [
        ((rows, width), F32, vmem),
        ((rows, width), BF16, vmem),
        ((micro, length, q_cols), BF16, vmem),
        ((micro, length, 2 * HEAD_DIM), BF16, vmem),
        ((micro, length, q_cols), BF16, vmem),
        ((micro, n_seq, rows // micro, width), BF16, any_spec),
        ((n_seq, rows, width), BF16, any_spec),
        ((n_dp, n_seq, shard, qkv_cols), BF16, any_spec),
        ((n_dp, shard, width), BF16, any_spec),
        ((n_dp, n_seq, shard, gu_cols), BF16, any_spec),
        ((n_dp, ff_block, width), BF16, any_spec),
    ]
    return pl.pallas_call(
        functools.partial(attention_kernel, n_seq, n_dp),
        out_shape=tuple(jax.ShapeDtypeStruct(s, t) for s, t, _ in outs),
        in_specs=[pl.BlockSpec(memory_space=pltpu.SMEM)] + [vmem] * 10 + [any_spec] * 2,
        out_specs=tuple(spec for _, _, spec in outs),
        scratch_shapes=[
            pltpu.VMEM((micro, n_seq, rows // micro, width), BF16),
            pltpu.VMEM((n_seq, rows, width), BF16),
            pltpu.VMEM((n_dp, n_seq, shard, qkv_cols), BF16),
            pltpu.VMEM((n_dp, shard, width), BF16),
            pltpu.VMEM((length, q_cols), F32),
            pltpu.VMEM((micro, n_seq, rows // micro, width), BF16),
            *Scatter.buffers(n_seq, rows // micro, width, micro),
            pltpu.VMEM((n_seq, shard, qkv_cols), BF16),
            pltpu.VMEM((n_seq, shard, gu_cols), BF16),
            pltpu.VMEM(bias_shape(length), F32),
            pltpu.SemaphoreType.DMA((4,)),
            *Gather.sems(n_seq) * micro,
            *Scatter.sems(n_seq) * micro,
            *Gather.sems(n_seq),
            *Spread.sems(n_seq, n_dp),
            *Spread.sems(n_seq, n_dp),
            *OutRows.sems(n_dp),
            *Copies.sems(n_dp),
        ],
        compiler_params=pltpu.CompilerParams(
            collective_id=2, has_side_effects=True, vmem_limit_bytes=VMEM_LIMIT
        ),
        cost_estimate=pl.CostEstimate(flops=10**10, bytes_accessed=40 << 20, transcendentals=0),
        name="attention",
    )(prefix, tok, cot, cos, sin, gains, w_query, w_key, w_value, w_gate, w_up, wo_own, wd_own)


def mlp_kernel(
    n_seq, n_dp, x_ref, hidden_ref, cot_hbm, wgu_hbm, wd_hbm,
    branch_ref, gh_ref, pout_hbm, dgu_hbm, dwd_ref,
    full, cot, wgu, wd, act, gg, gu, part, sib, rcv, dwd, land, total, stage_gu, stage_rows, load_sem, gu_sem, rows_sem, *sems,
):
    n = Line(n_seq)
    rows, width = x_ref.shape
    ff = wd.shape[0]
    pair = 2 * rows
    loads = [
        pltpu.make_async_copy(src, dst, load_sem.at[i])
        for i, (src, dst) in enumerate(
            [(wgu_hbm, wgu), (cot_hbm, cot), (wd_hbm, wd)]
        )
    ]
    for load in loads:
        load.start()
    full[n.s] = x_ref[...]
    greet_all(n, n_dp, None)
    gather = Gather(n, full, *sems[:3])
    scatter = Scatter(n, part, sib, rcv, *sems[3:7])
    down = RowSum(n_dp, dwd, land, *sems[7:10])
    gather.begin()
    for load in loads:
        load.wait()

    @pl.loop(0, n.n_line)
    def _(j):
        chip = n.order(j)
        gather.visit(chip)
        at = pl.ds(pl.multiple_of(chip * pair, pair), pair)
        two = pl.ds(pl.multiple_of(2 * chip, 2), 2)

        @pl.loop(0, ff // TILE)
        def _(f):
            cols = pl.ds(pl.multiple_of(f * TILE, TILE), TILE)
            x = full[two].reshape(pair, width)
            gate = nn(x, wgu[:, cols])
            up = nn(x, wgu[:, pl.ds(pl.multiple_of(ff + f * TILE, TILE), TILE)])
            grad = nt(cot[two].reshape(pair, width), wd[cols, :])
            sig = jax.nn.sigmoid(gate)
            silu = gate * sig
            act[at, cols] = (silu * up).astype(BF16)
            gg[at, cols] = (grad * up * (sig + silu * (1.0 - sig))).astype(BF16)
            gu[at, cols] = (grad * silu).astype(BF16)

        @pl.loop(0, width // TILE)
        def _(w):
            cols = pl.ds(pl.multiple_of(w * TILE, TILE), TILE)
            value = nt(gg[at, :], wgu[cols, :ff]) + nt(gu[at, :], wgu[cols, ff:])
            part[two, :, cols] = value.astype(BF16).reshape(2, rows, TILE)

    scatter.begin()
    owners = TILE // dwd.shape[1]

    @pl.loop(0, ff // TILE)
    def _(f):
        cols = pl.ds(pl.multiple_of(f * TILE, TILE), TILE)
        at = pl.ds(f * owners, owners)
        for w in range(0, width, 2 * TILE):
            span = cot[:, :, w : w + 2 * TILE].reshape(n_seq * rows, 2 * TILE)
            value = tn(act[:, cols], span).astype(BF16)
            dwd[at, :, w : w + 2 * TILE] = value.reshape(owners, dwd.shape[1], 2 * TILE)

    down.begin()

    def gate_up_grads(first, end):
        @pl.loop(first, end)
        def _(w):
            slot = lax.rem(w, 2)
            cols = pl.ds(pl.multiple_of(w * TILE, TILE), TILE)
            x = full[:, :, cols].reshape(n_seq * rows, TILE)
            copy = pltpu.make_async_copy(stage_gu.at[slot], dgu_hbm.at[cols, :], gu_sem.at[slot])
            pl.when(w >= 2)(lambda: copy.wait())
            stage_gu[slot, :, :ff] = tn(x, gg[...]).astype(BF16)
            stage_gu[slot, :, ff:] = tn(x, gu[...]).astype(BF16)
            copy.start()

    def out_parts(first, end):
        @pl.loop(first, end)
        def _(chip):
            slot = lax.rem(chip, 2)
            at = pl.ds(pl.multiple_of(chip * pair, pair), pair)
            two = pl.ds(pl.multiple_of(2 * chip, 2), 2)
            copies = [
                pltpu.make_async_copy(
                    stage_rows.at[slot, pl.ds(i * rows, rows)], pout_hbm.at[2 * chip + i], rows_sem.at[slot + 2 * i]
                )
                for i in range(2)
            ]

            @pl.when(chip >= 2)
            def _():
                for copy in copies:
                    copy.wait()

            for w in range(0, width, 2 * TILE):
                stage_rows[slot, :pair, w : w + 2 * TILE] = nn(act[at, :], wd[:, w : w + 2 * TILE]).astype(BF16)
            for copy in copies:
                copy.start()

    def drain_out():
        for slot in range(2):
            for i in range(2):
                pltpu.make_async_copy(
                    stage_rows.at[slot, pl.ds(i * rows, rows)], pout_hbm.at[i], rows_sem.at[slot + 2 * i]
                ).wait()

    for time in range(n.last):
        scatter.step(time)
        if time == 0:
            out_parts(0, n.n_line)
        gate_up_grads(*spread_work(width // TILE, n.last, time))
    scatter.finish(total)
    grad_hidden = cot[n.s].astype(F32) + norm_back(hidden_ref[...], total[...])
    gh_ref[...] = grad_hidden
    branch_ref[...] = grad_hidden.astype(BF16)
    drain_out()
    for slot in range(2):
        pltpu.make_async_copy(stage_gu.at[slot], dgu_hbm.at[pl.ds(0, TILE), :], gu_sem.at[slot]).wait()
    down.finish(dwd_ref)
    gather.end()


def mlp_call(x, hidden, cot, wgu, wd, n_seq, n_dp):
    rows, width = x.shape
    ff = wd.shape[0]
    every = n_seq * rows
    any_spec = pl.BlockSpec(memory_space=pl.ANY)
    vmem = pl.BlockSpec(memory_space=pltpu.VMEM)
    return pl.pallas_call(
        functools.partial(mlp_kernel, n_seq, n_dp),
        out_shape=(
            jax.ShapeDtypeStruct((rows, width), BF16),
            jax.ShapeDtypeStruct((rows, width), F32),
            jax.ShapeDtypeStruct((n_seq, rows, width), BF16),
            jax.ShapeDtypeStruct((width, 2 * ff), BF16),
            jax.ShapeDtypeStruct((ff // n_dp, width), F32),
        ),
        in_specs=[vmem] * 2 + [any_spec] * 3,
        out_specs=(vmem, vmem, any_spec, any_spec, vmem),
        scratch_shapes=[
            pltpu.VMEM((n_seq, rows, width), BF16),
            pltpu.VMEM((n_seq, rows, width), BF16),
            pltpu.VMEM((width, 2 * ff), BF16),
            pltpu.VMEM((ff, width), BF16),
            pltpu.VMEM((every, ff), BF16),
            pltpu.VMEM((every, ff), BF16),
            pltpu.VMEM((every, ff), BF16),
            pltpu.VMEM((n_seq, rows, width), BF16),
            *Scatter.buffers(n_seq, rows, width),
            pltpu.VMEM((n_dp, ff // n_dp, width), BF16),
            pltpu.VMEM((n_dp, ff // n_dp, width), BF16),
            pltpu.VMEM((rows, width), F32),
            pltpu.VMEM((2, TILE, 2 * ff), BF16),
            pltpu.VMEM((2, TILE, width), BF16),
            pltpu.SemaphoreType.DMA((3,)),
            pltpu.SemaphoreType.DMA((2,)),
            pltpu.SemaphoreType.DMA((4,)),
            *Gather.sems(n_seq),
            *Scatter.sems(n_seq),
            *RowSum.sems(n_dp),
        ],
        compiler_params=pltpu.CompilerParams(
            collective_id=1, has_side_effects=True, vmem_limit_bytes=VMEM_LIMIT
        ),
        cost_estimate=pl.CostEstimate(flops=18 * every * width * ff, bytes_accessed=40 << 20, transcendentals=0),
        name="mlp",
    )(x, hidden, cot, wgu, wd)


def backward_kernel(
    n_seq, n_dp, prefix_ref, branch_ref, tok_ref, q_ref, kv_ref, mixed_ref, cos_ref, sin_ref, gains_ref,
    w_query_ref, w_key_ref, w_value_ref, gh_hbm, hidden_hbm, pout_hbm, normed_hbm, wqkv_hbm, wo_hbm, dgu_hbm,
    out_ref, in_ref, dgain_ref, dq_ref, dk_ref, dv_ref, dwo_out, dgate_ref, dup_ref,
    full, tiles, wqkv, wo, gm, acc_q, acc_k, acc_v, bias, gqkv, part, sib, rcv, sib_o, rcv_o,
    land_gu, final_gu, dqkv, land_qkv, final_qkv, dwo, land_o, final_o, total, load_sem, tile_sem, *sems,
):
    n = Line(n_seq)
    rows, width = branch_ref.shape
    micro, length, q_cols = q_ref.shape
    span = rows // micro
    pair = 2 * rows
    loads = [
        pltpu.make_async_copy(src, dst, load_sem.at[i])
        for i, (src, dst) in enumerate(
            [(pout_hbm, part), (wo_hbm, wo), (wqkv_hbm, wqkv), (hidden_hbm, total), (gh_hbm, in_ref)]
        )
    ]
    for load in loads:
        load.start()
    for m in range(micro):
        full[m, n.s] = branch_ref[m * span : (m + 1) * span, :]
    sems = list(sems)
    take = lambda count: [sems.pop(0) for _ in range(count)]
    gathers = [Gather(n, full, *take(3), m=m) for m in range(micro)]
    scatter = Scatter(n, part, sib, rcv, *take(4))
    scatter_out = Scatter(n, part, sib_o, rcv_o, *take(4))
    gu_sum = Collect(n, n_dp, dgu_hbm, land_gu, final_gu, *take(5))
    qkv_sum = Collect(n, n_dp, dqkv, land_qkv, final_qkv, *take(5))
    out_sum = OutSum(n, n_dp, dwo, land_o, final_o, *take(5))
    greet_all(n, n_dp, out_sum)
    gathers[0].begin()
    gu_sum.begin(3)
    loads[0].wait()
    loads[1].wait()
    late = n_seq * 5 // 8
    scatter_out.begin()
    gathers[1].begin()
    for j in range(n.n_line):
        gathers[0].visit(n.order(j))
    loads[2].wait()

    heads = q_cols // HEAD_DIM
    scale = 1.0 / math.sqrt(HEAD_DIM)
    q_tile = min(length, QUERY_TILE)
    low = low_lanes((length, q_cols + 2 * HEAD_DIM))
    here = lax.div(lax.broadcasted_iota(jnp.int32, (length, q_cols), 1), HEAD_DIM)

    def attend_back(m, h):
        key, val = head_lanes(kv_ref[m], h, q_cols)

        @pl.loop(0, length // q_tile)
        def _(i):
            at = pl.ds(pl.multiple_of(i * q_tile, q_tile), q_tile)
            query, grad = q_ref[m, at, :], gm[m, at, :]
            scores = nt(key, query) + bias_tile(bias, prefix_ref[m], 1, length, q_tile, i)
            weights = jnp.exp(scores - jnp.max(scores, axis=0, keepdims=True))
            probs = weights * (1.0 / jnp.sum(weights, axis=0, keepdims=True))
            grad_probs = nt(val, grad)
            delta = jnp.sum(probs * grad_probs, axis=0, keepdims=True)
            grad_scores = (probs * (grad_probs - delta)).astype(BF16)
            acc_q[at, :] += tn(grad_scores, key)
            acc_k[...] += jnp.where(here == h, nn(grad_scores, query), 0.0)
            acc_v[...] += jnp.where(here == h, nn(probs.astype(BF16), grad), 0.0)

    shard = dwo.shape[1]

    def out_grads():

        @pl.loop(0, width // TILE)
        def _(w):
            cols = pl.ds(pl.multiple_of(w * TILE, TILE), TILE)
            d_out = jnp.zeros((q_cols, TILE), F32)
            for m in range(micro):
                d_out = d_out + tn(mixed_ref[m], full[m, :, :, cols].reshape(length, TILE))
            dwo[:, :, cols] = d_out.astype(BF16).reshape(n_dp, shard, TILE)

        out_sum.begin()

    for m in range(micro):
        gm[m] = nt(full[m].reshape(length, width), wo[...].reshape(q_cols, width)).astype(BF16)
        fill_bias(bias, prefix_ref[m], 1, length)
        for ref in (acc_q, acc_k, acc_v):
            ref[...] = jnp.zeros_like(ref)
        for h in range(heads):
            if m + 1 < micro:
                for j in range(*spread_work(n.n_line, heads, h)):
                    gathers[m + 1].visit(n.order(j))
            if m == 0:
                for time in range(*spread_work(n.last, heads, h)):
                    scatter_out.step(time)
            if m == 1 and h == 0:
                out_grads()
            for j in range(*spread_work(late, micro * heads, m * heads + h)):
                gu_sum.reduce(j, j + 1)
            attend_back(m, h)

        def fold(ref):
            total = ref[:, : 2 * HEAD_DIM]
            for w in range(2 * HEAD_DIM, q_cols, 2 * HEAD_DIM):
                total = total + ref[:, w : w + 2 * HEAD_DIM]
            return total + pltpu.roll(total, HEAD_DIM, 1)

        first = lax.broadcasted_iota(jnp.int32, (length, 2 * HEAD_DIM), 1) < HEAD_DIM
        grads = jnp.concatenate([acc_q[...], jnp.where(first, fold(acc_k) * scale, fold(acc_v))], axis=1)
        gqkv[m] = (grads * cos_ref[...] - turn(grads, low) * sin_ref[...]).astype(BF16)

    loads[3].wait()
    scatter_out.finish(total, True)
    out_ref[...] = total[...].astype(BF16)
    for m in range(micro):

        @pl.loop(0, width // TILE)
        def _(w):
            at = pl.ds(pl.multiple_of(w * TILE, TILE), TILE)
            value = nt(gqkv[m], wqkv[at, :])
            part[:, m * span : (m + 1) * span, at] = value.astype(BF16).reshape(n_seq, span, TILE)

    scatter.begin()

    half = n_seq // 2
    depth = half * shard

    def fetch(w):
        cols = pl.ds(pl.multiple_of(w * depth, depth), depth)
        slot = lax.rem(w, 2)
        return pltpu.make_async_copy(normed_hbm.at[:, :, :, cols], tiles.at[slot], tile_sem.at[slot])

    fetch(jnp.int32(0)).start()

    @pl.loop(0, n_dp * 2)
    def _(w):
        pl.when(w + 1 < n_dp * 2)(lambda: fetch(w + 1).start())
        fetch(w).wait()
        slot = lax.rem(w, 2)
        d_qkv = jnp.zeros((depth, q_cols + 2 * HEAD_DIM), F32)
        for m in range(micro):
            d_qkv = d_qkv + tn(tiles[slot, m].reshape(length, depth), gqkv[m])
        at = pl.ds(pl.multiple_of(lax.rem(w, 2) * half, half), half)
        dqkv[lax.div(w, 2), at] = d_qkv.astype(BF16).reshape(half, shard, q_cols + 2 * HEAD_DIM)

    qkv_sum.begin(n_seq)
    out_sum.reduce()
    for time in range(n.last):
        scatter.step(time)
        first, end = spread_work(n_seq - late, n.last, time)
        gu_sum.reduce(late + first, late + end)
    qkv_sum.reduce(0, n_seq)
    scatter.finish(total)
    loads[4].wait()
    in_ref[...] += norm_back(tok_ref[...].astype(F32), total[...])
    gu_sum.end()
    ff_block = dgate_ref.shape[1] // (n_dp * n_seq)
    gain_attn = gains_ref[:, :1]
    for i, ref in enumerate((dgate_ref, dup_ref)):
        for owner in range(n_dp):
            for t in range(n_seq):
                cols = slice((owner * n_seq + t) * ff_block, (owner * n_seq + t + 1) * ff_block)
                first = (i * n_dp + owner) * ff_block
                ref[:, cols] = final_gu[t, :, first : first + ff_block]
    qkv_sum.end()
    repeat = n_seq // KV_HEADS
    dots = jnp.zeros((shard, 1), F32)
    for t in range(n_seq):
        cols = slice(t * q_cols, (t + 1) * q_cols)
        value = final_qkv[t, :, :q_cols].astype(F32)
        dots = dots + jnp.sum(value * w_query_ref[:, cols].astype(F32), axis=1, keepdims=True)
        dq_ref[:, cols] = value * gain_attn
    for g in range(KV_HEADS):
        cols = slice(g * HEAD_DIM, (g + 1) * HEAD_DIM)
        for i, (ref, w_ref) in enumerate(((dk_ref, w_key_ref), (dv_ref, w_value_ref))):
            lanes = slice(q_cols + i * HEAD_DIM, q_cols + (i + 1) * HEAD_DIM)
            value = final_qkv[g * repeat, :, lanes].astype(F32)
            for t in range(g * repeat + 1, (g + 1) * repeat):
                value = value + final_qkv[t, :, lanes].astype(F32)
            dots = dots + jnp.sum(value * w_ref[:, cols].astype(F32), axis=1, keepdims=True)
            ref[:, cols] = value * gain_attn
    dgain_ref[...] = dots * jnp.ones((shard, 2 * HEAD_DIM), F32)
    out_sum.end()
    dwo_out[...] = final_o[...].astype(F32)
    for gather in gathers:
        gather.end()


def backward_call(
    prefix, branch, tok, q, kv, mixed, cos, sin, gains, w_query, w_key, w_value,
    gh, hidden, pout, normed, wqkv, wo, dgu,
):
    rows, width = branch.shape
    n_dp, n_seq, shard, gu_cols = dgu.shape
    ff = gu_cols // 2 * n_seq
    micro, length, q_cols = q.shape
    qkv_cols = q_cols + 2 * HEAD_DIM
    any_spec = pl.BlockSpec(memory_space=pl.ANY)
    vmem = pl.BlockSpec(memory_space=pltpu.VMEM)
    line_rows = pltpu.VMEM((n_seq, rows, width), BF16)
    return pl.pallas_call(
        functools.partial(backward_kernel, n_seq, n_dp),
        out_shape=(
            jax.ShapeDtypeStruct((rows, width), BF16),
            jax.ShapeDtypeStruct((rows, width), F32),
            jax.ShapeDtypeStruct((shard, 2 * HEAD_DIM), F32),
            *(jax.ShapeDtypeStruct(w.shape, F32) for w in (w_query, w_key, w_value)),
            jax.ShapeDtypeStruct((shard, width), F32),
            jax.ShapeDtypeStruct((shard, ff), BF16),
            jax.ShapeDtypeStruct((shard, ff), BF16),
        ),
        in_specs=[pl.BlockSpec(memory_space=pltpu.SMEM)] + [vmem] * 11 + [any_spec] * 7,
        out_specs=(vmem,) * 9,
        scratch_shapes=[
            pltpu.VMEM((micro, n_seq, rows // micro, width), BF16),
            pltpu.VMEM((2, micro, n_seq, rows // micro, n_seq // 2 * shard), BF16),
            pltpu.VMEM((width, qkv_cols), BF16),
            pltpu.VMEM(wo.shape, BF16),
            pltpu.VMEM((micro, length, q_cols), BF16),
            pltpu.VMEM((length, q_cols), F32),
            pltpu.VMEM((length, q_cols), F32),
            pltpu.VMEM((length, q_cols), F32),
            pltpu.VMEM(bias_shape(length), F32),
            pltpu.VMEM((micro, length, qkv_cols), BF16),
            line_rows,
            *Scatter.buffers(n_seq, rows, width),
            *Scatter.buffers(n_seq, rows, width),
            pltpu.VMEM((n_dp, n_seq, shard, gu_cols), BF16),
            pltpu.VMEM((n_seq, shard, gu_cols), BF16),
            pltpu.VMEM((n_dp, n_seq, shard, qkv_cols), BF16),
            pltpu.VMEM((n_dp, n_seq, shard, qkv_cols), BF16),
            pltpu.VMEM((n_seq, shard, qkv_cols), BF16),
            pltpu.VMEM((n_dp, shard, width), BF16),
            pltpu.VMEM((n_dp, shard, width), BF16),
            pltpu.VMEM((shard, width), BF16),
            pltpu.VMEM((rows, width), F32),
            pltpu.SemaphoreType.DMA((5,)),
            pltpu.SemaphoreType.DMA((2,)),
            *Gather.sems(n_seq) * micro,
            *Scatter.sems(n_seq),
            *Scatter.sems(n_seq),
            *Collect.sems(n_seq, n_dp),
            *Collect.sems(n_seq, n_dp),
            *OutSum.sems(n_dp),
        ],
        compiler_params=pltpu.CompilerParams(
            collective_id=3, has_side_effects=True, vmem_limit_bytes=VMEM_LIMIT
        ),
        cost_estimate=pl.CostEstimate(flops=10**10, bytes_accessed=40 << 20, transcendentals=0),
        name="backward",
    )(
        prefix, branch, tok, q, kv, mixed, cos, sin, gains, w_query, w_key, w_value,
        gh, hidden, pout, normed, wqkv, wo, dgu,
    )


def body(
    tokens, cotangent, prefix_len, attn_gain, w_query, w_key, w_value, w_out, mlp_gain, w_gate, w_up, w_down
):
    n_dp = lax.axis_size("dp")
    n_seq = lax.axis_size("seq")
    micro, span, width = tokens.shape
    shard = w_query.shape[0]
    rows = micro * span
    cos, sin = rope_tables(span * n_seq, HEADS // n_seq * HEAD_DIM)
    gains = jnp.concatenate(
        [jnp.broadcast_to(g.astype(F32)[:, None], (shard, 2 * HEAD_DIM)) for g in (attn_gain, mlp_gain)], axis=1
    )
    tok = tokens.reshape(rows, width)
    cot = cotangent.reshape(rows, width)
    hidden, normed_mlp, q, kv, mixed, normed, cot_all, wqkv, wo, wgu, wd = attention_call(
        prefix_len, tok, cot, cos, sin, gains, w_query, w_key, w_value, w_gate, w_up, w_out, w_down, n_seq, n_dp
    )
    branch, grad_hidden, out_part, dgu, w_down_grad = mlp_call(
        normed_mlp, hidden, cot_all, wgu.reshape(width, -1), wd.reshape(-1, width), n_seq, n_dp
    )
    block_out, input_grad, attn_gain_grad, *w_grads, w_out_grad, d_gate, d_up = backward_call(
        prefix_len, branch, tok, q, kv, mixed, cos, sin, gains, w_query, w_key, w_value,
        grad_hidden, hidden, out_part, normed, wqkv.reshape(width, -1), wo.reshape(-1, width), dgu.reshape(n_dp, n_seq, shard, -1),
    )
    mlp_gain_grad = jnp.sum(d_gate.astype(F32) * w_gate.astype(F32), axis=1)
    mlp_gain_grad = mlp_gain_grad + jnp.sum(d_up.astype(F32) * w_up.astype(F32), axis=1)
    gain_column = mlp_gain.astype(F32)[:, None]
    return (
        block_out.reshape(micro, span, width),
        input_grad.reshape(micro, span, width),
        attn_gain_grad[:, 0],
        *w_grads,
        w_out_grad,
        mlp_gain_grad,
        d_gate.astype(F32) * gain_column,
        d_up.astype(F32) * gain_column,
        w_down_grad,
    )


def solution(mesh):
    rows = P("dp", "seq", None)
    vec = P(("dp", "seq"))
    mat = P(("dp", "seq"), None)
    in_specs = (rows, rows, P("dp"), vec, mat, mat, mat, mat, vec, mat, mat, mat)
    out_specs = (rows, rows, vec, mat, mat, mat, mat, vec, mat, mat, mat)
    return jax.shard_map(body, mesh=mesh, in_specs=in_specs, out_specs=out_specs, check_vma=False)
```

```python
import functools
import math

import jax
import jax.numpy as jnp
import numpy as np
from jax import lax
from jax.experimental import pallas as pl
from jax.experimental.pallas import tpu as pltpu
from jax.sharding import PartitionSpec as P

HEADS = 32
KV_HEADS = 8
HEAD_DIM = 64
EPSILON = 1e-05
THETA = 500000.0
NEGATIVE = -1e30
BF16 = jnp.bfloat16
F32 = jnp.float32
MESH = pl.DeviceIdType.MESH
TILE = 256
QUERY_TILE = 256
AHEAD = 4
VMEM_LIMIT = 61 << 20


def rope_tables(length, q_cols):
    half = HEAD_DIM // 2
    f32 = np.float32
    index_half = np.arange(half, dtype=f32)
    inverse = np.power(f32(THETA), f32(-2.0) * index_half / f32(HEAD_DIM)).astype(f32)
    wavelength = (f32(2.0 * math.pi) / inverse).astype(f32)
    smooth = ((f32(8192.0) / wavelength - f32(1.0)) / f32(3.0)).astype(f32)
    blended = ((f32(1.0) - smooth) * inverse / f32(32.0) + smooth * inverse).astype(f32)
    inverse = np.where(
        wavelength < 2048.0, inverse, np.where(wavelength > 8192.0, inverse / f32(32.0), blended)
    ).astype(f32)
    angles = (np.arange(length, dtype=f32)[:, None] * inverse[None, :]).astype(f32)
    cos, sin = np.cos(angles).astype(f32), np.sin(angles).astype(f32)
    count = q_cols // HEAD_DIM + 1
    ones, zeros = np.ones((length, HEAD_DIM), f32), np.zeros((length, HEAD_DIM), f32)
    cos = np.concatenate([cos, cos] * count + [ones], axis=1)
    sin = np.concatenate([-sin, sin] * count + [zeros], axis=1)
    return jnp.asarray(cos), jnp.asarray(sin)


def nn(a, b):
    return jnp.dot(a, b, preferred_element_type=F32)


def tn(a, b):
    return lax.dot_general(a, b, (((0,), (0,)), ((), ())), preferred_element_type=F32)


def nt(a, b):
    return lax.dot_general(a, b, (((1,), (1,)), ((), ())), preferred_element_type=F32)


class Line:
    def __init__(self, n_seq):
        self.n_line = n_seq // 2
        self.last = self.n_line - 1
        self.s = lax.axis_index("seq")
        self.c = lax.rem(self.s, 2)
        self.l = lax.div(self.s, 2)
        self.sibling = self.s + 1 - 2 * self.c
        self.right = jnp.minimum(self.s + 2, n_seq - 2 + self.c)
        self.left = jnp.maximum(self.s - 2, self.c)
        self.has_right = self.l < self.last
        self.has_left = self.l > 0

    def greet(self, n_dp):
        barrier = pltpu.get_barrier_semaphore()
        d = lax.axis_index("dp")
        for k in range(1, n_dp):
            pl.semaphore_signal(barrier, 1, device_id={"dp": lax.rem(d + k, n_dp)}, device_id_type=MESH)
        pl.semaphore_signal(barrier, 1, device_id={"seq": self.sibling}, device_id_type=MESH)

        @pl.when(self.has_right)
        def _():
            pl.semaphore_signal(barrier, 1, device_id={"seq": self.right}, device_id_type=MESH)

        @pl.when(self.has_left)
        def _():
            pl.semaphore_signal(barrier, 1, device_id={"seq": self.left}, device_id_type=MESH)

        pl.semaphore_wait(barrier, n_dp - 1 + jnp.where(self.has_right & self.has_left, 3, 2))

    def order(self, j):
        near = jnp.minimum(self.l, self.last - self.l)
        half = lax.div(j + 1, 2)
        both = jnp.where(lax.rem(j, 2) == 1, self.l - half, self.l + half)
        far = jnp.where(self.l <= self.last - self.l, j, self.last - j)
        return jnp.where(j <= 2 * near, both, far)


def remote(src, dst, send, recv, seq):
    return pltpu.make_async_remote_copy(
        src_ref=src, dst_ref=dst, send_sem=send, recv_sem=recv, device_id={"seq": seq}, device_id_type=MESH
    )


class Gather:
    def __init__(self, line, full, send_z, send_c, recv, m=None):
        self.m = m
        self.line, self.full, self.send_z, self.send_c, self.recv = line, full, send_z, send_c, recv

    @staticmethod
    def sems(n_seq):
        n_line = n_seq // 2
        return [
            pltpu.SemaphoreType.DMA((n_line + 1,)),
            pltpu.SemaphoreType.DMA((n_line,)),
            pltpu.SemaphoreType.DMA((n_seq,)),
        ]

    def copy(self, index, send, seq):
        chunk = self.full.at[index] if self.m is None else self.full.at[self.m, index]
        return remote(chunk, chunk, send, self.recv.at[index], seq)

    def begin(self):
        n = self.line
        pl.when(n.has_right)(lambda: self.copy(n.s, self.send_z.at[n.l], n.right).start())
        pl.when(n.has_left)(lambda: self.copy(n.s, self.send_z.at[n.n_line], n.left).start())
        self.copy(n.s, self.send_c.at[n.l], n.sibling).start()

    def visit(self, chip):
        n = self.line
        mine = 2 * chip + n.c

        @pl.when(chip != n.l)
        def _():
            self.copy(mine, self.send_c.at[chip], n.sibling).wait_recv()
            pl.when((chip < n.l) & n.has_right)(
                lambda: self.copy(mine, self.send_z.at[chip], n.right).start()
            )
            pl.when((chip > n.l) & n.has_left)(
                lambda: self.copy(mine, self.send_z.at[chip], n.left).start()
            )
            self.copy(mine, self.send_c.at[chip], n.sibling).start()

        self.copy(2 * chip + 1 - n.c, self.send_c.at[chip], n.sibling).wait_recv()

    def end(self):
        n = self.line

        @pl.loop(0, n.n_line)
        def _(chip):
            mine = 2 * chip + n.c
            self.copy(mine, self.send_c.at[chip], n.sibling).wait_send()
            pl.when((chip <= n.l) & n.has_right)(
                lambda: self.copy(mine, self.send_z.at[chip], n.right).wait_send()
            )
            pl.when((chip > n.l) & n.has_left)(
                lambda: self.copy(mine, self.send_z.at[chip], n.left).wait_send()
            )

        pl.when(n.has_left)(lambda: self.copy(n.s, self.send_z.at[n.n_line], n.left).wait_send())


class Scatter:
    def __init__(self, line, part, sib, rcv, send_z, send_c, recv_z, recv_c, m=None):
        self.line, self.m = line, m
        self.part, self.sib, self.rcv = part, sib, rcv
        self.send_z, self.send_c, self.recv_z, self.recv_c = send_z, send_c, recv_z, recv_c

    @staticmethod
    def sems(n_seq):
        n_line = n_seq // 2
        return [
            pltpu.SemaphoreType.DMA((n_line,)),
            pltpu.SemaphoreType.DMA((n_line,)),
            pltpu.SemaphoreType.DMA((n_line + 1,)),
            pltpu.SemaphoreType.DMA((n_line,)),
        ]

    @staticmethod
    def buffers(n_seq, rows, width, *lead):
        n_line = n_seq // 2
        return [
            pltpu.VMEM((*lead, n_line, rows, width), BF16),
            pltpu.VMEM((*lead, n_line + 1, rows, width), BF16),
        ]

    def at(self, index):
        return index if self.m is None else (self.m, index)

    def across(self, chip):
        n = self.line
        return remote(
            self.part.at[self.at(2 * chip + 1 - n.c)],
            self.sib.at[self.at(chip)],
            self.send_c.at[chip],
            self.recv_c.at[chip],
            n.sibling,
        )

    def hop(self, chip, slot, seq):
        n = self.line
        return remote(
            self.part.at[self.at(2 * chip + n.c)],
            self.rcv.at[self.at(slot)],
            self.send_z.at[chip],
            self.recv_z.at[slot],
            seq,
        )

    def begin(self):
        n = self.line

        @pl.loop(0, n.n_line)
        def _(j):
            half = lax.div(j, 2)
            self.across(jnp.where(lax.rem(j, 2) == 0, n.last - half, half)).start()

    def add(self, chip, source):
        mine = self.at(2 * chip + self.line.c)
        self.part[mine] = (self.part[mine].astype(F32) + source.astype(F32)).astype(BF16)

    def step(self, time):
        n = self.line

        @pl.when(n.l <= time)
        def _():
            chip = n.last - time + n.l
            self.across(chip).wait_recv()
            self.add(chip, self.sib[self.at(chip)])

            @pl.when(n.has_left)
            def _():
                self.hop(chip, chip, n.right).wait_recv()
                self.add(chip, self.rcv[self.at(chip)])

            self.hop(chip, chip, n.right).start()

        @pl.when(n.last - n.l <= time)
        def _():
            chip = time - n.last + n.l
            self.across(chip).wait_recv()
            self.add(chip, self.sib[self.at(chip)])

            @pl.when(n.has_right)
            def _():
                self.hop(chip, chip, n.left).wait_recv()
                self.add(chip, self.rcv[self.at(chip)])

            self.hop(chip, jnp.where(chip == n.l - 1, n.n_line, chip), n.left).start()

    def finish(self, out, add=False):
        n = self.line
        mine = 2 * n.l + n.c
        self.across(n.l).wait_recv()
        value = self.part[self.at(mine)].astype(F32) + self.sib[self.at(n.l)].astype(F32)
        out[...] = out[...] + value if add else value

        @pl.when(n.has_left)
        def _():
            self.hop(n.l, n.l, n.right).wait_recv()
            out[...] += self.rcv[self.at(n.l)].astype(F32)

        @pl.when(n.has_right)
        def _():
            self.hop(n.l, n.n_line, n.left).wait_recv()
            out[...] += self.rcv[self.at(n.n_line)].astype(F32)

        @pl.loop(0, n.n_line)
        def _(chip):
            self.across(chip).wait_send()
            pl.when(chip > n.l)(lambda: self.hop(chip, chip, n.right).wait_send())
            pl.when(chip < n.l)(lambda: self.hop(chip, chip, n.left).wait_send())


def norm_back(u, ge):
    r = lax.rsqrt(jnp.mean(u * u, axis=1, keepdims=True) + EPSILON)
    return r * ge - u * (r * r * r * jnp.mean(u * ge, axis=1, keepdims=True))


def spread_work(units, slots, index):
    return (units * index // slots, units * (index + 1) // slots)


class Square:
    def __init__(self):
        self.d = lax.axis_index("dp")
        self.first = self.d + 1 - 2 * lax.rem(self.d, 2)
        self.second = lax.rem(self.d + 2, 4)
        self.across = 3 - self.d


class Spread:
    def __init__(self, line, n_dp, blocks, dst, own_sem, send_z, send_xy, recv):
        self.line, self.n_dp, self.blocks, self.dst = line, n_dp, blocks, dst
        self.own_sem, self.send_z, self.send_xy, self.recv = own_sem, send_z, send_xy, recv
        self.n_seq = 2 * line.n_line
        self.d = lax.axis_index("dp")

    @staticmethod
    def sems(n_seq, n_dp):
        return [
            pltpu.SemaphoreType.DMA((1,)),
            pltpu.SemaphoreType.DMA((n_seq,)),
            pltpu.SemaphoreType.DMA((n_seq, n_dp)),
            pltpu.SemaphoreType.DMA((n_dp, n_seq)),
        ]

    def source(self, j):
        return lax.rem(self.line.s - j + self.n_seq, self.n_seq)

    def hop(self, t):
        n = self.line
        return pltpu.make_async_remote_copy(
            src_ref=self.blocks.at[t],
            dst_ref=self.dst.at[self.d, n.s],
            send_sem=self.send_z.at[t],
            recv_sem=self.recv.at[self.d, n.s],
            device_id={"seq": t},
            device_id_type=MESH,
        )

    def own(self):
        n = self.line
        return pltpu.make_async_copy(self.blocks.at[n.s], self.dst.at[self.d, n.s], self.own_sem.at[0])

    def to_dp(self, src, dst, send, recv, peer):
        return pltpu.make_async_remote_copy(
            src_ref=src, dst_ref=dst, send_sem=send, recv_sem=recv, device_id={"dp": peer}, device_id_type=MESH
        )

    def over(self, source, own=False):
        src = self.blocks.at[self.line.s] if own else self.dst.at[self.d, source]
        peers = [lax.rem(self.d + k, self.n_dp) for k in range(1, self.n_dp)]
        return [
            self.to_dp(src, self.dst.at[self.d, source], self.send_xy.at[source, k], self.recv.at[self.d, source], peer)
            for k, peer in enumerate(peers)
        ]

    def landed(self, d, source):
        block = self.dst.at[d, source]
        return self.to_dp(block, block, self.send_z.at[0], self.recv.at[d, source], d)

    def begin(self, end):
        n = self.line

        @pl.loop(1, end)
        def _(j):
            self.hop(lax.rem(n.s + j, self.n_seq)).start()

        self.own().start()

    def forward_one(self, j, ahead):
        n = self.line

        @pl.when(j < self.n_seq)
        def _():
            pl.when(j + ahead < self.n_seq)(lambda: self.hop(lax.rem(n.s + j + ahead, self.n_seq)).start())
            source = self.source(j)
            self.landed(self.d, source).wait_recv()
            for copy in self.over(source):
                copy.start()

    def forward_own(self):
        for copy in self.over(self.line.s, True):
            copy.start()

    def arrive(self):
        @pl.loop(0, self.n_seq)
        def _(source):
            for k in range(1, self.n_dp):
                self.landed(lax.rem(self.d + k, self.n_dp), source).wait_recv()

        self.own().wait()

    def end(self):
        n = self.line

        @pl.loop(0, self.n_seq)
        def _(j):
            pl.when(j != n.s)(lambda: self.hop(j).wait_send())
            for copy in self.over(j):
                copy.wait_send()


class Copies:
    def __init__(self, n_dp, own, dst, own_sem, send, recv):
        self.n_dp, self.own_ref, self.dst = n_dp, own, dst
        self.own_sem, self.send, self.recv = own_sem, send, recv
        self.d = lax.axis_index("dp")
        self.relay = n_dp == 4
        self.square = Square()
        self.half = own.shape[0] // 2

    @staticmethod
    def sems(n_dp):
        return [
            pltpu.SemaphoreType.DMA((1,)),
            pltpu.SemaphoreType.DMA((n_dp,)),
            pltpu.SemaphoreType.DMA((n_dp + 1,)),
        ]

    def copy(self, src, slot, part, send, recv, peer):
        return pltpu.make_async_remote_copy(
            src_ref=src,
            dst_ref=self.dst.at[slot] if part is None else self.dst.at[slot, part],
            send_sem=self.send.at[send],
            recv_sem=self.recv.at[recv],
            device_id={"dp": peer},
            device_id_type=MESH,
        )

    def direct(self):
        peers = [lax.rem(self.d + k, self.n_dp) for k in range(1, self.n_dp)]
        if self.relay:
            peers = [self.square.first, self.square.second]
        return [self.copy(self.own_ref, self.d, None, k + 1, self.d, peer) for k, peer in enumerate(peers)]

    def landed(self, slot):
        return self.copy(self.dst.at[slot], slot, None, 0, slot, slot)

    def halves(self):
        q = self.square
        low, high = pl.ds(0, self.half), pl.ds(self.half, self.half)
        return (
            self.copy(self.dst.at[q.first, low], q.first, low, 3, q.first, q.second),
            self.copy(self.dst.at[q.second, high], q.second, high, 0, self.n_dp, q.first),
        )

    def own(self):
        return pltpu.make_async_copy(self.own_ref, self.dst.at[self.d], self.own_sem.at[0])

    def begin(self):
        for copy in self.direct():
            copy.start()
        self.own().start()

    def pass_on(self):
        if not self.relay:
            return
        one, two = self.halves()
        self.landed(self.square.first).wait_recv()
        one.start()
        self.landed(self.square.second).wait_recv()
        two.start()

    def end(self):
        for copy in self.direct():
            copy.wait_send()
        if self.relay:
            low, high = pl.ds(0, self.half), pl.ds(self.half, self.half)
            across = self.square.across
            self.copy(self.dst.at[across, low], across, low, 0, across, across).wait_recv()
            self.copy(self.dst.at[across, high], across, high, 0, self.n_dp, across).wait_recv()
            for copy in self.halves():
                copy.wait_send()
        else:
            for k in range(1, self.n_dp):
                self.landed(lax.rem(self.d + k, self.n_dp)).wait_recv()
        self.own().wait()


class Relay:
    def __init__(self, line, n_dp):
        n_seq = 2 * line.n_line
        self.n_dp = n_dp
        self.d = lax.axis_index("dp")
        block = self.d * n_seq + line.s
        self.slot, self.target = lax.rem(block, n_dp), lax.div(block, n_dp)
        block = line.s * n_dp + self.d
        self.owner_d, self.owner_s = lax.div(block, n_seq), lax.rem(block, n_seq)
        self.stays = (self.slot == self.d) & (self.target == line.s)
        self.moves = jnp.logical_not(self.stays)

    def to_relay(self, src, dst, send, recv):
        return pltpu.make_async_remote_copy(
            src_ref=src, dst_ref=dst, send_sem=send, recv_sem=recv,
            device_id=(self.slot, self.target), device_id_type=MESH,
        )

    def to_owner(self, src, dst, send, recv):
        return pltpu.make_async_remote_copy(
            src_ref=src, dst_ref=dst, send_sem=send, recv_sem=recv,
            device_id=(self.owner_d, self.owner_s), device_id_type=MESH,
        )

    def over(self, k, src, dst, send, recv):
        return pltpu.make_async_remote_copy(
            src_ref=src, dst_ref=dst, send_sem=send, recv_sem=recv,
            device_id={"dp": lax.rem(self.d + k, self.n_dp)}, device_id_type=MESH,
        )


class OutRows(Relay):
    def __init__(self, line, n_dp, own, dst, own_sem, send_z, send_xy, recv):
        super().__init__(line, n_dp)
        self.own_ref, self.dst = own, dst
        self.own_sem, self.send_z, self.send_xy, self.recv = own_sem, send_z, send_xy, recv

    @staticmethod
    def sems(n_dp):
        return [
            pltpu.SemaphoreType.DMA((1,)),
            pltpu.SemaphoreType.DMA((1,)),
            pltpu.SemaphoreType.DMA((n_dp,)),
            pltpu.SemaphoreType.DMA((n_dp,)),
        ]

    def hop(self):
        return self.to_relay(self.own_ref, self.dst.at[self.slot], self.send_z.at[0], self.recv.at[self.slot])

    def own(self):
        return pltpu.make_async_copy(self.own_ref, self.dst.at[self.slot], self.own_sem.at[0])

    def copy(self, k):
        return self.over(k, self.dst.at[self.d], self.dst.at[self.d], self.send_xy.at[k], self.recv.at[self.d])

    def landed(self, slot):
        return self.over(1, self.dst.at[slot], self.dst.at[slot], self.send_xy.at[1], self.recv.at[slot])

    def begin(self):
        pl.when(self.stays)(lambda: self.own().start())
        pl.when(self.moves)(lambda: self.hop().start())

    def forward(self):
        pl.when(self.stays)(lambda: self.own().wait())
        pl.when(self.moves)(lambda: self.landed(self.d).wait_recv())
        for k in range(1, self.n_dp):
            self.copy(k).start()

    def arrive(self):
        for k in range(1, self.n_dp):
            self.landed(lax.rem(self.d + k, self.n_dp)).wait_recv()

    def end(self):
        pl.when(self.moves)(lambda: self.hop().wait_send())
        for k in range(1, self.n_dp):
            self.copy(k).wait_send()


class OutSum(Relay):
    def __init__(self, line, n_dp, src, land, final, own_sem, send_xy, recv_xy, send_z, recv_z):
        super().__init__(line, n_dp)
        self.src, self.land, self.final = src, land, final
        self.own_sem, self.send_xy, self.recv_xy, self.send_z, self.recv_z = own_sem, send_xy, recv_xy, send_z, recv_z

    @staticmethod
    def sems(n_dp):
        return [
            pltpu.SemaphoreType.DMA((1,)),
            pltpu.SemaphoreType.DMA((n_dp,)),
            pltpu.SemaphoreType.DMA((n_dp,)),
            pltpu.SemaphoreType.DMA((1,)),
            pltpu.SemaphoreType.DMA((1,)),
        ]

    def copy(self, k):
        return self.over(
            k, self.src.at[lax.rem(self.d + k, self.n_dp)], self.land.at[self.d], self.send_xy.at[k], self.recv_xy.at[self.d]
        )

    def landed(self, owner):
        return self.over(1, self.land.at[owner], self.land.at[owner], self.send_xy.at[1], self.recv_xy.at[owner])

    def own(self):
        return pltpu.make_async_copy(self.src.at[self.d], self.land.at[self.d], self.own_sem.at[0])

    def hop(self):
        return self.to_owner(self.land.at[self.d], self.final, self.send_z.at[0], self.recv_z.at[0])

    def begin(self):
        self.own().start()
        for k in range(1, self.n_dp):
            self.copy(k).start()

    def reduce(self):
        self.own().wait()
        for k in range(1, self.n_dp):
            self.landed(lax.rem(self.d + k, self.n_dp)).wait_recv()
        total = self.land[0].astype(F32)
        for owner in range(1, self.n_dp):
            total = total + self.land[owner].astype(F32)
        total = total.astype(BF16)

        @pl.when(self.stays)
        def _():
            self.final[...] = total

        @pl.when(self.moves)
        def _():
            self.land[self.d] = total
            self.hop().start()

    def end(self):
        pl.when(self.moves)(lambda: self.hop().wait())
        for k in range(1, self.n_dp):
            self.copy(k).wait_send()


class Collect:
    def __init__(self, line, n_dp, src, land, final, own_sem, send_xy, recv_xy, send_z, recv_z):
        self.line, self.n_dp, self.n_seq = line, n_dp, 2 * line.n_line
        self.src, self.land, self.final = src, land, final
        self.own_sem, self.send_xy, self.recv_xy, self.send_z, self.recv_z = own_sem, send_xy, recv_xy, send_z, recv_z
        self.d = lax.axis_index("dp")

    @staticmethod
    def sems(n_seq, n_dp):
        return [
            pltpu.SemaphoreType.DMA((1,)),
            pltpu.SemaphoreType.DMA((n_seq, n_dp)),
            pltpu.SemaphoreType.DMA((n_dp, n_seq)),
            pltpu.SemaphoreType.DMA((n_seq,)),
            pltpu.SemaphoreType.DMA((n_seq,)),
        ]

    def over(self, t, k):
        peer = lax.rem(self.d + k, self.n_dp)
        return pltpu.make_async_remote_copy(
            src_ref=self.src.at[peer, t],
            dst_ref=self.land.at[self.d, t],
            send_sem=self.send_xy.at[t, k],
            recv_sem=self.recv_xy.at[self.d, t],
            device_id={"dp": peer},
            device_id_type=MESH,
        )

    def landed(self, owner, t):
        return pltpu.make_async_remote_copy(
            src_ref=self.land.at[owner, t],
            dst_ref=self.land.at[owner, t],
            send_sem=self.send_xy.at[t, 1],
            recv_sem=self.recv_xy.at[owner, t],
            device_id={"dp": owner},
            device_id_type=MESH,
        )

    def own(self):
        return pltpu.make_async_copy(self.src.at[self.d], self.land.at[self.d], self.own_sem.at[0])

    def hop(self, t, slot):
        return pltpu.make_async_remote_copy(
            src_ref=self.land.at[self.d, t],
            dst_ref=self.final.at[slot],
            send_sem=self.send_z.at[t],
            recv_sem=self.recv_z.at[slot],
            device_id={"seq": t},
            device_id_type=MESH,
        )

    def place(self, j):
        return lax.rem(self.line.s + 1 + j, self.n_seq)

    def begin(self, ahead):
        self.ahead = ahead
        self.own().start()

        @pl.loop(0, ahead)
        def _(j):
            self.send(j)

    def send(self, j):
        for k in range(1, self.n_dp):
            self.over(self.place(j), k).start()

    def reduce(self, first, end):
        if first == 0:
            self.own().wait()

        @pl.loop(first, end)
        def _(j):
            t = self.place(j)
            pl.when(j + self.ahead < self.n_seq)(lambda: self.send(j + self.ahead))
            for k in range(1, self.n_dp):
                self.landed(lax.rem(self.d + k, self.n_dp), t).wait_recv()
            total = self.land[0, t].astype(F32)
            for owner in range(1, self.n_dp):
                total = total + self.land[owner, t].astype(F32)
            total = total.astype(BF16)

            @pl.when(t == self.line.s)
            def _():
                self.final[t] = total

            @pl.when(t != self.line.s)
            def _():
                self.land[self.d, t] = total
                self.hop(t, self.line.s).start()

    def end(self):
        @pl.loop(0, self.n_seq)
        def _(t):
            pl.when(t != self.line.s)(lambda: self.hop(t, t).wait())
            for k in range(1, self.n_dp):
                self.over(t, k).wait_send()


class RowSum:
    def __init__(self, n_dp, src, land, own_sem, send, recv):
        self.n_dp, self.src, self.land = n_dp, src, land
        self.own_sem, self.send, self.recv = own_sem, send, recv
        self.d = lax.axis_index("dp")

    @staticmethod
    def sems(n_dp):
        return [
            pltpu.SemaphoreType.DMA((1,)),
            pltpu.SemaphoreType.DMA((n_dp,)),
            pltpu.SemaphoreType.DMA((n_dp,)),
        ]

    def copy(self, k, slot):
        peer = lax.rem(self.d + k, self.n_dp)
        return pltpu.make_async_remote_copy(
            src_ref=self.src.at[peer],
            dst_ref=self.land.at[slot],
            send_sem=self.send.at[k],
            recv_sem=self.recv.at[slot],
            device_id={"dp": peer},
            device_id_type=MESH,
        )

    def own(self):
        return pltpu.make_async_copy(self.src.at[self.d], self.land.at[self.d], self.own_sem.at[0])

    def begin(self):
        self.own().start()
        for k in range(1, self.n_dp):
            self.copy(k, self.d).start()

    def finish(self, out):
        self.own().wait()
        for k in range(1, self.n_dp):
            self.copy(k, lax.rem(self.d + k, self.n_dp)).wait()
        total = self.land[0].astype(F32)
        for owner in range(1, self.n_dp):
            total = total + self.land[owner].astype(F32)
        out[...] = total


def greet_all(line, n_dp, relay):
    barrier = pltpu.get_barrier_semaphore()
    n_seq = 2 * line.n_line
    d = lax.axis_index("dp")
    for j in range(1, n_seq):
        pl.semaphore_signal(barrier, 1, device_id={"seq": lax.rem(line.s + j, n_seq)}, device_id_type=MESH)
    for k in range(1, n_dp):
        pl.semaphore_signal(barrier, 1, device_id={"dp": lax.rem(d + k, n_dp)}, device_id_type=MESH)

    if relay is None:
        pl.semaphore_wait(barrier, n_seq + n_dp - 2)
        return

    @pl.when(relay.moves)
    def _():
        for device in ((relay.slot, relay.target), (relay.owner_d, relay.owner_s)):
            pl.semaphore_signal(barrier, 1, device_id=device, device_id_type=MESH)

    pl.semaphore_wait(barrier, n_seq + n_dp - 2 + jnp.where(relay.moves, 2, 0))


def turn(values, lanes_low):
    half = HEAD_DIM // 2
    width = values.shape[-1]
    return jnp.where(
        lanes_low, pltpu.roll(values, width - half, values.ndim - 1), pltpu.roll(values, half, values.ndim - 1)
    )


def low_lanes(shape):
    return lax.rem(lax.broadcasted_iota(jnp.int32, shape, len(shape) - 1), HEAD_DIM) < HEAD_DIM // 2


def head_lanes(kv, h, q_cols):
    wide = jnp.concatenate([kv] * (q_cols // (2 * HEAD_DIM)), axis=1).astype(F32)
    swapped = pltpu.roll(wide, HEAD_DIM, 1)
    here = lax.div(lax.broadcasted_iota(jnp.int32, wide.shape, 1), HEAD_DIM) == h
    key, value = (wide, swapped) if h % 2 == 0 else (swapped, wide)
    key = jnp.where(here, key * (1.0 / math.sqrt(HEAD_DIM)), 0.0).astype(BF16)
    return key, jnp.where(here, value, 0.0).astype(BF16)


def hidden_keys(first, second, prefix, query_axis):
    query, key = (first, second) if query_axis == 0 else (second, first)
    return jnp.where((key <= query) | (key < prefix), 0.0, NEGATIVE)


def bias_shape(length):
    return (length, length) if length <= 2 * QUERY_TILE else (8, 128)


def fill_bias(bias, prefix, query_axis, length):
    if bias.shape[0] != length:
        return
    tile = min(length, QUERY_TILE)

    @pl.loop(0, length // tile)
    def _(i):
        at = pl.ds(pl.multiple_of(i * tile, tile), tile)
        first = i * tile + lax.broadcasted_iota(jnp.int32, (tile, length), 0)
        second = lax.broadcasted_iota(jnp.int32, (tile, length), 1)
        bias[at, :] = hidden_keys(first, second, prefix, query_axis)


def bias_tile(bias, prefix, query_axis, length, tile, i):
    at = pl.ds(pl.multiple_of(i * tile, tile), tile)
    if bias.shape[0] == length:
        return bias[at, :] if query_axis == 0 else bias[:, at]
    shape = (tile, length) if query_axis == 0 else (length, tile)
    first = lax.broadcasted_iota(jnp.int32, shape, 0)
    second = lax.broadcasted_iota(jnp.int32, shape, 1)
    if query_axis == 0:
        first = first + i * tile
    else:
        second = second + i * tile
    return hidden_keys(first, second, prefix, query_axis)


def attention_kernel(
    n_seq, n_dp, prefix_ref, tok_ref, cot_ref, cos_ref, sin_ref, gains_ref,
    w_query_ref, w_key_ref, w_value_ref, w_gate_ref, w_up_ref, wo_own, wd_own,
    hidden_ref, nmlp_ref, q_ref, kv_ref, mixed_ref, normed_hbm, cot_hbm, wqkv_hbm, wo_hbm, wgu_hbm, wd_hbm,
    full, cot, wqkv, wo, acc, part, sib, rcv, qkvb, gub, bias, save_sem, *sems,
):
    n = Line(n_seq)
    rows, width = tok_ref.shape
    micro, length, q_cols = q_ref.shape
    span = rows // micro
    cols_all = wqkv.shape[3]
    pair = 2 * rows
    tok = tok_ref[...].astype(F32)
    normed = (tok * lax.rsqrt(jnp.mean(tok * tok, axis=1, keepdims=True) + EPSILON)).astype(BF16)
    for m in range(micro):
        full[m, n.s] = normed[m * span : (m + 1) * span]
    cot[n.s] = cot_ref[...]

    sems = list(sems)
    take = lambda count: [sems.pop(0) for _ in range(count)]
    gathers = [Gather(n, full, *take(3), m=m) for m in range(micro)]
    scatters = [Scatter(n, part, sib, rcv, *take(4), m=m) for m in range(micro)]
    gather_cot = Gather(n, cot, *take(3))
    qkv_w = Spread(n, n_dp, qkvb, wqkv, *take(4))
    gu_w = Spread(n, n_dp, gub, wgu_hbm, *take(4))
    out_w = OutRows(n, n_dp, wo_own, wo, *take(4))
    down_w = Copies(n_dp, wd_own, wd_hbm, *take(3))

    repeat = n_seq // KV_HEADS
    ff_block = wd_own.shape[0]
    gain_attn = gains_ref[:, :1]
    gain_mlp = gains_ref[:, 2 * HEAD_DIM : 2 * HEAD_DIM + 1]
    for t in range(n_seq):
        head = slice(t // repeat * HEAD_DIM, (t // repeat + 1) * HEAD_DIM)
        qkvb[t, :, :q_cols] = (w_query_ref[:, t * q_cols : (t + 1) * q_cols].astype(F32) * gain_attn).astype(BF16)
        key_value = jnp.concatenate([w_key_ref[:, head], w_value_ref[:, head]], axis=1)
        qkvb[t, :, q_cols:] = (key_value.astype(F32) * gain_attn).astype(BF16)

    greet_all(n, n_dp, out_w)
    qkv_w.begin(n_seq)
    gathers[0].begin()
    out_w.begin()
    qkv_w.forward_own()
    for i, ref in enumerate((w_gate_ref, w_up_ref)):
        for owner in range(n_dp):
            for t in range(n_seq):
                cols = slice((owner * n_seq + t) * ff_block, (owner * n_seq + t + 1) * ff_block)
                first = (i * n_dp + owner) * ff_block
                gub[t, :, first : first + ff_block] = (ref[:, cols].astype(F32) * gain_mlp).astype(BF16)

    @pl.loop(1, n_seq)
    def _(j):
        qkv_w.forward_one(j, n_seq)

    out_w.forward()
    gathers[1].begin()
    down_w.begin()
    gu_w.forward_own()
    for j in range(n.n_line):
        gathers[0].visit(n.order(j))
    qkv_w.arrive()
    pltpu.make_async_copy(wqkv, wqkv_hbm, save_sem.at[1]).start()
    gu_w.begin(1 + AHEAD)

    low = low_lanes((span, cols_all))
    half_line = length // span // 2
    heads = q_cols // HEAD_DIM
    q_tile = min(length, QUERY_TILE)

    def project(m):
        @pl.loop(0, 2)
        def _(i):
            some = pl.ds(pl.multiple_of(i * half_line, half_line), half_line)
            value = nn(full[m, some].reshape(half_line * span, width), wqkv[...].reshape(width, cols_all))
            for k in range(half_line):
                at = pl.ds(pl.multiple_of((i * half_line + k) * span, span), span)
                block = value[k * span : (k + 1) * span]
                turned = (block * cos_ref[at, :] + turn(block, low) * sin_ref[at, :]).astype(BF16)
                q_ref[m, at, :] = turned[:, :q_cols]
                kv_ref[m, at, :] = turned[:, q_cols:]

    def attend(m, h):
        key, val = head_lanes(kv_ref[m], h, q_cols)

        @pl.loop(0, length // q_tile)
        def _(i):
            at = pl.ds(pl.multiple_of(i * q_tile, q_tile), q_tile)
            scores = nt(q_ref[m, at, :], key) + bias_tile(bias, prefix_ref[m], 0, length, q_tile, i)
            weights = jnp.exp(scores - jnp.max(scores, axis=1, keepdims=True))
            inverse = 1.0 / jnp.sum(weights, axis=1, keepdims=True)
            mixed = nn((weights * inverse).astype(BF16), val)
            if h == 0:
                acc[at, :] = mixed
            else:
                acc[at, :] += mixed

    sent = 0
    for m in range(micro):
        project(m)
        fill_bias(bias, prefix_ref[m], 0, length)
        for h in range(heads):
            if m + 1 < micro:
                for j in range(*spread_work(n.n_line, heads, h)):
                    gathers[m + 1].visit(n.order(j))
            if m == 1 and h == 0:
                down_w.pass_on()
            attend(m, h)
            done = m * heads + h
            for _ in range(*spread_work(n_seq - 1, micro * heads - 1, done - 1) if done else (0,)):
                sent += 1
                gu_w.forward_one(sent, AHEAD)
        mixed_ref[m] = acc[...].astype(BF16)
        if m == 0:
            out_w.arrive()
            pltpu.make_async_copy(wo, wo_hbm, save_sem.at[2]).start()

        @pl.loop(0, width // TILE)
        def _(w):
            cols = pl.ds(pl.multiple_of(w * TILE, TILE), TILE)
            value = nn(mixed_ref[m], wo[:, :, cols].reshape(q_cols, TILE))
            part[m, :, :, cols] = value.astype(BF16).reshape(n_seq, span, TILE)

        scatters[m].begin()
        if m == 0:
            gather_cot.begin()

    pltpu.make_async_copy(full, normed_hbm, save_sem.at[0]).start()
    gather_cot.visit(n.l)
    for time in range(n.last):
        for scatter in scatters:
            scatter.step(time)
        gather_cot.visit(n.order(time + 1))
    pltpu.make_async_copy(cot, cot_hbm, save_sem.at[3]).start()
    for m in range(micro):
        at = slice(m * span, (m + 1) * span)
        scatters[m].finish(hidden_ref.at[at])
    hidden = hidden_ref[...] + tok_ref[...].astype(F32)
    hidden_ref[...] = hidden
    nmlp_ref[...] = (hidden * lax.rsqrt(jnp.mean(hidden * hidden, axis=1, keepdims=True) + EPSILON)).astype(BF16)
    gu_w.arrive()
    down_w.end()
    pltpu.make_async_copy(full, normed_hbm, save_sem.at[0]).wait()
    pltpu.make_async_copy(wqkv, wqkv_hbm, save_sem.at[1]).wait()
    pltpu.make_async_copy(wo, wo_hbm, save_sem.at[2]).wait()
    pltpu.make_async_copy(cot, cot_hbm, save_sem.at[3]).wait()
    for gather in gathers:
        gather.end()
    gather_cot.end()
    qkv_w.end()
    gu_w.end()
    out_w.end()


def attention_call(prefix, tok, cot, cos, sin, gains, w_query, w_key, w_value, w_gate, w_up, wo_own, wd_own, n_seq, n_dp):
    rows, width = tok.shape
    micro = prefix.shape[0]
    length = cos.shape[0]
    shard = wo_own.shape[0]
    q_cols = width // n_seq
    qkv_cols = q_cols + 2 * HEAD_DIM
    ff_block = wd_own.shape[0]
    gu_cols = 2 * n_dp * ff_block
    every = n_seq * rows
    any_spec = pl.BlockSpec(memory_space=pl.ANY)
    vmem = pl.BlockSpec(memory_space=pltpu.VMEM)
    outs = [
        ((rows, width), F32, vmem),
        ((rows, width), BF16, vmem),
        ((micro, length, q_cols), BF16, vmem),
        ((micro, length, 2 * HEAD_DIM), BF16, vmem),
        ((micro, length, q_cols), BF16, vmem),
        ((micro, n_seq, rows // micro, width), BF16, any_spec),
        ((n_seq, rows, width), BF16, any_spec),
        ((n_dp, n_seq, shard, qkv_cols), BF16, any_spec),
        ((n_dp, shard, width), BF16, any_spec),
        ((n_dp, n_seq, shard, gu_cols), BF16, any_spec),
        ((n_dp, ff_block, width), BF16, any_spec),
    ]
    return pl.pallas_call(
        functools.partial(attention_kernel, n_seq, n_dp),
        out_shape=tuple(jax.ShapeDtypeStruct(s, t) for s, t, _ in outs),
        in_specs=[pl.BlockSpec(memory_space=pltpu.SMEM)] + [vmem] * 10 + [any_spec] * 2,
        out_specs=tuple(spec for _, _, spec in outs),
        scratch_shapes=[
            pltpu.VMEM((micro, n_seq, rows // micro, width), BF16),
            pltpu.VMEM((n_seq, rows, width), BF16),
            pltpu.VMEM((n_dp, n_seq, shard, qkv_cols), BF16),
            pltpu.VMEM((n_dp, shard, width), BF16),
            pltpu.VMEM((length, q_cols), F32),
            pltpu.VMEM((micro, n_seq, rows // micro, width), BF16),
            *Scatter.buffers(n_seq, rows // micro, width, micro),
            pltpu.VMEM((n_seq, shard, qkv_cols), BF16),
            pltpu.VMEM((n_seq, shard, gu_cols), BF16),
            pltpu.VMEM(bias_shape(length), F32),
            pltpu.SemaphoreType.DMA((4,)),
            *Gather.sems(n_seq) * micro,
            *Scatter.sems(n_seq) * micro,
            *Gather.sems(n_seq),
            *Spread.sems(n_seq, n_dp),
            *Spread.sems(n_seq, n_dp),
            *OutRows.sems(n_dp),
            *Copies.sems(n_dp),
        ],
        compiler_params=pltpu.CompilerParams(
            collective_id=2, has_side_effects=True, vmem_limit_bytes=VMEM_LIMIT
        ),
        cost_estimate=pl.CostEstimate(flops=10**10, bytes_accessed=40 << 20, transcendentals=0),
        name="attention",
    )(prefix, tok, cot, cos, sin, gains, w_query, w_key, w_value, w_gate, w_up, wo_own, wd_own)


def mlp_kernel(
    n_seq, n_dp, x_ref, hidden_ref, cot_hbm, wgu_hbm, wd_hbm,
    branch_ref, gh_ref, pout_hbm, dgu_hbm, dwd_ref,
    full, cot, wgu, wd, act, gg, gu, part, sib, rcv, dwd, land, total, stage_gu, stage_rows, load_sem, gu_sem, rows_sem, *sems,
):
    n = Line(n_seq)
    rows, width = x_ref.shape
    ff = wd.shape[0]
    pair = 2 * rows
    loads = [
        pltpu.make_async_copy(src, dst, load_sem.at[i])
        for i, (src, dst) in enumerate(
            [(wgu_hbm, wgu), (cot_hbm, cot), (wd_hbm, wd)]
        )
    ]
    for load in loads:
        load.start()
    full[n.s] = x_ref[...]
    greet_all(n, n_dp, None)
    gather = Gather(n, full, *sems[:3])
    scatter = Scatter(n, part, sib, rcv, *sems[3:7])
    down = RowSum(n_dp, dwd, land, *sems[7:10])
    gather.begin()
    for load in loads:
        load.wait()

    @pl.loop(0, n.n_line)
    def _(j):
        chip = n.order(j)
        gather.visit(chip)
        at = pl.ds(pl.multiple_of(chip * pair, pair), pair)
        two = pl.ds(pl.multiple_of(2 * chip, 2), 2)

        @pl.loop(0, ff // TILE)
        def _(f):
            cols = pl.ds(pl.multiple_of(f * TILE, TILE), TILE)
            x = full[two].reshape(pair, width)
            gate = nn(x, wgu[:, cols])
            up = nn(x, wgu[:, pl.ds(pl.multiple_of(ff + f * TILE, TILE), TILE)])
            grad = nt(cot[two].reshape(pair, width), wd[cols, :])
            sig = jax.nn.sigmoid(gate)
            silu = gate * sig
            act[at, cols] = (silu * up).astype(BF16)
            gg[at, cols] = (grad * up * (sig + silu * (1.0 - sig))).astype(BF16)
            gu[at, cols] = (grad * silu).astype(BF16)

        @pl.loop(0, width // TILE)
        def _(w):
            cols = pl.ds(pl.multiple_of(w * TILE, TILE), TILE)
            value = nt(gg[at, :], wgu[cols, :ff]) + nt(gu[at, :], wgu[cols, ff:])
            part[two, :, cols] = value.astype(BF16).reshape(2, rows, TILE)

    scatter.begin()
    scatter.step(0)
    owners = TILE // dwd.shape[1]

    def down_grad(f):
        cols = pl.ds(pl.multiple_of(f * TILE, TILE), TILE)
        at = pl.ds(f * owners, owners)
        for w in range(0, width, 2 * TILE):
            span = cot[:, :, w : w + 2 * TILE].reshape(n_seq * rows, 2 * TILE)
            value = tn(act[:, cols], span).astype(BF16)
            dwd[at, :, w : w + 2 * TILE] = value.reshape(owners, dwd.shape[1], 2 * TILE)

    if owners == 1:

        @pl.loop(1, n_dp + 1)
        def _(k):
            down_grad(lax.rem(down.d + k, n_dp))
            pl.when(k < n_dp)(lambda: down.copy(k, down.d).start())

        down.own().start()
    else:
        pl.loop(0, ff // TILE)(down_grad)
        down.begin()

    def gate_up_grads(first, end):
        @pl.loop(first, end)
        def _(w):
            slot = lax.rem(w, 2)
            cols = pl.ds(pl.multiple_of(w * TILE, TILE), TILE)
            x = full[:, :, cols].reshape(n_seq * rows, TILE)
            copy = pltpu.make_async_copy(stage_gu.at[slot], dgu_hbm.at[cols, :], gu_sem.at[slot])
            pl.when(w >= 2)(lambda: copy.wait())
            stage_gu[slot, :, :ff] = tn(x, gg[...]).astype(BF16)
            stage_gu[slot, :, ff:] = tn(x, gu[...]).astype(BF16)
            copy.start()

    def out_parts(first, end):
        @pl.loop(first, end)
        def _(chip):
            slot = lax.rem(chip, 2)
            at = pl.ds(pl.multiple_of(chip * pair, pair), pair)
            two = pl.ds(pl.multiple_of(2 * chip, 2), 2)
            copies = [
                pltpu.make_async_copy(
                    stage_rows.at[slot, pl.ds(i * rows, rows)], pout_hbm.at[2 * chip + i], rows_sem.at[slot + 2 * i]
                )
                for i in range(2)
            ]

            @pl.when(chip >= 2)
            def _():
                for copy in copies:
                    copy.wait()

            for w in range(0, width, 2 * TILE):
                stage_rows[slot, :pair, w : w + 2 * TILE] = nn(act[at, :], wd[:, w : w + 2 * TILE]).astype(BF16)
            for copy in copies:
                copy.start()

    def drain_out():
        for slot in range(2):
            for i in range(2):
                pltpu.make_async_copy(
                    stage_rows.at[slot, pl.ds(i * rows, rows)], pout_hbm.at[i], rows_sem.at[slot + 2 * i]
                ).wait()

    for time in range(n.last):
        if time > 0:
            scatter.step(time)
        if time == 0:
            out_parts(0, n.n_line)
        gate_up_grads(*spread_work(width // TILE, n.last, time))
    scatter.finish(total)
    grad_hidden = cot[n.s].astype(F32) + norm_back(hidden_ref[...], total[...])
    gh_ref[...] = grad_hidden
    branch_ref[...] = grad_hidden.astype(BF16)
    drain_out()
    for slot in range(2):
        pltpu.make_async_copy(stage_gu.at[slot], dgu_hbm.at[pl.ds(0, TILE), :], gu_sem.at[slot]).wait()
    down.finish(dwd_ref)
    gather.end()


def mlp_call(x, hidden, cot, wgu, wd, n_seq, n_dp):
    rows, width = x.shape
    ff = wd.shape[0]
    every = n_seq * rows
    any_spec = pl.BlockSpec(memory_space=pl.ANY)
    vmem = pl.BlockSpec(memory_space=pltpu.VMEM)
    return pl.pallas_call(
        functools.partial(mlp_kernel, n_seq, n_dp),
        out_shape=(
            jax.ShapeDtypeStruct((rows, width), BF16),
            jax.ShapeDtypeStruct((rows, width), F32),
            jax.ShapeDtypeStruct((n_seq, rows, width), BF16),
            jax.ShapeDtypeStruct((width, 2 * ff), BF16),
            jax.ShapeDtypeStruct((ff // n_dp, width), F32),
        ),
        in_specs=[vmem] * 2 + [any_spec] * 3,
        out_specs=(vmem, vmem, any_spec, any_spec, vmem),
        scratch_shapes=[
            pltpu.VMEM((n_seq, rows, width), BF16),
            pltpu.VMEM((n_seq, rows, width), BF16),
            pltpu.VMEM((width, 2 * ff), BF16),
            pltpu.VMEM((ff, width), BF16),
            pltpu.VMEM((every, ff), BF16),
            pltpu.VMEM((every, ff), BF16),
            pltpu.VMEM((every, ff), BF16),
            pltpu.VMEM((n_seq, rows, width), BF16),
            *Scatter.buffers(n_seq, rows, width),
            pltpu.VMEM((n_dp, ff // n_dp, width), BF16),
            pltpu.VMEM((n_dp, ff // n_dp, width), BF16),
            pltpu.VMEM((rows, width), F32),
            pltpu.VMEM((2, TILE, 2 * ff), BF16),
            pltpu.VMEM((2, TILE, width), BF16),
            pltpu.SemaphoreType.DMA((3,)),
            pltpu.SemaphoreType.DMA((2,)),
            pltpu.SemaphoreType.DMA((4,)),
            *Gather.sems(n_seq),
            *Scatter.sems(n_seq),
            *RowSum.sems(n_dp),
        ],
        compiler_params=pltpu.CompilerParams(
            collective_id=1, has_side_effects=True, vmem_limit_bytes=VMEM_LIMIT
        ),
        cost_estimate=pl.CostEstimate(flops=18 * every * width * ff, bytes_accessed=40 << 20, transcendentals=0),
        name="mlp",
    )(x, hidden, cot, wgu, wd)


def backward_kernel(
    n_seq, n_dp, prefix_ref, branch_ref, tok_ref, q_ref, kv_ref, mixed_ref, cos_ref, sin_ref, gains_ref,
    w_query_ref, w_key_ref, w_value_ref, gh_hbm, hidden_hbm, pout_hbm, normed_hbm, wqkv_hbm, wo_hbm, dgu_hbm,
    out_ref, in_ref, dgain_ref, dq_ref, dk_ref, dv_ref, dwo_out, dgate_ref, dup_ref,
    full, tiles, wqkv, wo, gm, acc_q, acc_k, acc_v, bias, gqkv, part, sib, rcv, sib_o, rcv_o,
    land_gu, final_gu, dqkv, land_qkv, final_qkv, dwo, land_o, final_o, total, load_sem, tile_sem, *sems,
):
    n = Line(n_seq)
    rows, width = branch_ref.shape
    micro, length, q_cols = q_ref.shape
    span = rows // micro
    pair = 2 * rows
    loads = [
        pltpu.make_async_copy(src, dst, load_sem.at[i])
        for i, (src, dst) in enumerate(
            [(pout_hbm, part), (wo_hbm, wo), (wqkv_hbm, wqkv), (hidden_hbm, total), (gh_hbm, in_ref)]
        )
    ]
    for load in loads:
        load.start()
    for m in range(micro):
        full[m, n.s] = branch_ref[m * span : (m + 1) * span, :]
    sems = list(sems)
    take = lambda count: [sems.pop(0) for _ in range(count)]
    gathers = [Gather(n, full, *take(3), m=m) for m in range(micro)]
    scatter = Scatter(n, part, sib, rcv, *take(4))
    scatter_out = Scatter(n, part, sib_o, rcv_o, *take(4))
    gu_sum = Collect(n, n_dp, dgu_hbm, land_gu, final_gu, *take(5))
    qkv_sum = Collect(n, n_dp, dqkv, land_qkv, final_qkv, *take(5))
    out_sum = OutSum(n, n_dp, dwo, land_o, final_o, *take(5))
    greet_all(n, n_dp, out_sum)
    gathers[0].begin()
    gu_sum.begin(3)
    loads[0].wait()
    loads[1].wait()
    late = n_seq * 5 // 8
    scatter_out.begin()
    gathers[1].begin()
    for j in range(n.n_line):
        gathers[0].visit(n.order(j))
    loads[2].wait()

    heads = q_cols // HEAD_DIM
    scale = 1.0 / math.sqrt(HEAD_DIM)
    q_tile = min(length, QUERY_TILE)
    low = low_lanes((length, q_cols + 2 * HEAD_DIM))
    here = lax.div(lax.broadcasted_iota(jnp.int32, (length, q_cols), 1), HEAD_DIM)

    def attend_back(m, h):
        key, val = head_lanes(kv_ref[m], h, q_cols)

        @pl.loop(0, length // q_tile)
        def _(i):
            at = pl.ds(pl.multiple_of(i * q_tile, q_tile), q_tile)
            query, grad = q_ref[m, at, :], gm[m, at, :]
            scores = nt(key, query) + bias_tile(bias, prefix_ref[m], 1, length, q_tile, i)
            weights = jnp.exp(scores - jnp.max(scores, axis=0, keepdims=True))
            probs = weights * (1.0 / jnp.sum(weights, axis=0, keepdims=True))
            grad_probs = nt(val, grad)
            delta = jnp.sum(probs * grad_probs, axis=0, keepdims=True)
            grad_scores = (probs * (grad_probs - delta)).astype(BF16)
            acc_q[at, :] += tn(grad_scores, key)
            acc_k[...] += jnp.where(here == h, nn(grad_scores, query), 0.0)
            acc_v[...] += jnp.where(here == h, nn(probs.astype(BF16), grad), 0.0)

    shard = dwo.shape[1]

    def out_grads():

        @pl.loop(0, width // TILE)
        def _(w):
            cols = pl.ds(pl.multiple_of(w * TILE, TILE), TILE)
            d_out = jnp.zeros((q_cols, TILE), F32)
            for m in range(micro):
                d_out = d_out + tn(mixed_ref[m], full[m, :, :, cols].reshape(length, TILE))
            dwo[:, :, cols] = d_out.astype(BF16).reshape(n_dp, shard, TILE)

        out_sum.begin()

    for m in range(micro):
        gm[m] = nt(full[m].reshape(length, width), wo[...].reshape(q_cols, width)).astype(BF16)
        fill_bias(bias, prefix_ref[m], 1, length)
        for ref in (acc_q, acc_k, acc_v):
            ref[...] = jnp.zeros_like(ref)
        for h in range(heads):
            if m + 1 < micro:
                for j in range(*spread_work(n.n_line, heads, h)):
                    gathers[m + 1].visit(n.order(j))
            if m == 0:
                for time in range(*spread_work(n.last, heads, h)):
                    scatter_out.step(time)
            if m == 1 and h == 0:
                out_grads()
            for j in range(*spread_work(late, micro * heads, m * heads + h)):
                gu_sum.reduce(j, j + 1)
            attend_back(m, h)

        def fold(ref):
            total = ref[:, : 2 * HEAD_DIM]
            for w in range(2 * HEAD_DIM, q_cols, 2 * HEAD_DIM):
                total = total + ref[:, w : w + 2 * HEAD_DIM]
            return total + pltpu.roll(total, HEAD_DIM, 1)

        first = lax.broadcasted_iota(jnp.int32, (length, 2 * HEAD_DIM), 1) < HEAD_DIM
        grads = jnp.concatenate([acc_q[...], jnp.where(first, fold(acc_k) * scale, fold(acc_v))], axis=1)
        gqkv[m] = (grads * cos_ref[...] - turn(grads, low) * sin_ref[...]).astype(BF16)

    loads[3].wait()
    scatter_out.finish(total, True)
    out_ref[...] = total[...].astype(BF16)
    for m in range(micro):

        @pl.loop(0, width // TILE)
        def _(w):
            at = pl.ds(pl.multiple_of(w * TILE, TILE), TILE)
            value = nt(gqkv[m], wqkv[at, :])
            part[:, m * span : (m + 1) * span, at] = value.astype(BF16).reshape(n_seq, span, TILE)

    scatter.begin()

    half = n_seq // 2
    depth = half * shard

    def fetch(w):
        cols = pl.ds(pl.multiple_of(w * depth, depth), depth)
        slot = lax.rem(w, 2)
        return pltpu.make_async_copy(normed_hbm.at[:, :, :, cols], tiles.at[slot], tile_sem.at[slot])

    fetch(jnp.int32(0)).start()

    @pl.loop(0, n_dp * 2)
    def _(w):
        pl.when(w + 1 < n_dp * 2)(lambda: fetch(w + 1).start())
        fetch(w).wait()
        slot = lax.rem(w, 2)
        d_qkv = jnp.zeros((depth, q_cols + 2 * HEAD_DIM), F32)
        for m in range(micro):
            d_qkv = d_qkv + tn(tiles[slot, m].reshape(length, depth), gqkv[m])
        at = pl.ds(pl.multiple_of(lax.rem(w, 2) * half, half), half)
        dqkv[lax.div(w, 2), at] = d_qkv.astype(BF16).reshape(half, shard, q_cols + 2 * HEAD_DIM)

    qkv_sum.begin(n_seq)
    out_sum.reduce()
    for time in range(n.last):
        scatter.step(time)
        first, end = spread_work(n_seq - late, n.last, time)
        gu_sum.reduce(late + first, late + end)
    qkv_sum.reduce(0, n_seq)
    scatter.finish(total)
    loads[4].wait()
    in_ref[...] += norm_back(tok_ref[...].astype(F32), total[...])
    gu_sum.end()
    ff_block = dgate_ref.shape[1] // (n_dp * n_seq)
    gain_attn = gains_ref[:, :1]
    for i, ref in enumerate((dgate_ref, dup_ref)):
        for owner in range(n_dp):
            for t in range(n_seq):
                cols = slice((owner * n_seq + t) * ff_block, (owner * n_seq + t + 1) * ff_block)
                first = (i * n_dp + owner) * ff_block
                ref[:, cols] = final_gu[t, :, first : first + ff_block]
    qkv_sum.end()
    repeat = n_seq // KV_HEADS
    dots = jnp.zeros((shard, 1), F32)
    for t in range(n_seq):
        cols = slice(t * q_cols, (t + 1) * q_cols)
        value = final_qkv[t, :, :q_cols].astype(F32)
        dots = dots + jnp.sum(value * w_query_ref[:, cols].astype(F32), axis=1, keepdims=True)
        dq_ref[:, cols] = value * gain_attn
    for g in range(KV_HEADS):
        cols = slice(g * HEAD_DIM, (g + 1) * HEAD_DIM)
        for i, (ref, w_ref) in enumerate(((dk_ref, w_key_ref), (dv_ref, w_value_ref))):
            lanes = slice(q_cols + i * HEAD_DIM, q_cols + (i + 1) * HEAD_DIM)
            value = final_qkv[g * repeat, :, lanes].astype(F32)
            for t in range(g * repeat + 1, (g + 1) * repeat):
                value = value + final_qkv[t, :, lanes].astype(F32)
            dots = dots + jnp.sum(value * w_ref[:, cols].astype(F32), axis=1, keepdims=True)
            ref[:, cols] = value * gain_attn
    dgain_ref[...] = dots * jnp.ones((shard, 2 * HEAD_DIM), F32)
    out_sum.end()
    dwo_out[...] = final_o[...].astype(F32)
    for gather in gathers:
        gather.end()


def backward_call(
    prefix, branch, tok, q, kv, mixed, cos, sin, gains, w_query, w_key, w_value,
    gh, hidden, pout, normed, wqkv, wo, dgu,
):
    rows, width = branch.shape
    n_dp, n_seq, shard, gu_cols = dgu.shape
    ff = gu_cols // 2 * n_seq
    micro, length, q_cols = q.shape
    qkv_cols = q_cols + 2 * HEAD_DIM
    any_spec = pl.BlockSpec(memory_space=pl.ANY)
    vmem = pl.BlockSpec(memory_space=pltpu.VMEM)
    line_rows = pltpu.VMEM((n_seq, rows, width), BF16)
    return pl.pallas_call(
        functools.partial(backward_kernel, n_seq, n_dp),
        out_shape=(
            jax.ShapeDtypeStruct((rows, width), BF16),
            jax.ShapeDtypeStruct((rows, width), F32),
            jax.ShapeDtypeStruct((shard, 2 * HEAD_DIM), F32),
            *(jax.ShapeDtypeStruct(w.shape, F32) for w in (w_query, w_key, w_value)),
            jax.ShapeDtypeStruct((shard, width), F32),
            jax.ShapeDtypeStruct((shard, ff), BF16),
            jax.ShapeDtypeStruct((shard, ff), BF16),
        ),
        in_specs=[pl.BlockSpec(memory_space=pltpu.SMEM)] + [vmem] * 11 + [any_spec] * 7,
        out_specs=(vmem,) * 9,
        scratch_shapes=[
            pltpu.VMEM((micro, n_seq, rows // micro, width), BF16),
            pltpu.VMEM((2, micro, n_seq, rows // micro, n_seq // 2 * shard), BF16),
            pltpu.VMEM((width, qkv_cols), BF16),
            pltpu.VMEM(wo.shape, BF16),
            pltpu.VMEM((micro, length, q_cols), BF16),
            pltpu.VMEM((length, q_cols), F32),
            pltpu.VMEM((length, q_cols), F32),
            pltpu.VMEM((length, q_cols), F32),
            pltpu.VMEM(bias_shape(length), F32),
            pltpu.VMEM((micro, length, qkv_cols), BF16),
            line_rows,
            *Scatter.buffers(n_seq, rows, width),
            *Scatter.buffers(n_seq, rows, width),
            pltpu.VMEM((n_dp, n_seq, shard, gu_cols), BF16),
            pltpu.VMEM((n_seq, shard, gu_cols), BF16),
            pltpu.VMEM((n_dp, n_seq, shard, qkv_cols), BF16),
            pltpu.VMEM((n_dp, n_seq, shard, qkv_cols), BF16),
            pltpu.VMEM((n_seq, shard, qkv_cols), BF16),
            pltpu.VMEM((n_dp, shard, width), BF16),
            pltpu.VMEM((n_dp, shard, width), BF16),
            pltpu.VMEM((shard, width), BF16),
            pltpu.VMEM((rows, width), F32),
            pltpu.SemaphoreType.DMA((5,)),
            pltpu.SemaphoreType.DMA((2,)),
            *Gather.sems(n_seq) * micro,
            *Scatter.sems(n_seq),
            *Scatter.sems(n_seq),
            *Collect.sems(n_seq, n_dp),
            *Collect.sems(n_seq, n_dp),
            *OutSum.sems(n_dp),
        ],
        compiler_params=pltpu.CompilerParams(
            collective_id=3, has_side_effects=True, vmem_limit_bytes=VMEM_LIMIT
        ),
        cost_estimate=pl.CostEstimate(flops=10**10, bytes_accessed=40 << 20, transcendentals=0),
        name="backward",
    )(
        prefix, branch, tok, q, kv, mixed, cos, sin, gains, w_query, w_key, w_value,
        gh, hidden, pout, normed, wqkv, wo, dgu,
    )


def body(
    tokens, cotangent, prefix_len, attn_gain, w_query, w_key, w_value, w_out, mlp_gain, w_gate, w_up, w_down
):
    n_dp = lax.axis_size("dp")
    n_seq = lax.axis_size("seq")
    micro, span, width = tokens.shape
    shard = w_query.shape[0]
    rows = micro * span
    cos, sin = rope_tables(span * n_seq, HEADS // n_seq * HEAD_DIM)
    gains = jnp.concatenate(
        [jnp.broadcast_to(g.astype(F32)[:, None], (shard, 2 * HEAD_DIM)) for g in (attn_gain, mlp_gain)], axis=1
    )
    tok = tokens.reshape(rows, width)
    cot = cotangent.reshape(rows, width)
    hidden, normed_mlp, q, kv, mixed, normed, cot_all, wqkv, wo, wgu, wd = attention_call(
        prefix_len, tok, cot, cos, sin, gains, w_query, w_key, w_value, w_gate, w_up, w_out, w_down, n_seq, n_dp
    )
    branch, grad_hidden, out_part, dgu, w_down_grad = mlp_call(
        normed_mlp, hidden, cot_all, wgu.reshape(width, -1), wd.reshape(-1, width), n_seq, n_dp
    )
    block_out, input_grad, attn_gain_grad, *w_grads, w_out_grad, d_gate, d_up = backward_call(
        prefix_len, branch, tok, q, kv, mixed, cos, sin, gains, w_query, w_key, w_value,
        grad_hidden, hidden, out_part, normed, wqkv.reshape(width, -1), wo.reshape(-1, width), dgu.reshape(n_dp, n_seq, shard, -1),
    )
    mlp_gain_grad = jnp.sum(d_gate.astype(F32) * w_gate.astype(F32), axis=1)
    mlp_gain_grad = mlp_gain_grad + jnp.sum(d_up.astype(F32) * w_up.astype(F32), axis=1)
    gain_column = mlp_gain.astype(F32)[:, None]
    return (
        block_out.reshape(micro, span, width),
        input_grad.reshape(micro, span, width),
        attn_gain_grad[:, 0],
        *w_grads,
        w_out_grad,
        mlp_gain_grad,
        d_gate.astype(F32) * gain_column,
        d_up.astype(F32) * gain_column,
        w_down_grad,
    )


def solution(mesh):
    rows = P("dp", "seq", None)
    vec = P(("dp", "seq"))
    mat = P(("dp", "seq"), None)
    in_specs = (rows, rows, P("dp"), vec, mat, mat, mat, mat, vec, mat, mat, mat)
    out_specs = (rows, rows, vec, mat, mat, mat, mat, vec, mat, mat, mat)
    return jax.shard_map(body, mesh=mesh, in_specs=in_specs, out_specs=out_specs, check_vma=False)
```

```python
import functools
import math

import jax
import jax.numpy as jnp
import numpy as np
from jax import lax
from jax.experimental import pallas as pl
from jax.experimental.pallas import tpu as pltpu
from jax.sharding import PartitionSpec as P

HEADS = 32
KV_HEADS = 8
HEAD_DIM = 64
EPSILON = 1e-05
THETA = 500000.0
NEGATIVE = -1e30
BF16 = jnp.bfloat16
F32 = jnp.float32
MESH = pl.DeviceIdType.MESH
TILE = 256
QUERY_TILE = 256
AHEAD = 4
VMEM_LIMIT = 61 << 20


def rope_tables(length, q_cols):
    half = HEAD_DIM // 2
    f32 = np.float32
    index_half = np.arange(half, dtype=f32)
    inverse = np.power(f32(THETA), f32(-2.0) * index_half / f32(HEAD_DIM)).astype(f32)
    wavelength = (f32(2.0 * math.pi) / inverse).astype(f32)
    smooth = ((f32(8192.0) / wavelength - f32(1.0)) / f32(3.0)).astype(f32)
    blended = ((f32(1.0) - smooth) * inverse / f32(32.0) + smooth * inverse).astype(f32)
    inverse = np.where(
        wavelength < 2048.0, inverse, np.where(wavelength > 8192.0, inverse / f32(32.0), blended)
    ).astype(f32)
    angles = (np.arange(length, dtype=f32)[:, None] * inverse[None, :]).astype(f32)
    cos, sin = np.cos(angles).astype(f32), np.sin(angles).astype(f32)
    count = q_cols // HEAD_DIM + 1
    ones, zeros = np.ones((length, HEAD_DIM), f32), np.zeros((length, HEAD_DIM), f32)
    cos = np.concatenate([cos, cos] * count + [ones], axis=1)
    sin = np.concatenate([-sin, sin] * count + [zeros], axis=1)
    return jnp.asarray(cos), jnp.asarray(sin)


def nn(a, b):
    return jnp.dot(a, b, preferred_element_type=F32)


def tn(a, b):
    return lax.dot_general(a, b, (((0,), (0,)), ((), ())), preferred_element_type=F32)


def nt(a, b):
    return lax.dot_general(a, b, (((1,), (1,)), ((), ())), preferred_element_type=F32)


class Line:
    def __init__(self, n_seq):
        self.n_line = n_seq // 2
        self.last = self.n_line - 1
        self.s = lax.axis_index("seq")
        self.c = lax.rem(self.s, 2)
        self.l = lax.div(self.s, 2)
        self.sibling = self.s + 1 - 2 * self.c
        self.right = jnp.minimum(self.s + 2, n_seq - 2 + self.c)
        self.left = jnp.maximum(self.s - 2, self.c)
        self.has_right = self.l < self.last
        self.has_left = self.l > 0

    def greet(self, n_dp):
        barrier = pltpu.get_barrier_semaphore()
        d = lax.axis_index("dp")
        for k in range(1, n_dp):
            pl.semaphore_signal(barrier, 1, device_id={"dp": lax.rem(d + k, n_dp)}, device_id_type=MESH)
        pl.semaphore_signal(barrier, 1, device_id={"seq": self.sibling}, device_id_type=MESH)

        @pl.when(self.has_right)
        def _():
            pl.semaphore_signal(barrier, 1, device_id={"seq": self.right}, device_id_type=MESH)

        @pl.when(self.has_left)
        def _():
            pl.semaphore_signal(barrier, 1, device_id={"seq": self.left}, device_id_type=MESH)

        pl.semaphore_wait(barrier, n_dp - 1 + jnp.where(self.has_right & self.has_left, 3, 2))

    def order(self, j):
        near = jnp.minimum(self.l, self.last - self.l)
        half = lax.div(j + 1, 2)
        both = jnp.where(lax.rem(j, 2) == 1, self.l - half, self.l + half)
        far = jnp.where(self.l <= self.last - self.l, j, self.last - j)
        return jnp.where(j <= 2 * near, both, far)


def remote(src, dst, send, recv, seq):
    return pltpu.make_async_remote_copy(
        src_ref=src, dst_ref=dst, send_sem=send, recv_sem=recv, device_id={"seq": seq}, device_id_type=MESH
    )


class Gather:
    def __init__(self, line, full, send_z, send_c, recv, m=None):
        self.m = m
        self.line, self.full, self.send_z, self.send_c, self.recv = line, full, send_z, send_c, recv

    @staticmethod
    def sems(n_seq):
        n_line = n_seq // 2
        return [
            pltpu.SemaphoreType.DMA((n_line + 1,)),
            pltpu.SemaphoreType.DMA((n_line,)),
            pltpu.SemaphoreType.DMA((n_seq,)),
        ]

    def copy(self, index, send, seq):
        chunk = self.full.at[index] if self.m is None else self.full.at[self.m, index]
        return remote(chunk, chunk, send, self.recv.at[index], seq)

    def begin(self):
        n = self.line
        pl.when(n.has_right)(lambda: self.copy(n.s, self.send_z.at[n.l], n.right).start())
        pl.when(n.has_left)(lambda: self.copy(n.s, self.send_z.at[n.n_line], n.left).start())
        self.copy(n.s, self.send_c.at[n.l], n.sibling).start()

    def visit(self, chip):
        n = self.line
        mine = 2 * chip + n.c

        @pl.when(chip != n.l)
        def _():
            self.copy(mine, self.send_c.at[chip], n.sibling).wait_recv()
            pl.when((chip < n.l) & n.has_right)(
                lambda: self.copy(mine, self.send_z.at[chip], n.right).start()
            )
            pl.when((chip > n.l) & n.has_left)(
                lambda: self.copy(mine, self.send_z.at[chip], n.left).start()
            )
            self.copy(mine, self.send_c.at[chip], n.sibling).start()

        self.copy(2 * chip + 1 - n.c, self.send_c.at[chip], n.sibling).wait_recv()

    def end(self):
        n = self.line

        @pl.loop(0, n.n_line)
        def _(chip):
            mine = 2 * chip + n.c
            self.copy(mine, self.send_c.at[chip], n.sibling).wait_send()
            pl.when((chip <= n.l) & n.has_right)(
                lambda: self.copy(mine, self.send_z.at[chip], n.right).wait_send()
            )
            pl.when((chip > n.l) & n.has_left)(
                lambda: self.copy(mine, self.send_z.at[chip], n.left).wait_send()
            )

        pl.when(n.has_left)(lambda: self.copy(n.s, self.send_z.at[n.n_line], n.left).wait_send())


class Scatter:
    def __init__(self, line, part, sib, rcv, send_z, send_c, recv_z, recv_c, m=None):
        self.line, self.m = line, m
        self.part, self.sib, self.rcv = part, sib, rcv
        self.send_z, self.send_c, self.recv_z, self.recv_c = send_z, send_c, recv_z, recv_c

    @staticmethod
    def sems(n_seq):
        n_line = n_seq // 2
        return [
            pltpu.SemaphoreType.DMA((n_line,)),
            pltpu.SemaphoreType.DMA((n_line,)),
            pltpu.SemaphoreType.DMA((n_line + 1,)),
            pltpu.SemaphoreType.DMA((n_line,)),
        ]

    @staticmethod
    def buffers(n_seq, rows, width, *lead):
        n_line = n_seq // 2
        return [
            pltpu.VMEM((*lead, n_line, rows, width), BF16),
            pltpu.VMEM((*lead, n_line + 1, rows, width), BF16),
        ]

    def at(self, index):
        return index if self.m is None else (self.m, index)

    def across(self, chip):
        n = self.line
        return remote(
            self.part.at[self.at(2 * chip + 1 - n.c)],
            self.sib.at[self.at(chip)],
            self.send_c.at[chip],
            self.recv_c.at[chip],
            n.sibling,
        )

    def hop(self, chip, slot, seq):
        n = self.line
        return remote(
            self.part.at[self.at(2 * chip + n.c)],
            self.rcv.at[self.at(slot)],
            self.send_z.at[chip],
            self.recv_z.at[slot],
            seq,
        )

    def begin(self):
        n = self.line

        @pl.loop(0, n.n_line)
        def _(j):
            half = lax.div(j, 2)
            self.across(jnp.where(lax.rem(j, 2) == 0, n.last - half, half)).start()

    def add(self, chip, source):
        mine = self.at(2 * chip + self.line.c)
        self.part[mine] = (self.part[mine].astype(F32) + source.astype(F32)).astype(BF16)

    def step(self, time):
        n = self.line

        @pl.when(n.l <= time)
        def _():
            chip = n.last - time + n.l
            self.across(chip).wait_recv()
            self.add(chip, self.sib[self.at(chip)])

            @pl.when(n.has_left)
            def _():
                self.hop(chip, chip, n.right).wait_recv()
                self.add(chip, self.rcv[self.at(chip)])

            self.hop(chip, chip, n.right).start()

        @pl.when(n.last - n.l <= time)
        def _():
            chip = time - n.last + n.l
            self.across(chip).wait_recv()
            self.add(chip, self.sib[self.at(chip)])

            @pl.when(n.has_right)
            def _():
                self.hop(chip, chip, n.left).wait_recv()
                self.add(chip, self.rcv[self.at(chip)])

            self.hop(chip, jnp.where(chip == n.l - 1, n.n_line, chip), n.left).start()

    def finish(self, out, add=False):
        n = self.line
        mine = 2 * n.l + n.c
        self.across(n.l).wait_recv()
        value = self.part[self.at(mine)].astype(F32) + self.sib[self.at(n.l)].astype(F32)
        out[...] = out[...] + value if add else value

        @pl.when(n.has_left)
        def _():
            self.hop(n.l, n.l, n.right).wait_recv()
            out[...] += self.rcv[self.at(n.l)].astype(F32)

        @pl.when(n.has_right)
        def _():
            self.hop(n.l, n.n_line, n.left).wait_recv()
            out[...] += self.rcv[self.at(n.n_line)].astype(F32)

        @pl.loop(0, n.n_line)
        def _(chip):
            self.across(chip).wait_send()
            pl.when(chip > n.l)(lambda: self.hop(chip, chip, n.right).wait_send())
            pl.when(chip < n.l)(lambda: self.hop(chip, chip, n.left).wait_send())


def norm_back(u, ge):
    r = lax.rsqrt(jnp.mean(u * u, axis=1, keepdims=True) + EPSILON)
    return r * ge - u * (r * r * r * jnp.mean(u * ge, axis=1, keepdims=True))


def spread_work(units, slots, index):
    return (units * index // slots, units * (index + 1) // slots)


class Square:
    def __init__(self):
        self.d = lax.axis_index("dp")
        self.first = self.d + 1 - 2 * lax.rem(self.d, 2)
        self.second = lax.rem(self.d + 2, 4)
        self.across = 3 - self.d


class Spread:
    def __init__(self, line, n_dp, blocks, dst, own_sem, send_z, send_xy, recv):
        self.line, self.n_dp, self.blocks, self.dst = line, n_dp, blocks, dst
        self.own_sem, self.send_z, self.send_xy, self.recv = own_sem, send_z, send_xy, recv
        self.n_seq = 2 * line.n_line
        self.d = lax.axis_index("dp")

    @staticmethod
    def sems(n_seq, n_dp):
        return [
            pltpu.SemaphoreType.DMA((1,)),
            pltpu.SemaphoreType.DMA((n_seq,)),
            pltpu.SemaphoreType.DMA((n_seq, n_dp)),
            pltpu.SemaphoreType.DMA((n_dp, n_seq)),
        ]

    def source(self, j):
        return lax.rem(self.line.s - j + self.n_seq, self.n_seq)

    def hop(self, t):
        n = self.line
        return pltpu.make_async_remote_copy(
            src_ref=self.blocks.at[t],
            dst_ref=self.dst.at[self.d, n.s],
            send_sem=self.send_z.at[t],
            recv_sem=self.recv.at[self.d, n.s],
            device_id={"seq": t},
            device_id_type=MESH,
        )

    def own(self):
        n = self.line
        return pltpu.make_async_copy(self.blocks.at[n.s], self.dst.at[self.d, n.s], self.own_sem.at[0])

    def to_dp(self, src, dst, send, recv, peer):
        return pltpu.make_async_remote_copy(
            src_ref=src, dst_ref=dst, send_sem=send, recv_sem=recv, device_id={"dp": peer}, device_id_type=MESH
        )

    def over(self, source, own=False):
        src = self.blocks.at[self.line.s] if own else self.dst.at[self.d, source]
        peers = [lax.rem(self.d + k, self.n_dp) for k in range(1, self.n_dp)]
        return [
            self.to_dp(src, self.dst.at[self.d, source], self.send_xy.at[source, k], self.recv.at[self.d, source], peer)
            for k, peer in enumerate(peers)
        ]

    def landed(self, d, source):
        block = self.dst.at[d, source]
        return self.to_dp(block, block, self.send_z.at[0], self.recv.at[d, source], d)

    def begin(self, end):
        n = self.line

        @pl.loop(1, end)
        def _(j):
            self.hop(lax.rem(n.s + j, self.n_seq)).start()

        self.own().start()

    def forward_one(self, j, ahead):
        n = self.line

        @pl.when(j < self.n_seq)
        def _():
            pl.when(j + ahead < self.n_seq)(lambda: self.hop(lax.rem(n.s + j + ahead, self.n_seq)).start())
            source = self.source(j)
            self.landed(self.d, source).wait_recv()
            for copy in self.over(source):
                copy.start()

    def forward_own(self):
        for copy in self.over(self.line.s, True):
            copy.start()

    def arrive(self):
        @pl.loop(0, self.n_seq)
        def _(source):
            for k in range(1, self.n_dp):
                self.landed(lax.rem(self.d + k, self.n_dp), source).wait_recv()

        self.own().wait()

    def end(self):
        n = self.line

        @pl.loop(0, self.n_seq)
        def _(j):
            pl.when(j != n.s)(lambda: self.hop(j).wait_send())
            for copy in self.over(j):
                copy.wait_send()


class Copies:
    def __init__(self, n_dp, own, dst, own_sem, send, recv):
        self.n_dp, self.own_ref, self.dst = n_dp, own, dst
        self.own_sem, self.send, self.recv = own_sem, send, recv
        self.d = lax.axis_index("dp")
        self.relay = n_dp == 4
        self.square = Square()
        self.half = own.shape[0] // 2

    @staticmethod
    def sems(n_dp):
        return [
            pltpu.SemaphoreType.DMA((1,)),
            pltpu.SemaphoreType.DMA((n_dp,)),
            pltpu.SemaphoreType.DMA((n_dp + 1,)),
        ]

    def copy(self, src, slot, part, send, recv, peer):
        return pltpu.make_async_remote_copy(
            src_ref=src,
            dst_ref=self.dst.at[slot] if part is None else self.dst.at[slot, part],
            send_sem=self.send.at[send],
            recv_sem=self.recv.at[recv],
            device_id={"dp": peer},
            device_id_type=MESH,
        )

    def direct(self):
        peers = [lax.rem(self.d + k, self.n_dp) for k in range(1, self.n_dp)]
        if self.relay:
            peers = [self.square.first, self.square.second]
        return [self.copy(self.own_ref, self.d, None, k + 1, self.d, peer) for k, peer in enumerate(peers)]

    def landed(self, slot):
        return self.copy(self.dst.at[slot], slot, None, 0, slot, slot)

    def halves(self):
        q = self.square
        low, high = pl.ds(0, self.half), pl.ds(self.half, self.half)
        return (
            self.copy(self.dst.at[q.first, low], q.first, low, 3, q.first, q.second),
            self.copy(self.dst.at[q.second, high], q.second, high, 0, self.n_dp, q.first),
        )

    def own(self):
        return pltpu.make_async_copy(self.own_ref, self.dst.at[self.d], self.own_sem.at[0])

    def begin(self):
        for copy in self.direct():
            copy.start()
        self.own().start()

    def pass_on(self):
        if not self.relay:
            return
        one, two = self.halves()
        self.landed(self.square.first).wait_recv()
        one.start()
        self.landed(self.square.second).wait_recv()
        two.start()

    def end(self):
        for copy in self.direct():
            copy.wait_send()
        if self.relay:
            low, high = pl.ds(0, self.half), pl.ds(self.half, self.half)
            across = self.square.across
            self.copy(self.dst.at[across, low], across, low, 0, across, across).wait_recv()
            self.copy(self.dst.at[across, high], across, high, 0, self.n_dp, across).wait_recv()
            for copy in self.halves():
                copy.wait_send()
        else:
            for k in range(1, self.n_dp):
                self.landed(lax.rem(self.d + k, self.n_dp)).wait_recv()
        self.own().wait()


class Relay:
    def __init__(self, line, n_dp):
        n_seq = 2 * line.n_line
        self.n_dp = n_dp
        self.d = lax.axis_index("dp")
        block = self.d * n_seq + line.s
        self.slot, self.target = lax.rem(block, n_dp), lax.div(block, n_dp)
        block = line.s * n_dp + self.d
        self.owner_d, self.owner_s = lax.div(block, n_seq), lax.rem(block, n_seq)
        self.stays = (self.slot == self.d) & (self.target == line.s)
        self.moves = jnp.logical_not(self.stays)

    def to_relay(self, src, dst, send, recv):
        return pltpu.make_async_remote_copy(
            src_ref=src, dst_ref=dst, send_sem=send, recv_sem=recv,
            device_id=(self.slot, self.target), device_id_type=MESH,
        )

    def to_owner(self, src, dst, send, recv):
        return pltpu.make_async_remote_copy(
            src_ref=src, dst_ref=dst, send_sem=send, recv_sem=recv,
            device_id=(self.owner_d, self.owner_s), device_id_type=MESH,
        )

    def over(self, k, src, dst, send, recv):
        return pltpu.make_async_remote_copy(
            src_ref=src, dst_ref=dst, send_sem=send, recv_sem=recv,
            device_id={"dp": lax.rem(self.d + k, self.n_dp)}, device_id_type=MESH,
        )


class OutRows(Relay):
    def __init__(self, line, n_dp, own, dst, own_sem, send_z, send_xy, recv):
        super().__init__(line, n_dp)
        self.own_ref, self.dst = own, dst
        self.own_sem, self.send_z, self.send_xy, self.recv = own_sem, send_z, send_xy, recv

    @staticmethod
    def sems(n_dp):
        return [
            pltpu.SemaphoreType.DMA((1,)),
            pltpu.SemaphoreType.DMA((1,)),
            pltpu.SemaphoreType.DMA((n_dp,)),
            pltpu.SemaphoreType.DMA((n_dp,)),
        ]

    def hop(self):
        return self.to_relay(self.own_ref, self.dst.at[self.slot], self.send_z.at[0], self.recv.at[self.slot])

    def own(self):
        return pltpu.make_async_copy(self.own_ref, self.dst.at[self.slot], self.own_sem.at[0])

    def copy(self, k):
        return self.over(k, self.dst.at[self.d], self.dst.at[self.d], self.send_xy.at[k], self.recv.at[self.d])

    def landed(self, slot):
        return self.over(1, self.dst.at[slot], self.dst.at[slot], self.send_xy.at[1], self.recv.at[slot])

    def begin(self):
        pl.when(self.stays)(lambda: self.own().start())
        pl.when(self.moves)(lambda: self.hop().start())

    def forward(self):
        pl.when(self.stays)(lambda: self.own().wait())
        pl.when(self.moves)(lambda: self.landed(self.d).wait_recv())
        for k in range(1, self.n_dp):
            self.copy(k).start()

    def arrive(self):
        for k in range(1, self.n_dp):
            self.landed(lax.rem(self.d + k, self.n_dp)).wait_recv()

    def end(self):
        pl.when(self.moves)(lambda: self.hop().wait_send())
        for k in range(1, self.n_dp):
            self.copy(k).wait_send()


class OutSum(Relay):
    def __init__(self, line, n_dp, src, land, final, own_sem, send_xy, recv_xy, send_z, recv_z):
        super().__init__(line, n_dp)
        self.src, self.land, self.final = src, land, final
        self.own_sem, self.send_xy, self.recv_xy, self.send_z, self.recv_z = own_sem, send_xy, recv_xy, send_z, recv_z

    @staticmethod
    def sems(n_dp):
        return [
            pltpu.SemaphoreType.DMA((1,)),
            pltpu.SemaphoreType.DMA((n_dp,)),
            pltpu.SemaphoreType.DMA((n_dp,)),
            pltpu.SemaphoreType.DMA((1,)),
            pltpu.SemaphoreType.DMA((1,)),
        ]

    def copy(self, k):
        return self.over(
            k, self.src.at[lax.rem(self.d + k, self.n_dp)], self.land.at[self.d], self.send_xy.at[k], self.recv_xy.at[self.d]
        )

    def landed(self, owner):
        return self.over(1, self.land.at[owner], self.land.at[owner], self.send_xy.at[1], self.recv_xy.at[owner])

    def own(self):
        return pltpu.make_async_copy(self.src.at[self.d], self.land.at[self.d], self.own_sem.at[0])

    def hop(self):
        return self.to_owner(self.land.at[self.d], self.final, self.send_z.at[0], self.recv_z.at[0])

    def begin(self):
        self.own().start()
        for k in range(1, self.n_dp):
            self.copy(k).start()

    def reduce(self):
        self.own().wait()
        for k in range(1, self.n_dp):
            self.landed(lax.rem(self.d + k, self.n_dp)).wait_recv()
        total = self.land[0].astype(F32)
        for owner in range(1, self.n_dp):
            total = total + self.land[owner].astype(F32)
        total = total.astype(BF16)

        @pl.when(self.stays)
        def _():
            self.final[...] = total

        @pl.when(self.moves)
        def _():
            self.land[self.d] = total
            self.hop().start()

    def end(self):
        pl.when(self.moves)(lambda: self.hop().wait())
        for k in range(1, self.n_dp):
            self.copy(k).wait_send()


class Collect:
    def __init__(self, line, n_dp, src, land, final, own_sem, send_xy, recv_xy, send_z, recv_z):
        self.line, self.n_dp, self.n_seq = line, n_dp, 2 * line.n_line
        self.src, self.land, self.final = src, land, final
        self.own_sem, self.send_xy, self.recv_xy, self.send_z, self.recv_z = own_sem, send_xy, recv_xy, send_z, recv_z
        self.d = lax.axis_index("dp")

    @staticmethod
    def sems(n_seq, n_dp):
        return [
            pltpu.SemaphoreType.DMA((1,)),
            pltpu.SemaphoreType.DMA((n_seq, n_dp)),
            pltpu.SemaphoreType.DMA((n_dp, n_seq)),
            pltpu.SemaphoreType.DMA((n_seq,)),
            pltpu.SemaphoreType.DMA((n_seq,)),
        ]

    def over(self, t, k):
        peer = lax.rem(self.d + k, self.n_dp)
        return pltpu.make_async_remote_copy(
            src_ref=self.src.at[peer, t],
            dst_ref=self.land.at[self.d, t],
            send_sem=self.send_xy.at[t, k],
            recv_sem=self.recv_xy.at[self.d, t],
            device_id={"dp": peer},
            device_id_type=MESH,
        )

    def landed(self, owner, t):
        return pltpu.make_async_remote_copy(
            src_ref=self.land.at[owner, t],
            dst_ref=self.land.at[owner, t],
            send_sem=self.send_xy.at[t, 1],
            recv_sem=self.recv_xy.at[owner, t],
            device_id={"dp": owner},
            device_id_type=MESH,
        )

    def own(self):
        return pltpu.make_async_copy(self.src.at[self.d], self.land.at[self.d], self.own_sem.at[0])

    def hop(self, t, slot):
        return pltpu.make_async_remote_copy(
            src_ref=self.land.at[self.d, t],
            dst_ref=self.final.at[slot],
            send_sem=self.send_z.at[t],
            recv_sem=self.recv_z.at[slot],
            device_id={"seq": t},
            device_id_type=MESH,
        )

    def place(self, j):
        return lax.rem(self.line.s + 1 + j, self.n_seq)

    def begin(self, ahead):
        self.ahead = ahead
        self.own().start()

        @pl.loop(0, ahead)
        def _(j):
            self.send(j)

    def send(self, j):
        for k in range(1, self.n_dp):
            self.over(self.place(j), k).start()

    def reduce(self, first, end):
        if first == 0:
            self.own().wait()

        @pl.loop(first, end)
        def _(j):
            t = self.place(j)
            pl.when(j + self.ahead < self.n_seq)(lambda: self.send(j + self.ahead))
            for k in range(1, self.n_dp):
                self.landed(lax.rem(self.d + k, self.n_dp), t).wait_recv()
            total = self.land[0, t].astype(F32)
            for owner in range(1, self.n_dp):
                total = total + self.land[owner, t].astype(F32)
            total = total.astype(BF16)

            @pl.when(t == self.line.s)
            def _():
                self.final[t] = total

            @pl.when(t != self.line.s)
            def _():
                self.land[self.d, t] = total
                self.hop(t, self.line.s).start()

    def end(self):
        @pl.loop(0, self.n_seq)
        def _(t):
            pl.when(t != self.line.s)(lambda: self.hop(t, t).wait())
            for k in range(1, self.n_dp):
                self.over(t, k).wait_send()


class RowSum:
    def __init__(self, n_dp, src, land, own_sem, send, recv):
        self.n_dp, self.src, self.land = n_dp, src, land
        self.own_sem, self.send, self.recv = own_sem, send, recv
        self.d = lax.axis_index("dp")

    @staticmethod
    def sems(n_dp):
        return [
            pltpu.SemaphoreType.DMA((1,)),
            pltpu.SemaphoreType.DMA((n_dp,)),
            pltpu.SemaphoreType.DMA((n_dp,)),
        ]

    def copy(self, k, slot):
        peer = lax.rem(self.d + k, self.n_dp)
        return pltpu.make_async_remote_copy(
            src_ref=self.src.at[peer],
            dst_ref=self.land.at[slot],
            send_sem=self.send.at[k],
            recv_sem=self.recv.at[slot],
            device_id={"dp": peer},
            device_id_type=MESH,
        )

    def own(self):
        return pltpu.make_async_copy(self.src.at[self.d], self.land.at[self.d], self.own_sem.at[0])

    def begin(self):
        self.own().start()
        for k in range(1, self.n_dp):
            self.copy(k, self.d).start()

    def finish(self, out):
        self.own().wait()
        for k in range(1, self.n_dp):
            self.copy(k, lax.rem(self.d + k, self.n_dp)).wait()
        total = self.land[0].astype(F32)
        for owner in range(1, self.n_dp):
            total = total + self.land[owner].astype(F32)
        out[...] = total


def greet_all(line, n_dp, relay, between=None):
    barrier = pltpu.get_barrier_semaphore()
    n_seq = 2 * line.n_line
    d = lax.axis_index("dp")
    for j in range(1, n_seq):
        pl.semaphore_signal(barrier, 1, device_id={"seq": lax.rem(line.s + j, n_seq)}, device_id_type=MESH)
    for k in range(1, n_dp):
        pl.semaphore_signal(barrier, 1, device_id={"dp": lax.rem(d + k, n_dp)}, device_id_type=MESH)

    if relay is None:
        if between is not None:
            between()
        pl.semaphore_wait(barrier, n_seq + n_dp - 2)
        return

    @pl.when(relay.moves)
    def _():
        for device in ((relay.slot, relay.target), (relay.owner_d, relay.owner_s)):
            pl.semaphore_signal(barrier, 1, device_id=device, device_id_type=MESH)

    if between is not None:
        between()
    pl.semaphore_wait(barrier, n_seq + n_dp - 2 + jnp.where(relay.moves, 2, 0))


def turn(values, lanes_low):
    half = HEAD_DIM // 2
    width = values.shape[-1]
    return jnp.where(
        lanes_low, pltpu.roll(values, width - half, values.ndim - 1), pltpu.roll(values, half, values.ndim - 1)
    )


def low_lanes(shape):
    return lax.rem(lax.broadcasted_iota(jnp.int32, shape, len(shape) - 1), HEAD_DIM) < HEAD_DIM // 2


def head_lanes(kv, h, q_cols):
    wide = jnp.concatenate([kv] * (q_cols // (2 * HEAD_DIM)), axis=1).astype(F32)
    swapped = pltpu.roll(wide, HEAD_DIM, 1)
    here = lax.div(lax.broadcasted_iota(jnp.int32, wide.shape, 1), HEAD_DIM) == h
    key, value = (wide, swapped) if h % 2 == 0 else (swapped, wide)
    key = jnp.where(here, key * (1.0 / math.sqrt(HEAD_DIM)), 0.0).astype(BF16)
    return key, jnp.where(here, value, 0.0).astype(BF16)


def hidden_keys(first, second, prefix, query_axis):
    query, key = (first, second) if query_axis == 0 else (second, first)
    return jnp.where((key <= query) | (key < prefix), 0.0, NEGATIVE)


def bias_shape(length):
    return (length, length) if length <= 2 * QUERY_TILE else (8, 128)


def fill_bias(bias, prefix, query_axis, length):
    if bias.shape[0] != length:
        return
    tile = min(length, QUERY_TILE)

    @pl.loop(0, length // tile)
    def _(i):
        at = pl.ds(pl.multiple_of(i * tile, tile), tile)
        first = i * tile + lax.broadcasted_iota(jnp.int32, (tile, length), 0)
        second = lax.broadcasted_iota(jnp.int32, (tile, length), 1)
        bias[at, :] = hidden_keys(first, second, prefix, query_axis)


def bias_tile(bias, prefix, query_axis, length, tile, i):
    at = pl.ds(pl.multiple_of(i * tile, tile), tile)
    if bias.shape[0] == length:
        return bias[at, :] if query_axis == 0 else bias[:, at]
    shape = (tile, length) if query_axis == 0 else (length, tile)
    first = lax.broadcasted_iota(jnp.int32, shape, 0)
    second = lax.broadcasted_iota(jnp.int32, shape, 1)
    if query_axis == 0:
        first = first + i * tile
    else:
        second = second + i * tile
    return hidden_keys(first, second, prefix, query_axis)


def attention_kernel(
    n_seq, n_dp, prefix_ref, tok_ref, cot_ref, cos_ref, sin_ref, gains_ref,
    w_query_ref, w_key_ref, w_value_ref, w_gate_ref, w_up_ref, wo_own, wd_own,
    hidden_ref, nmlp_ref, q_ref, kv_ref, mixed_ref, normed_hbm, cot_hbm, wqkv_hbm, wo_hbm, wgu_hbm, wd_hbm,
    full, cot, wqkv, wo, acc, part, sib, rcv, qkvb, gub, bias, save_sem, *sems,
):
    n = Line(n_seq)
    rows, width = tok_ref.shape
    micro, length, q_cols = q_ref.shape
    span = rows // micro
    cols_all = wqkv.shape[3]
    pair = 2 * rows

    def prepare():
        tok = tok_ref[...].astype(F32)
        normed = (tok * lax.rsqrt(jnp.mean(tok * tok, axis=1, keepdims=True) + EPSILON)).astype(BF16)
        for m in range(micro):
            full[m, n.s] = normed[m * span : (m + 1) * span]
        cot[n.s] = cot_ref[...]
        for t in range(n_seq):
            head = slice(t // repeat * HEAD_DIM, (t // repeat + 1) * HEAD_DIM)
            qkvb[t, :, :q_cols] = (w_query_ref[:, t * q_cols : (t + 1) * q_cols].astype(F32) * gain_attn).astype(BF16)
            key_value = jnp.concatenate([w_key_ref[:, head], w_value_ref[:, head]], axis=1)
            qkvb[t, :, q_cols:] = (key_value.astype(F32) * gain_attn).astype(BF16)

    sems = list(sems)
    take = lambda count: [sems.pop(0) for _ in range(count)]
    gathers = [Gather(n, full, *take(3), m=m) for m in range(micro)]
    scatters = [Scatter(n, part, sib, rcv, *take(4), m=m) for m in range(micro)]
    gather_cot = Gather(n, cot, *take(3))
    qkv_w = Spread(n, n_dp, qkvb, wqkv, *take(4))
    gu_w = Spread(n, n_dp, gub, wgu_hbm, *take(4))
    out_w = OutRows(n, n_dp, wo_own, wo, *take(4))
    down_w = Copies(n_dp, wd_own, wd_hbm, *take(3))

    repeat = n_seq // KV_HEADS
    ff_block = wd_own.shape[0]
    gain_attn = gains_ref[:, :1]
    gain_mlp = gains_ref[:, 2 * HEAD_DIM : 2 * HEAD_DIM + 1]

    greet_all(n, n_dp, out_w, prepare)
    qkv_w.begin(n_seq)
    gathers[0].begin()
    out_w.begin()
    qkv_w.forward_own()
    for i, ref in enumerate((w_gate_ref, w_up_ref)):
        for owner in range(n_dp):
            for t in range(n_seq):
                cols = slice((owner * n_seq + t) * ff_block, (owner * n_seq + t + 1) * ff_block)
                first = (i * n_dp + owner) * ff_block
                gub[t, :, first : first + ff_block] = (ref[:, cols].astype(F32) * gain_mlp).astype(BF16)

    @pl.loop(1, n_seq)
    def _(j):
        qkv_w.forward_one(j, n_seq)

    out_w.forward()
    gathers[1].begin()
    down_w.begin()
    gu_w.forward_own()
    for j in range(n.n_line):
        gathers[0].visit(n.order(j))
    qkv_w.arrive()
    pltpu.make_async_copy(wqkv, wqkv_hbm, save_sem.at[1]).start()
    gu_w.begin(1 + AHEAD)

    low = low_lanes((span, cols_all))
    half_line = length // span // 2
    heads = q_cols // HEAD_DIM
    q_tile = min(length, QUERY_TILE)

    def project(m):
        @pl.loop(0, 2)
        def _(i):
            some = pl.ds(pl.multiple_of(i * half_line, half_line), half_line)
            value = nn(full[m, some].reshape(half_line * span, width), wqkv[...].reshape(width, cols_all))
            for k in range(half_line):
                at = pl.ds(pl.multiple_of((i * half_line + k) * span, span), span)
                block = value[k * span : (k + 1) * span]
                turned = (block * cos_ref[at, :] + turn(block, low) * sin_ref[at, :]).astype(BF16)
                q_ref[m, at, :] = turned[:, :q_cols]
                kv_ref[m, at, :] = turned[:, q_cols:]

    def attend(m, h):
        key, val = head_lanes(kv_ref[m], h, q_cols)

        @pl.loop(0, length // q_tile)
        def _(i):
            at = pl.ds(pl.multiple_of(i * q_tile, q_tile), q_tile)
            scores = nt(q_ref[m, at, :], key) + bias_tile(bias, prefix_ref[m], 0, length, q_tile, i)
            weights = jnp.exp(scores - jnp.max(scores, axis=1, keepdims=True))
            inverse = 1.0 / jnp.sum(weights, axis=1, keepdims=True)
            mixed = nn((weights * inverse).astype(BF16), val)
            if h == 0:
                acc[at, :] = mixed
            else:
                acc[at, :] += mixed

    sent = 0
    for m in range(micro):
        project(m)
        fill_bias(bias, prefix_ref[m], 0, length)
        for h in range(heads):
            if m + 1 < micro:
                for j in range(*spread_work(n.n_line, heads, h)):
                    gathers[m + 1].visit(n.order(j))
            if m == 1 and h == 0:
                down_w.pass_on()
            attend(m, h)
            done = m * heads + h
            for _ in range(*spread_work(n_seq - 1, micro * heads - 1, done - 1) if done else (0,)):
                sent += 1
                gu_w.forward_one(sent, AHEAD)
        mixed_ref[m] = acc[...].astype(BF16)
        if m == 0:
            out_w.arrive()
            pltpu.make_async_copy(wo, wo_hbm, save_sem.at[2]).start()

        @pl.loop(0, width // TILE)
        def _(w):
            cols = pl.ds(pl.multiple_of(w * TILE, TILE), TILE)
            value = nn(mixed_ref[m], wo[:, :, cols].reshape(q_cols, TILE))
            part[m, :, :, cols] = value.astype(BF16).reshape(n_seq, span, TILE)

        scatters[m].begin()
        if m == 0:
            gather_cot.begin()

    pltpu.make_async_copy(full, normed_hbm, save_sem.at[0]).start()
    gather_cot.visit(n.l)
    for time in range(n.last):
        for scatter in scatters:
            scatter.step(time)
        gather_cot.visit(n.order(time + 1))
    pltpu.make_async_copy(cot, cot_hbm, save_sem.at[3]).start()
    for m in range(micro):
        at = slice(m * span, (m + 1) * span)
        scatters[m].finish(hidden_ref.at[at])
    hidden = hidden_ref[...] + tok_ref[...].astype(F32)
    hidden_ref[...] = hidden
    nmlp_ref[...] = (hidden * lax.rsqrt(jnp.mean(hidden * hidden, axis=1, keepdims=True) + EPSILON)).astype(BF16)
    gu_w.arrive()
    down_w.end()
    pltpu.make_async_copy(full, normed_hbm, save_sem.at[0]).wait()
    pltpu.make_async_copy(wqkv, wqkv_hbm, save_sem.at[1]).wait()
    pltpu.make_async_copy(wo, wo_hbm, save_sem.at[2]).wait()
    pltpu.make_async_copy(cot, cot_hbm, save_sem.at[3]).wait()
    for gather in gathers:
        gather.end()
    gather_cot.end()
    qkv_w.end()
    gu_w.end()
    out_w.end()


def attention_call(prefix, tok, cot, cos, sin, gains, w_query, w_key, w_value, w_gate, w_up, wo_own, wd_own, n_seq, n_dp):
    rows, width = tok.shape
    micro = prefix.shape[0]
    length = cos.shape[0]
    shard = wo_own.shape[0]
    q_cols = width // n_seq
    qkv_cols = q_cols + 2 * HEAD_DIM
    ff_block = wd_own.shape[0]
    gu_cols = 2 * n_dp * ff_block
    every = n_seq * rows
    any_spec = pl.BlockSpec(memory_space=pl.ANY)
    vmem = pl.BlockSpec(memory_space=pltpu.VMEM)
    outs = [
        ((rows, width), F32, vmem),
        ((rows, width), BF16, vmem),
        ((micro, length, q_cols), BF16, vmem),
        ((micro, length, 2 * HEAD_DIM), BF16, vmem),
        ((micro, length, q_cols), BF16, vmem),
        ((micro, n_seq, rows // micro, width), BF16, any_spec),
        ((n_seq, rows, width), BF16, any_spec),
        ((n_dp, n_seq, shard, qkv_cols), BF16, any_spec),
        ((n_dp, shard, width), BF16, any_spec),
        ((n_dp, n_seq, shard, gu_cols), BF16, any_spec),
        ((n_dp, ff_block, width), BF16, any_spec),
    ]
    return pl.pallas_call(
        functools.partial(attention_kernel, n_seq, n_dp),
        out_shape=tuple(jax.ShapeDtypeStruct(s, t) for s, t, _ in outs),
        in_specs=[pl.BlockSpec(memory_space=pltpu.SMEM)] + [vmem] * 10 + [any_spec] * 2,
        out_specs=tuple(spec for _, _, spec in outs),
        scratch_shapes=[
            pltpu.VMEM((micro, n_seq, rows // micro, width), BF16),
            pltpu.VMEM((n_seq, rows, width), BF16),
            pltpu.VMEM((n_dp, n_seq, shard, qkv_cols), BF16),
            pltpu.VMEM((n_dp, shard, width), BF16),
            pltpu.VMEM((length, q_cols), F32),
            pltpu.VMEM((micro, n_seq, rows // micro, width), BF16),
            *Scatter.buffers(n_seq, rows // micro, width, micro),
            pltpu.VMEM((n_seq, shard, qkv_cols), BF16),
            pltpu.VMEM((n_seq, shard, gu_cols), BF16),
            pltpu.VMEM(bias_shape(length), F32),
            pltpu.SemaphoreType.DMA((4,)),
            *Gather.sems(n_seq) * micro,
            *Scatter.sems(n_seq) * micro,
            *Gather.sems(n_seq),
            *Spread.sems(n_seq, n_dp),
            *Spread.sems(n_seq, n_dp),
            *OutRows.sems(n_dp),
            *Copies.sems(n_dp),
        ],
        compiler_params=pltpu.CompilerParams(
            collective_id=2, has_side_effects=True, vmem_limit_bytes=VMEM_LIMIT
        ),
        cost_estimate=pl.CostEstimate(flops=10**10, bytes_accessed=40 << 20, transcendentals=0),
        name="attention",
    )(prefix, tok, cot, cos, sin, gains, w_query, w_key, w_value, w_gate, w_up, wo_own, wd_own)


def mlp_kernel(
    n_seq, n_dp, x_ref, hidden_ref, cot_hbm, wgu_hbm, wd_hbm,
    branch_ref, gh_ref, pout_hbm, dgu_hbm, dwd_ref,
    full, cot, wgu, wd, act, gg, gu, part, sib, rcv, dwd, land, total, stage_gu, stage_rows, load_sem, gu_sem, rows_sem, *sems,
):
    n = Line(n_seq)
    rows, width = x_ref.shape
    ff = wd.shape[0]
    pair = 2 * rows
    loads = [
        pltpu.make_async_copy(src, dst, load_sem.at[i])
        for i, (src, dst) in enumerate(
            [(wgu_hbm, wgu), (cot_hbm, cot), (wd_hbm, wd)]
        )
    ]

    def prepare():
        for load in loads:
            load.start()
        full[n.s] = x_ref[...]

    greet_all(n, n_dp, None, prepare)
    gather = Gather(n, full, *sems[:3])
    scatter = Scatter(n, part, sib, rcv, *sems[3:7])
    down = RowSum(n_dp, dwd, land, *sems[7:10])
    gather.begin()
    for load in loads:
        load.wait()

    @pl.loop(0, n.n_line)
    def _(j):
        chip = n.order(j)
        near = 2 * jnp.minimum(n.l, n.last - n.l)
        odd = lax.rem(j, 2) == 1
        pl.when((j == 0) | odd | (j > near))(lambda: gather.visit(chip))
        pl.when(odd & (j < near))(lambda: gather.visit(n.order(j + 1)))
        at = pl.ds(pl.multiple_of(chip * pair, pair), pair)
        two = pl.ds(pl.multiple_of(2 * chip, 2), 2)

        @pl.loop(0, ff // TILE)
        def _(f):
            cols = pl.ds(pl.multiple_of(f * TILE, TILE), TILE)
            x = full[two].reshape(pair, width)
            gate = nn(x, wgu[:, cols])
            up = nn(x, wgu[:, pl.ds(pl.multiple_of(ff + f * TILE, TILE), TILE)])
            grad = nt(cot[two].reshape(pair, width), wd[cols, :])
            sig = jax.nn.sigmoid(gate)
            silu = gate * sig
            act[at, cols] = (silu * up).astype(BF16)
            gg[at, cols] = (grad * up * (sig + silu * (1.0 - sig))).astype(BF16)
            gu[at, cols] = (grad * silu).astype(BF16)

        @pl.loop(0, width // TILE)
        def _(w):
            cols = pl.ds(pl.multiple_of(w * TILE, TILE), TILE)
            value = nt(gg[at, :], wgu[cols, :ff]) + nt(gu[at, :], wgu[cols, ff:])
            part[two, :, cols] = value.astype(BF16).reshape(2, rows, TILE)

    scatter.begin()
    scatter.step(0)
    owners = TILE // dwd.shape[1]

    def down_grad(f):
        cols = pl.ds(pl.multiple_of(f * TILE, TILE), TILE)
        at = pl.ds(f * owners, owners)
        for w in range(0, width, 2 * TILE):
            span = cot[:, :, w : w + 2 * TILE].reshape(n_seq * rows, 2 * TILE)
            value = tn(act[:, cols], span).astype(BF16)
            dwd[at, :, w : w + 2 * TILE] = value.reshape(owners, dwd.shape[1], 2 * TILE)

    if owners == 1:

        @pl.loop(1, n_dp + 1)
        def _(k):
            down_grad(lax.rem(down.d + k, n_dp))
            pl.when(k < n_dp)(lambda: down.copy(k, down.d).start())

        down.own().start()
    else:
        pl.loop(0, ff // TILE)(down_grad)
        down.begin()

    def gate_up_grads(first, end):
        @pl.loop(first, end)
        def _(w):
            slot = lax.rem(w, 2)
            cols = pl.ds(pl.multiple_of(w * TILE, TILE), TILE)
            x = full[:, :, cols].reshape(n_seq * rows, TILE)
            copy = pltpu.make_async_copy(stage_gu.at[slot], dgu_hbm.at[cols, :], gu_sem.at[slot])
            pl.when(w >= 2)(lambda: copy.wait())
            stage_gu[slot, :, :ff] = tn(x, gg[...]).astype(BF16)
            stage_gu[slot, :, ff:] = tn(x, gu[...]).astype(BF16)
            copy.start()

    def out_parts(first, end):
        @pl.loop(first, end)
        def _(chip):
            slot = lax.rem(chip, 2)
            at = pl.ds(pl.multiple_of(chip * pair, pair), pair)
            two = pl.ds(pl.multiple_of(2 * chip, 2), 2)
            copies = [
                pltpu.make_async_copy(
                    stage_rows.at[slot, pl.ds(i * rows, rows)], pout_hbm.at[2 * chip + i], rows_sem.at[slot + 2 * i]
                )
                for i in range(2)
            ]

            @pl.when(chip >= 2)
            def _():
                for copy in copies:
                    copy.wait()

            for w in range(0, width, 2 * TILE):
                stage_rows[slot, :pair, w : w + 2 * TILE] = nn(act[at, :], wd[:, w : w + 2 * TILE]).astype(BF16)
            for copy in copies:
                copy.start()

    def drain_out():
        for slot in range(2):
            for i in range(2):
                pltpu.make_async_copy(
                    stage_rows.at[slot, pl.ds(i * rows, rows)], pout_hbm.at[i], rows_sem.at[slot + 2 * i]
                ).wait()

    for time in range(n.last):
        if time > 0:
            scatter.step(time)
        if time == 0:
            out_parts(0, n.n_line)
        gate_up_grads(*spread_work(width // TILE, n.last, time))
    scatter.finish(total)
    grad_hidden = cot[n.s].astype(F32) + norm_back(hidden_ref[...], total[...])
    gh_ref[...] = grad_hidden
    branch_ref[...] = grad_hidden.astype(BF16)
    drain_out()
    for slot in range(2):
        pltpu.make_async_copy(stage_gu.at[slot], dgu_hbm.at[pl.ds(0, TILE), :], gu_sem.at[slot]).wait()
    down.finish(dwd_ref)
    gather.end()


def mlp_call(x, hidden, cot, wgu, wd, n_seq, n_dp):
    rows, width = x.shape
    ff = wd.shape[0]
    every = n_seq * rows
    any_spec = pl.BlockSpec(memory_space=pl.ANY)
    vmem = pl.BlockSpec(memory_space=pltpu.VMEM)
    return pl.pallas_call(
        functools.partial(mlp_kernel, n_seq, n_dp),
        out_shape=(
            jax.ShapeDtypeStruct((rows, width), BF16),
            jax.ShapeDtypeStruct((rows, width), F32),
            jax.ShapeDtypeStruct((n_seq, rows, width), BF16),
            jax.ShapeDtypeStruct((width, 2 * ff), BF16),
            jax.ShapeDtypeStruct((ff // n_dp, width), F32),
        ),
        in_specs=[vmem] * 2 + [any_spec] * 3,
        out_specs=(vmem, vmem, any_spec, any_spec, vmem),
        scratch_shapes=[
            pltpu.VMEM((n_seq, rows, width), BF16),
            pltpu.VMEM((n_seq, rows, width), BF16),
            pltpu.VMEM((width, 2 * ff), BF16),
            pltpu.VMEM((ff, width), BF16),
            pltpu.VMEM((every, ff), BF16),
            pltpu.VMEM((every, ff), BF16),
            pltpu.VMEM((every, ff), BF16),
            pltpu.VMEM((n_seq, rows, width), BF16),
            *Scatter.buffers(n_seq, rows, width),
            pltpu.VMEM((n_dp, ff // n_dp, width), BF16),
            pltpu.VMEM((n_dp, ff // n_dp, width), BF16),
            pltpu.VMEM((rows, width), F32),
            pltpu.VMEM((2, TILE, 2 * ff), BF16),
            pltpu.VMEM((2, TILE, width), BF16),
            pltpu.SemaphoreType.DMA((3,)),
            pltpu.SemaphoreType.DMA((2,)),
            pltpu.SemaphoreType.DMA((4,)),
            *Gather.sems(n_seq),
            *Scatter.sems(n_seq),
            *RowSum.sems(n_dp),
        ],
        compiler_params=pltpu.CompilerParams(
            collective_id=1, has_side_effects=True, vmem_limit_bytes=VMEM_LIMIT
        ),
        cost_estimate=pl.CostEstimate(flops=18 * every * width * ff, bytes_accessed=40 << 20, transcendentals=0),
        name="mlp",
    )(x, hidden, cot, wgu, wd)


def backward_kernel(
    n_seq, n_dp, prefix_ref, branch_ref, tok_ref, q_ref, kv_ref, mixed_ref, cos_ref, sin_ref, gains_ref,
    w_query_ref, w_key_ref, w_value_ref, gh_hbm, hidden_hbm, pout_hbm, normed_hbm, wqkv_hbm, wo_hbm, dgu_hbm,
    out_ref, in_ref, dgain_ref, dq_ref, dk_ref, dv_ref, dwo_out, dgate_ref, dup_ref,
    full, tiles, wqkv, wo, gm, acc_q, acc_k, acc_v, bias, gqkv, part, sib, rcv, sib_o, rcv_o,
    land_gu, final_gu, dqkv, land_qkv, final_qkv, dwo, land_o, final_o, total, load_sem, tile_sem, *sems,
):
    n = Line(n_seq)
    rows, width = branch_ref.shape
    micro, length, q_cols = q_ref.shape
    span = rows // micro
    pair = 2 * rows
    loads = [
        pltpu.make_async_copy(src, dst, load_sem.at[i])
        for i, (src, dst) in enumerate(
            [(pout_hbm, part), (wo_hbm, wo), (wqkv_hbm, wqkv), (hidden_hbm, total), (gh_hbm, in_ref)]
        )
    ]

    def prepare():
        for load in loads:
            load.start()
        for m in range(micro):
            full[m, n.s] = branch_ref[m * span : (m + 1) * span, :]

    sems = list(sems)
    take = lambda count: [sems.pop(0) for _ in range(count)]
    gathers = [Gather(n, full, *take(3), m=m) for m in range(micro)]
    scatter = Scatter(n, part, sib, rcv, *take(4))
    scatter_out = Scatter(n, part, sib_o, rcv_o, *take(4))
    gu_sum = Collect(n, n_dp, dgu_hbm, land_gu, final_gu, *take(5))
    qkv_sum = Collect(n, n_dp, dqkv, land_qkv, final_qkv, *take(5))
    out_sum = OutSum(n, n_dp, dwo, land_o, final_o, *take(5))
    greet_all(n, n_dp, out_sum, prepare)
    gathers[0].begin()
    gu_sum.begin(3)
    loads[0].wait()
    loads[1].wait()
    late = n_seq * 5 // 8
    scatter_out.begin()
    gathers[1].begin()
    for j in range(n.n_line):
        gathers[0].visit(n.order(j))
    loads[2].wait()

    heads = q_cols // HEAD_DIM
    scale = 1.0 / math.sqrt(HEAD_DIM)
    q_tile = min(length, QUERY_TILE)
    low = low_lanes((length, q_cols + 2 * HEAD_DIM))
    here = lax.div(lax.broadcasted_iota(jnp.int32, (length, q_cols), 1), HEAD_DIM)

    def attend_back(m, h):
        key, val = head_lanes(kv_ref[m], h, q_cols)

        @pl.loop(0, length // q_tile)
        def _(i):
            at = pl.ds(pl.multiple_of(i * q_tile, q_tile), q_tile)
            query, grad = q_ref[m, at, :], gm[m, at, :]
            scores = nt(key, query) + bias_tile(bias, prefix_ref[m], 1, length, q_tile, i)
            weights = jnp.exp(scores - jnp.max(scores, axis=0, keepdims=True))
            probs = weights * (1.0 / jnp.sum(weights, axis=0, keepdims=True))
            grad_probs = nt(val, grad)
            delta = jnp.sum(probs * grad_probs, axis=0, keepdims=True)
            grad_scores = (probs * (grad_probs - delta)).astype(BF16)
            acc_q[at, :] += tn(grad_scores, key)
            acc_k[...] += jnp.where(here == h, nn(grad_scores, query), 0.0)
            acc_v[...] += jnp.where(here == h, nn(probs.astype(BF16), grad), 0.0)

    shard = dwo.shape[1]

    def out_grads():

        @pl.loop(0, width // TILE)
        def _(w):
            cols = pl.ds(pl.multiple_of(w * TILE, TILE), TILE)
            d_out = jnp.zeros((q_cols, TILE), F32)
            for m in range(micro):
                d_out = d_out + tn(mixed_ref[m], full[m, :, :, cols].reshape(length, TILE))
            dwo[:, :, cols] = d_out.astype(BF16).reshape(n_dp, shard, TILE)

        out_sum.begin()

    for m in range(micro):
        gm[m] = nt(full[m].reshape(length, width), wo[...].reshape(q_cols, width)).astype(BF16)
        fill_bias(bias, prefix_ref[m], 1, length)
        for ref in (acc_q, acc_k, acc_v):
            ref[...] = jnp.zeros_like(ref)
        for h in range(heads):
            if m + 1 < micro:
                for j in range(*spread_work(n.n_line, heads, h)):
                    gathers[m + 1].visit(n.order(j))
            if m == 0:
                for time in range(*spread_work(n.last, heads, h)):
                    scatter_out.step(time)
            if m == 1 and h == 0:
                out_grads()
            for j in range(*spread_work(late, micro * heads, m * heads + h)):
                gu_sum.reduce(j, j + 1)
            attend_back(m, h)

        def fold(ref):
            total = ref[:, : 2 * HEAD_DIM]
            for w in range(2 * HEAD_DIM, q_cols, 2 * HEAD_DIM):
                total = total + ref[:, w : w + 2 * HEAD_DIM]
            return total + pltpu.roll(total, HEAD_DIM, 1)

        first = lax.broadcasted_iota(jnp.int32, (length, 2 * HEAD_DIM), 1) < HEAD_DIM
        grads = jnp.concatenate([acc_q[...], jnp.where(first, fold(acc_k) * scale, fold(acc_v))], axis=1)
        gqkv[m] = (grads * cos_ref[...] - turn(grads, low) * sin_ref[...]).astype(BF16)

    loads[3].wait()
    scatter_out.finish(total, True)
    out_ref[...] = total[...].astype(BF16)
    for m in range(micro):

        @pl.loop(0, width // TILE)
        def _(w):
            at = pl.ds(pl.multiple_of(w * TILE, TILE), TILE)
            value = nt(gqkv[m], wqkv[at, :])
            part[:, m * span : (m + 1) * span, at] = value.astype(BF16).reshape(n_seq, span, TILE)

    scatter.begin()
    scatter.step(0)

    half = n_seq // 2
    depth = half * shard

    def fetch(w):
        cols = pl.ds(pl.multiple_of(w * depth, depth), depth)
        slot = lax.rem(w, 2)
        return pltpu.make_async_copy(normed_hbm.at[:, :, :, cols], tiles.at[slot], tile_sem.at[slot])

    fetch(jnp.int32(0)).start()

    @pl.loop(0, n_dp * 2)
    def _(w):
        pl.when(w + 1 < n_dp * 2)(lambda: fetch(w + 1).start())
        fetch(w).wait()
        slot = lax.rem(w, 2)
        d_qkv = jnp.zeros((depth, q_cols + 2 * HEAD_DIM), F32)
        for m in range(micro):
            d_qkv = d_qkv + tn(tiles[slot, m].reshape(length, depth), gqkv[m])
        at = pl.ds(pl.multiple_of(lax.rem(w, 2) * half, half), half)
        dqkv[lax.div(w, 2), at] = d_qkv.astype(BF16).reshape(half, shard, q_cols + 2 * HEAD_DIM)

    qkv_sum.begin(n_seq)
    out_sum.reduce()
    for time in range(n.last):
        if time > 0:
            scatter.step(time)
        first, end = spread_work(n_seq - late, n.last, time)
        gu_sum.reduce(late + first, late + end)
    qkv_sum.reduce(0, n_seq)
    scatter.finish(total)
    loads[4].wait()
    in_ref[...] += norm_back(tok_ref[...].astype(F32), total[...])
    gu_sum.end()
    ff_block = dgate_ref.shape[1] // (n_dp * n_seq)
    gain_attn = gains_ref[:, :1]
    for i, ref in enumerate((dgate_ref, dup_ref)):
        for owner in range(n_dp):
            for t in range(n_seq):
                cols = slice((owner * n_seq + t) * ff_block, (owner * n_seq + t + 1) * ff_block)
                first = (i * n_dp + owner) * ff_block
                ref[:, cols] = final_gu[t, :, first : first + ff_block]
    qkv_sum.end()
    repeat = n_seq // KV_HEADS
    dots = jnp.zeros((shard, 1), F32)
    for t in range(n_seq):
        cols = slice(t * q_cols, (t + 1) * q_cols)
        value = final_qkv[t, :, :q_cols].astype(F32)
        dots = dots + jnp.sum(value * w_query_ref[:, cols].astype(F32), axis=1, keepdims=True)
        dq_ref[:, cols] = value * gain_attn
    for g in range(KV_HEADS):
        cols = slice(g * HEAD_DIM, (g + 1) * HEAD_DIM)
        for i, (ref, w_ref) in enumerate(((dk_ref, w_key_ref), (dv_ref, w_value_ref))):
            lanes = slice(q_cols + i * HEAD_DIM, q_cols + (i + 1) * HEAD_DIM)
            value = final_qkv[g * repeat, :, lanes].astype(F32)
            for t in range(g * repeat + 1, (g + 1) * repeat):
                value = value + final_qkv[t, :, lanes].astype(F32)
            dots = dots + jnp.sum(value * w_ref[:, cols].astype(F32), axis=1, keepdims=True)
            ref[:, cols] = value * gain_attn
    dgain_ref[...] = dots * jnp.ones((shard, 2 * HEAD_DIM), F32)
    out_sum.end()
    dwo_out[...] = final_o[...].astype(F32)
    for gather in gathers:
        gather.end()


def backward_call(
    prefix, branch, tok, q, kv, mixed, cos, sin, gains, w_query, w_key, w_value,
    gh, hidden, pout, normed, wqkv, wo, dgu,
):
    rows, width = branch.shape
    n_dp, n_seq, shard, gu_cols = dgu.shape
    ff = gu_cols // 2 * n_seq
    micro, length, q_cols = q.shape
    qkv_cols = q_cols + 2 * HEAD_DIM
    any_spec = pl.BlockSpec(memory_space=pl.ANY)
    vmem = pl.BlockSpec(memory_space=pltpu.VMEM)
    line_rows = pltpu.VMEM((n_seq, rows, width), BF16)
    return pl.pallas_call(
        functools.partial(backward_kernel, n_seq, n_dp),
        out_shape=(
            jax.ShapeDtypeStruct((rows, width), BF16),
            jax.ShapeDtypeStruct((rows, width), F32),
            jax.ShapeDtypeStruct((shard, 2 * HEAD_DIM), F32),
            *(jax.ShapeDtypeStruct(w.shape, F32) for w in (w_query, w_key, w_value)),
            jax.ShapeDtypeStruct((shard, width), F32),
            jax.ShapeDtypeStruct((shard, ff), BF16),
            jax.ShapeDtypeStruct((shard, ff), BF16),
        ),
        in_specs=[pl.BlockSpec(memory_space=pltpu.SMEM)] + [vmem] * 11 + [any_spec] * 7,
        out_specs=(vmem,) * 9,
        scratch_shapes=[
            pltpu.VMEM((micro, n_seq, rows // micro, width), BF16),
            pltpu.VMEM((2, micro, n_seq, rows // micro, n_seq // 2 * shard), BF16),
            pltpu.VMEM((width, qkv_cols), BF16),
            pltpu.VMEM(wo.shape, BF16),
            pltpu.VMEM((micro, length, q_cols), BF16),
            pltpu.VMEM((length, q_cols), F32),
            pltpu.VMEM((length, q_cols), F32),
            pltpu.VMEM((length, q_cols), F32),
            pltpu.VMEM(bias_shape(length), F32),
            pltpu.VMEM((micro, length, qkv_cols), BF16),
            line_rows,
            *Scatter.buffers(n_seq, rows, width),
            *Scatter.buffers(n_seq, rows, width),
            pltpu.VMEM((n_dp, n_seq, shard, gu_cols), BF16),
            pltpu.VMEM((n_seq, shard, gu_cols), BF16),
            pltpu.VMEM((n_dp, n_seq, shard, qkv_cols), BF16),
            pltpu.VMEM((n_dp, n_seq, shard, qkv_cols), BF16),
            pltpu.VMEM((n_seq, shard, qkv_cols), BF16),
            pltpu.VMEM((n_dp, shard, width), BF16),
            pltpu.VMEM((n_dp, shard, width), BF16),
            pltpu.VMEM((shard, width), BF16),
            pltpu.VMEM((rows, width), F32),
            pltpu.SemaphoreType.DMA((5,)),
            pltpu.SemaphoreType.DMA((2,)),
            *Gather.sems(n_seq) * micro,
            *Scatter.sems(n_seq),
            *Scatter.sems(n_seq),
            *Collect.sems(n_seq, n_dp),
            *Collect.sems(n_seq, n_dp),
            *OutSum.sems(n_dp),
        ],
        compiler_params=pltpu.CompilerParams(
            collective_id=3, has_side_effects=True, vmem_limit_bytes=VMEM_LIMIT
        ),
        cost_estimate=pl.CostEstimate(flops=10**10, bytes_accessed=40 << 20, transcendentals=0),
        name="backward",
    )(
        prefix, branch, tok, q, kv, mixed, cos, sin, gains, w_query, w_key, w_value,
        gh, hidden, pout, normed, wqkv, wo, dgu,
    )


def body(
    tokens, cotangent, prefix_len, attn_gain, w_query, w_key, w_value, w_out, mlp_gain, w_gate, w_up, w_down
):
    n_dp = lax.axis_size("dp")
    n_seq = lax.axis_size("seq")
    micro, span, width = tokens.shape
    shard = w_query.shape[0]
    rows = micro * span
    cos, sin = rope_tables(span * n_seq, HEADS // n_seq * HEAD_DIM)
    gains = jnp.concatenate(
        [jnp.broadcast_to(g.astype(F32)[:, None], (shard, 2 * HEAD_DIM)) for g in (attn_gain, mlp_gain)], axis=1
    )
    tok = tokens.reshape(rows, width)
    cot = cotangent.reshape(rows, width)
    hidden, normed_mlp, q, kv, mixed, normed, cot_all, wqkv, wo, wgu, wd = attention_call(
        prefix_len, tok, cot, cos, sin, gains, w_query, w_key, w_value, w_gate, w_up, w_out, w_down, n_seq, n_dp
    )
    branch, grad_hidden, out_part, dgu, w_down_grad = mlp_call(
        normed_mlp, hidden, cot_all, wgu.reshape(width, -1), wd.reshape(-1, width), n_seq, n_dp
    )
    block_out, input_grad, attn_gain_grad, *w_grads, w_out_grad, d_gate, d_up = backward_call(
        prefix_len, branch, tok, q, kv, mixed, cos, sin, gains, w_query, w_key, w_value,
        grad_hidden, hidden, out_part, normed, wqkv.reshape(width, -1), wo.reshape(-1, width), dgu.reshape(n_dp, n_seq, shard, -1),
    )
    mlp_gain_grad = jnp.sum(d_gate.astype(F32) * w_gate.astype(F32), axis=1)
    mlp_gain_grad = mlp_gain_grad + jnp.sum(d_up.astype(F32) * w_up.astype(F32), axis=1)
    gain_column = mlp_gain.astype(F32)[:, None]
    return (
        block_out.reshape(micro, span, width),
        input_grad.reshape(micro, span, width),
        attn_gain_grad[:, 0],
        *w_grads,
        w_out_grad,
        mlp_gain_grad,
        d_gate.astype(F32) * gain_column,
        d_up.astype(F32) * gain_column,
        w_down_grad,
    )


def solution(mesh):
    rows = P("dp", "seq", None)
    vec = P(("dp", "seq"))
    mat = P(("dp", "seq"), None)
    in_specs = (rows, rows, P("dp"), vec, mat, mat, mat, mat, vec, mat, mat, mat)
    out_specs = (rows, rows, vec, mat, mat, mat, mat, vec, mat, mat, mat)
    return jax.shard_map(body, mesh=mesh, in_specs=in_specs, out_specs=out_specs, check_vma=False)
```

```python
import functools
import math

import jax
import jax.numpy as jnp
import numpy as np
from jax import lax
from jax.experimental import pallas as pl
from jax.experimental.pallas import tpu as pltpu
from jax.sharding import PartitionSpec as P

HEADS = 32
KV_HEADS = 8
HEAD_DIM = 64
EPSILON = 1e-05
THETA = 500000.0
NEGATIVE = -1e30
BF16 = jnp.bfloat16
F32 = jnp.float32
MESH = pl.DeviceIdType.MESH
TILE = 256
QUERY_TILE = 256
AHEAD = 4
VMEM_LIMIT = 61 << 20


def rope_tables(length, q_cols):
    half = HEAD_DIM // 2
    f32 = np.float32
    index_half = np.arange(half, dtype=f32)
    inverse = np.power(f32(THETA), f32(-2.0) * index_half / f32(HEAD_DIM)).astype(f32)
    wavelength = (f32(2.0 * math.pi) / inverse).astype(f32)
    smooth = ((f32(8192.0) / wavelength - f32(1.0)) / f32(3.0)).astype(f32)
    blended = ((f32(1.0) - smooth) * inverse / f32(32.0) + smooth * inverse).astype(f32)
    inverse = np.where(
        wavelength < 2048.0, inverse, np.where(wavelength > 8192.0, inverse / f32(32.0), blended)
    ).astype(f32)
    angles = (np.arange(length, dtype=f32)[:, None] * inverse[None, :]).astype(f32)
    cos, sin = np.cos(angles).astype(f32), np.sin(angles).astype(f32)
    count = q_cols // HEAD_DIM + 1
    ones, zeros = np.ones((length, HEAD_DIM), f32), np.zeros((length, HEAD_DIM), f32)
    cos = np.concatenate([cos, cos] * count + [ones], axis=1)
    sin = np.concatenate([-sin, sin] * count + [zeros], axis=1)
    return jnp.asarray(cos), jnp.asarray(sin)


def nn(a, b):
    return jnp.dot(a, b, preferred_element_type=F32)


def tn(a, b):
    return lax.dot_general(a, b, (((0,), (0,)), ((), ())), preferred_element_type=F32)


def nt(a, b):
    return lax.dot_general(a, b, (((1,), (1,)), ((), ())), preferred_element_type=F32)


class Line:
    def __init__(self, n_seq):
        self.n_line = n_seq // 2
        self.last = self.n_line - 1
        self.s = lax.axis_index("seq")
        self.c = lax.rem(self.s, 2)
        self.l = lax.div(self.s, 2)
        self.sibling = self.s + 1 - 2 * self.c
        self.right = jnp.minimum(self.s + 2, n_seq - 2 + self.c)
        self.left = jnp.maximum(self.s - 2, self.c)
        self.has_right = self.l < self.last
        self.has_left = self.l > 0

    def greet(self, n_dp):
        barrier = pltpu.get_barrier_semaphore()
        d = lax.axis_index("dp")
        for k in range(1, n_dp):
            pl.semaphore_signal(barrier, 1, device_id={"dp": lax.rem(d + k, n_dp)}, device_id_type=MESH)
        pl.semaphore_signal(barrier, 1, device_id={"seq": self.sibling}, device_id_type=MESH)

        @pl.when(self.has_right)
        def _():
            pl.semaphore_signal(barrier, 1, device_id={"seq": self.right}, device_id_type=MESH)

        @pl.when(self.has_left)
        def _():
            pl.semaphore_signal(barrier, 1, device_id={"seq": self.left}, device_id_type=MESH)

        pl.semaphore_wait(barrier, n_dp - 1 + jnp.where(self.has_right & self.has_left, 3, 2))

    def order(self, j):
        near = jnp.minimum(self.l, self.last - self.l)
        half = lax.div(j + 1, 2)
        both = jnp.where(lax.rem(j, 2) == 1, self.l - half, self.l + half)
        far = jnp.where(self.l <= self.last - self.l, j, self.last - j)
        return jnp.where(j <= 2 * near, both, far)


def remote(src, dst, send, recv, seq):
    return pltpu.make_async_remote_copy(
        src_ref=src, dst_ref=dst, send_sem=send, recv_sem=recv, device_id={"seq": seq}, device_id_type=MESH
    )


class Gather:
    def __init__(self, line, full, send_z, send_c, recv, m=None):
        self.m = m
        self.line, self.full, self.send_z, self.send_c, self.recv = line, full, send_z, send_c, recv

    @staticmethod
    def sems(n_seq):
        n_line = n_seq // 2
        return [
            pltpu.SemaphoreType.DMA((n_line + 1,)),
            pltpu.SemaphoreType.DMA((n_line,)),
            pltpu.SemaphoreType.DMA((n_seq,)),
        ]

    def copy(self, index, send, seq):
        chunk = self.full.at[index] if self.m is None else self.full.at[self.m, index]
        return remote(chunk, chunk, send, self.recv.at[index], seq)

    def begin(self):
        n = self.line
        pl.when(n.has_right)(lambda: self.copy(n.s, self.send_z.at[n.l], n.right).start())
        pl.when(n.has_left)(lambda: self.copy(n.s, self.send_z.at[n.n_line], n.left).start())
        self.copy(n.s, self.send_c.at[n.l], n.sibling).start()

    def visit(self, chip):
        n = self.line
        mine = 2 * chip + n.c

        @pl.when(chip != n.l)
        def _():
            self.copy(mine, self.send_c.at[chip], n.sibling).wait_recv()
            pl.when((chip < n.l) & n.has_right)(
                lambda: self.copy(mine, self.send_z.at[chip], n.right).start()
            )
            pl.when((chip > n.l) & n.has_left)(
                lambda: self.copy(mine, self.send_z.at[chip], n.left).start()
            )
            self.copy(mine, self.send_c.at[chip], n.sibling).start()

        self.copy(2 * chip + 1 - n.c, self.send_c.at[chip], n.sibling).wait_recv()

    def end(self):
        n = self.line

        @pl.loop(0, n.n_line)
        def _(chip):
            mine = 2 * chip + n.c
            self.copy(mine, self.send_c.at[chip], n.sibling).wait_send()
            pl.when((chip <= n.l) & n.has_right)(
                lambda: self.copy(mine, self.send_z.at[chip], n.right).wait_send()
            )
            pl.when((chip > n.l) & n.has_left)(
                lambda: self.copy(mine, self.send_z.at[chip], n.left).wait_send()
            )

        pl.when(n.has_left)(lambda: self.copy(n.s, self.send_z.at[n.n_line], n.left).wait_send())


class Scatter:
    def __init__(self, line, part, sib, rcv, send_z, send_c, recv_z, recv_c, m=None):
        self.line, self.m = line, m
        self.part, self.sib, self.rcv = part, sib, rcv
        self.send_z, self.send_c, self.recv_z, self.recv_c = send_z, send_c, recv_z, recv_c

    @staticmethod
    def sems(n_seq):
        n_line = n_seq // 2
        return [
            pltpu.SemaphoreType.DMA((n_line,)),
            pltpu.SemaphoreType.DMA((n_line,)),
            pltpu.SemaphoreType.DMA((n_line + 1,)),
            pltpu.SemaphoreType.DMA((n_line,)),
        ]

    @staticmethod
    def buffers(n_seq, rows, width, *lead):
        n_line = n_seq // 2
        return [
            pltpu.VMEM((*lead, n_line, rows, width), BF16),
            pltpu.VMEM((*lead, n_line + 1, rows, width), BF16),
        ]

    def at(self, index):
        return index if self.m is None else (self.m, index)

    def across(self, chip):
        n = self.line
        return remote(
            self.part.at[self.at(2 * chip + 1 - n.c)],
            self.sib.at[self.at(chip)],
            self.send_c.at[chip],
            self.recv_c.at[chip],
            n.sibling,
        )

    def hop(self, chip, slot, seq):
        n = self.line
        return remote(
            self.part.at[self.at(2 * chip + n.c)],
            self.rcv.at[self.at(slot)],
            self.send_z.at[chip],
            self.recv_z.at[slot],
            seq,
        )

    def begin(self):
        n = self.line

        @pl.loop(0, n.n_line)
        def _(j):
            half = lax.div(j, 2)
            self.across(jnp.where(lax.rem(j, 2) == 0, n.last - half, half)).start()

    def add(self, chip, source):
        mine = self.at(2 * chip + self.line.c)
        self.part[mine] = (self.part[mine].astype(F32) + source.astype(F32)).astype(BF16)

    def step(self, time):
        n = self.line

        @pl.when(n.l <= time)
        def _():
            chip = n.last - time + n.l
            self.across(chip).wait_recv()
            self.add(chip, self.sib[self.at(chip)])

            @pl.when(n.has_left)
            def _():
                self.hop(chip, chip, n.right).wait_recv()
                self.add(chip, self.rcv[self.at(chip)])

            self.hop(chip, chip, n.right).start()

        @pl.when(n.last - n.l <= time)
        def _():
            chip = time - n.last + n.l
            self.across(chip).wait_recv()
            self.add(chip, self.sib[self.at(chip)])

            @pl.when(n.has_right)
            def _():
                self.hop(chip, chip, n.left).wait_recv()
                self.add(chip, self.rcv[self.at(chip)])

            self.hop(chip, jnp.where(chip == n.l - 1, n.n_line, chip), n.left).start()

    def finish(self, out, add=False):
        n = self.line
        mine = 2 * n.l + n.c
        self.across(n.l).wait_recv()
        value = self.part[self.at(mine)].astype(F32) + self.sib[self.at(n.l)].astype(F32)
        out[...] = out[...] + value if add else value

        @pl.when(n.has_left)
        def _():
            self.hop(n.l, n.l, n.right).wait_recv()
            out[...] += self.rcv[self.at(n.l)].astype(F32)

        @pl.when(n.has_right)
        def _():
            self.hop(n.l, n.n_line, n.left).wait_recv()
            out[...] += self.rcv[self.at(n.n_line)].astype(F32)

        @pl.loop(0, n.n_line)
        def _(chip):
            self.across(chip).wait_send()
            pl.when(chip > n.l)(lambda: self.hop(chip, chip, n.right).wait_send())
            pl.when(chip < n.l)(lambda: self.hop(chip, chip, n.left).wait_send())


def norm_back(u, ge):
    r = lax.rsqrt(jnp.mean(u * u, axis=1, keepdims=True) + EPSILON)
    return r * ge - u * (r * r * r * jnp.mean(u * ge, axis=1, keepdims=True))


def spread_work(units, slots, index):
    return (units * index // slots, units * (index + 1) // slots)


class Square:
    def __init__(self):
        self.d = lax.axis_index("dp")
        self.first = self.d + 1 - 2 * lax.rem(self.d, 2)
        self.second = lax.rem(self.d + 2, 4)
        self.across = 3 - self.d


class Spread:
    def __init__(self, line, n_dp, blocks, dst, own_sem, send_z, send_xy, recv):
        self.line, self.n_dp, self.blocks, self.dst = line, n_dp, blocks, dst
        self.own_sem, self.send_z, self.send_xy, self.recv = own_sem, send_z, send_xy, recv
        self.n_seq = 2 * line.n_line
        self.d = lax.axis_index("dp")

    @staticmethod
    def sems(n_seq, n_dp):
        return [
            pltpu.SemaphoreType.DMA((1,)),
            pltpu.SemaphoreType.DMA((n_seq,)),
            pltpu.SemaphoreType.DMA((n_seq, n_dp)),
            pltpu.SemaphoreType.DMA((n_dp, n_seq)),
        ]

    def source(self, j):
        return lax.rem(self.line.s - j + self.n_seq, self.n_seq)

    def hop(self, t):
        n = self.line
        return pltpu.make_async_remote_copy(
            src_ref=self.blocks.at[t],
            dst_ref=self.dst.at[self.d, n.s],
            send_sem=self.send_z.at[t],
            recv_sem=self.recv.at[self.d, n.s],
            device_id={"seq": t},
            device_id_type=MESH,
        )

    def own(self):
        n = self.line
        return pltpu.make_async_copy(self.blocks.at[n.s], self.dst.at[self.d, n.s], self.own_sem.at[0])

    def to_dp(self, src, dst, send, recv, peer):
        return pltpu.make_async_remote_copy(
            src_ref=src, dst_ref=dst, send_sem=send, recv_sem=recv, device_id={"dp": peer}, device_id_type=MESH
        )

    def over(self, source, own=False):
        src = self.blocks.at[self.line.s] if own else self.dst.at[self.d, source]
        peers = [lax.rem(self.d + k, self.n_dp) for k in range(1, self.n_dp)]
        return [
            self.to_dp(src, self.dst.at[self.d, source], self.send_xy.at[source, k], self.recv.at[self.d, source], peer)
            for k, peer in enumerate(peers)
        ]

    def landed(self, d, source):
        block = self.dst.at[d, source]
        return self.to_dp(block, block, self.send_z.at[0], self.recv.at[d, source], d)

    def begin(self, end):
        n = self.line

        @pl.loop(1, end)
        def _(j):
            self.hop(lax.rem(n.s + j, self.n_seq)).start()

        self.own().start()

    def forward_one(self, j, ahead):
        n = self.line

        @pl.when(j < self.n_seq)
        def _():
            pl.when(j + ahead < self.n_seq)(lambda: self.hop(lax.rem(n.s + j + ahead, self.n_seq)).start())
            source = self.source(j)
            self.landed(self.d, source).wait_recv()
            for copy in self.over(source):
                copy.start()

    def forward_own(self):
        for copy in self.over(self.line.s, True):
            copy.start()

    def arrive(self):
        @pl.loop(0, self.n_seq)
        def _(source):
            for k in range(1, self.n_dp):
                self.landed(lax.rem(self.d + k, self.n_dp), source).wait_recv()

        self.own().wait()

    def end(self):
        n = self.line

        @pl.loop(0, self.n_seq)
        def _(j):
            pl.when(j != n.s)(lambda: self.hop(j).wait_send())
            for copy in self.over(j):
                copy.wait_send()


class Copies:
    def __init__(self, n_dp, own, dst, own_sem, send, recv):
        self.n_dp, self.own_ref, self.dst = n_dp, own, dst
        self.own_sem, self.send, self.recv = own_sem, send, recv
        self.d = lax.axis_index("dp")
        self.relay = n_dp == 4
        self.square = Square()
        self.half = own.shape[0] // 2

    @staticmethod
    def sems(n_dp):
        return [
            pltpu.SemaphoreType.DMA((1,)),
            pltpu.SemaphoreType.DMA((n_dp,)),
            pltpu.SemaphoreType.DMA((n_dp + 1,)),
        ]

    def copy(self, src, slot, part, send, recv, peer):
        return pltpu.make_async_remote_copy(
            src_ref=src,
            dst_ref=self.dst.at[slot] if part is None else self.dst.at[slot, part],
            send_sem=self.send.at[send],
            recv_sem=self.recv.at[recv],
            device_id={"dp": peer},
            device_id_type=MESH,
        )

    def direct(self):
        peers = [lax.rem(self.d + k, self.n_dp) for k in range(1, self.n_dp)]
        if self.relay:
            peers = [self.square.first, self.square.second]
        return [self.copy(self.own_ref, self.d, None, k + 1, self.d, peer) for k, peer in enumerate(peers)]

    def landed(self, slot):
        return self.copy(self.dst.at[slot], slot, None, 0, slot, slot)

    def halves(self):
        q = self.square
        low, high = pl.ds(0, self.half), pl.ds(self.half, self.half)
        return (
            self.copy(self.dst.at[q.first, low], q.first, low, 3, q.first, q.second),
            self.copy(self.dst.at[q.second, high], q.second, high, 0, self.n_dp, q.first),
        )

    def own(self):
        return pltpu.make_async_copy(self.own_ref, self.dst.at[self.d], self.own_sem.at[0])

    def begin(self):
        for copy in self.direct():
            copy.start()
        self.own().start()

    def pass_on(self):
        if not self.relay:
            return
        one, two = self.halves()
        self.landed(self.square.first).wait_recv()
        one.start()
        self.landed(self.square.second).wait_recv()
        two.start()

    def end(self):
        for copy in self.direct():
            copy.wait_send()
        if self.relay:
            low, high = pl.ds(0, self.half), pl.ds(self.half, self.half)
            across = self.square.across
            self.copy(self.dst.at[across, low], across, low, 0, across, across).wait_recv()
            self.copy(self.dst.at[across, high], across, high, 0, self.n_dp, across).wait_recv()
            for copy in self.halves():
                copy.wait_send()
        else:
            for k in range(1, self.n_dp):
                self.landed(lax.rem(self.d + k, self.n_dp)).wait_recv()
        self.own().wait()


class Relay:
    def __init__(self, line, n_dp):
        n_seq = 2 * line.n_line
        self.n_dp = n_dp
        self.d = lax.axis_index("dp")
        block = self.d * n_seq + line.s
        self.slot, self.target = lax.rem(block, n_dp), lax.div(block, n_dp)
        block = line.s * n_dp + self.d
        self.owner_d, self.owner_s = lax.div(block, n_seq), lax.rem(block, n_seq)
        self.stays = (self.slot == self.d) & (self.target == line.s)
        self.moves = jnp.logical_not(self.stays)

    def to_relay(self, src, dst, send, recv):
        return pltpu.make_async_remote_copy(
            src_ref=src, dst_ref=dst, send_sem=send, recv_sem=recv,
            device_id=(self.slot, self.target), device_id_type=MESH,
        )

    def to_owner(self, src, dst, send, recv):
        return pltpu.make_async_remote_copy(
            src_ref=src, dst_ref=dst, send_sem=send, recv_sem=recv,
            device_id=(self.owner_d, self.owner_s), device_id_type=MESH,
        )

    def over(self, k, src, dst, send, recv):
        return pltpu.make_async_remote_copy(
            src_ref=src, dst_ref=dst, send_sem=send, recv_sem=recv,
            device_id={"dp": lax.rem(self.d + k, self.n_dp)}, device_id_type=MESH,
        )


class OutRows(Relay):
    def __init__(self, line, n_dp, own, dst, own_sem, send_z, send_xy, recv):
        super().__init__(line, n_dp)
        self.own_ref, self.dst = own, dst
        self.own_sem, self.send_z, self.send_xy, self.recv = own_sem, send_z, send_xy, recv

    @staticmethod
    def sems(n_dp):
        return [
            pltpu.SemaphoreType.DMA((1,)),
            pltpu.SemaphoreType.DMA((1,)),
            pltpu.SemaphoreType.DMA((n_dp,)),
            pltpu.SemaphoreType.DMA((n_dp,)),
        ]

    def hop(self):
        return self.to_relay(self.own_ref, self.dst.at[self.slot], self.send_z.at[0], self.recv.at[self.slot])

    def own(self):
        return pltpu.make_async_copy(self.own_ref, self.dst.at[self.slot], self.own_sem.at[0])

    def copy(self, k):
        return self.over(k, self.dst.at[self.d], self.dst.at[self.d], self.send_xy.at[k], self.recv.at[self.d])

    def landed(self, slot):
        return self.over(1, self.dst.at[slot], self.dst.at[slot], self.send_xy.at[1], self.recv.at[slot])

    def begin(self):
        pl.when(self.stays)(lambda: self.own().start())
        pl.when(self.moves)(lambda: self.hop().start())

    def forward(self):
        pl.when(self.stays)(lambda: self.own().wait())
        pl.when(self.moves)(lambda: self.landed(self.d).wait_recv())
        for k in range(1, self.n_dp):
            self.copy(k).start()

    def arrive(self):
        for k in range(1, self.n_dp):
            self.landed(lax.rem(self.d + k, self.n_dp)).wait_recv()

    def end(self):
        pl.when(self.moves)(lambda: self.hop().wait_send())
        for k in range(1, self.n_dp):
            self.copy(k).wait_send()


class OutSum(Relay):
    def __init__(self, line, n_dp, src, land, final, own_sem, send_xy, recv_xy, send_z, recv_z):
        super().__init__(line, n_dp)
        self.src, self.land, self.final = src, land, final
        self.own_sem, self.send_xy, self.recv_xy, self.send_z, self.recv_z = own_sem, send_xy, recv_xy, send_z, recv_z

    @staticmethod
    def sems(n_dp):
        return [
            pltpu.SemaphoreType.DMA((1,)),
            pltpu.SemaphoreType.DMA((n_dp,)),
            pltpu.SemaphoreType.DMA((n_dp,)),
            pltpu.SemaphoreType.DMA((1,)),
            pltpu.SemaphoreType.DMA((1,)),
        ]

    def copy(self, k):
        return self.over(
            k, self.src.at[lax.rem(self.d + k, self.n_dp)], self.land.at[self.d], self.send_xy.at[k], self.recv_xy.at[self.d]
        )

    def landed(self, owner):
        return self.over(1, self.land.at[owner], self.land.at[owner], self.send_xy.at[1], self.recv_xy.at[owner])

    def own(self):
        return pltpu.make_async_copy(self.src.at[self.d], self.land.at[self.d], self.own_sem.at[0])

    def hop(self):
        return self.to_owner(self.land.at[self.d], self.final, self.send_z.at[0], self.recv_z.at[0])

    def begin(self):
        self.own().start()
        for k in range(1, self.n_dp):
            self.copy(k).start()

    def reduce(self):
        self.own().wait()
        for k in range(1, self.n_dp):
            self.landed(lax.rem(self.d + k, self.n_dp)).wait_recv()
        total = self.land[0].astype(F32)
        for owner in range(1, self.n_dp):
            total = total + self.land[owner].astype(F32)
        total = total.astype(BF16)

        @pl.when(self.stays)
        def _():
            self.final[...] = total

        @pl.when(self.moves)
        def _():
            self.land[self.d] = total
            self.hop().start()

    def end(self):
        pl.when(self.moves)(lambda: self.hop().wait())
        for k in range(1, self.n_dp):
            self.copy(k).wait_send()


class Collect:
    def __init__(self, line, n_dp, src, land, final, own_sem, send_xy, recv_xy, send_z, recv_z):
        self.line, self.n_dp, self.n_seq = line, n_dp, 2 * line.n_line
        self.src, self.land, self.final = src, land, final
        self.own_sem, self.send_xy, self.recv_xy, self.send_z, self.recv_z = own_sem, send_xy, recv_xy, send_z, recv_z
        self.d = lax.axis_index("dp")

    @staticmethod
    def sems(n_seq, n_dp):
        return [
            pltpu.SemaphoreType.DMA((1,)),
            pltpu.SemaphoreType.DMA((n_seq, n_dp)),
            pltpu.SemaphoreType.DMA((n_dp, n_seq)),
            pltpu.SemaphoreType.DMA((n_seq,)),
            pltpu.SemaphoreType.DMA((n_seq,)),
        ]

    def over(self, t, k):
        peer = lax.rem(self.d + k, self.n_dp)
        return pltpu.make_async_remote_copy(
            src_ref=self.src.at[peer, t],
            dst_ref=self.land.at[self.d, t],
            send_sem=self.send_xy.at[t, k],
            recv_sem=self.recv_xy.at[self.d, t],
            device_id={"dp": peer},
            device_id_type=MESH,
        )

    def landed(self, owner, t):
        return pltpu.make_async_remote_copy(
            src_ref=self.land.at[owner, t],
            dst_ref=self.land.at[owner, t],
            send_sem=self.send_xy.at[t, 1],
            recv_sem=self.recv_xy.at[owner, t],
            device_id={"dp": owner},
            device_id_type=MESH,
        )

    def own(self):
        return pltpu.make_async_copy(self.src.at[self.d], self.land.at[self.d], self.own_sem.at[0])

    def hop(self, t, slot):
        return pltpu.make_async_remote_copy(
            src_ref=self.land.at[self.d, t],
            dst_ref=self.final.at[slot],
            send_sem=self.send_z.at[t],
            recv_sem=self.recv_z.at[slot],
            device_id={"seq": t},
            device_id_type=MESH,
        )

    def place(self, j):
        return lax.rem(self.line.s + 1 + j, self.n_seq)

    def begin(self, ahead):
        self.ahead = ahead
        self.own().start()

        @pl.loop(0, ahead)
        def _(j):
            self.send(j)

    def send(self, j):
        for k in range(1, self.n_dp):
            self.over(self.place(j), k).start()

    def reduce(self, first, end):
        if first == 0:
            self.own().wait()

        @pl.loop(first, end)
        def _(j):
            t = self.place(j)
            pl.when(j + self.ahead < self.n_seq)(lambda: self.send(j + self.ahead))
            for k in range(1, self.n_dp):
                self.landed(lax.rem(self.d + k, self.n_dp), t).wait_recv()
            total = self.land[0, t].astype(F32)
            for owner in range(1, self.n_dp):
                total = total + self.land[owner, t].astype(F32)
            total = total.astype(BF16)

            @pl.when(t == self.line.s)
            def _():
                self.final[t] = total

            @pl.when(t != self.line.s)
            def _():
                self.land[self.d, t] = total
                self.hop(t, self.line.s).start()

    def end(self):
        @pl.loop(0, self.n_seq)
        def _(t):
            pl.when(t != self.line.s)(lambda: self.hop(t, t).wait())
            for k in range(1, self.n_dp):
                self.over(t, k).wait_send()


class RowSum:
    def __init__(self, n_dp, src, land, own_sem, send, recv):
        self.n_dp, self.src, self.land = n_dp, src, land
        self.own_sem, self.send, self.recv = own_sem, send, recv
        self.d = lax.axis_index("dp")

    @staticmethod
    def sems(n_dp):
        return [
            pltpu.SemaphoreType.DMA((1,)),
            pltpu.SemaphoreType.DMA((n_dp,)),
            pltpu.SemaphoreType.DMA((n_dp,)),
        ]

    def copy(self, k, slot):
        peer = lax.rem(self.d + k, self.n_dp)
        return pltpu.make_async_remote_copy(
            src_ref=self.src.at[peer],
            dst_ref=self.land.at[slot],
            send_sem=self.send.at[k],
            recv_sem=self.recv.at[slot],
            device_id={"dp": peer},
            device_id_type=MESH,
        )

    def own(self):
        return pltpu.make_async_copy(self.src.at[self.d], self.land.at[self.d], self.own_sem.at[0])

    def begin(self):
        self.own().start()
        for k in range(1, self.n_dp):
            self.copy(k, self.d).start()

    def finish(self, out):
        self.own().wait()
        for k in range(1, self.n_dp):
            self.copy(k, lax.rem(self.d + k, self.n_dp)).wait()
        total = self.land[0].astype(F32)
        for owner in range(1, self.n_dp):
            total = total + self.land[owner].astype(F32)
        out[...] = total


def greet_all(line, n_dp, relay, between=None):
    barrier = pltpu.get_barrier_semaphore()
    n_seq = 2 * line.n_line
    d = lax.axis_index("dp")
    for j in range(1, n_seq):
        pl.semaphore_signal(barrier, 1, device_id={"seq": lax.rem(line.s + j, n_seq)}, device_id_type=MESH)
    for k in range(1, n_dp):
        pl.semaphore_signal(barrier, 1, device_id={"dp": lax.rem(d + k, n_dp)}, device_id_type=MESH)

    if relay is None:
        if between is not None:
            between()
        pl.semaphore_wait(barrier, n_seq + n_dp - 2)
        return

    @pl.when(relay.moves)
    def _():
        for device in ((relay.slot, relay.target), (relay.owner_d, relay.owner_s)):
            pl.semaphore_signal(barrier, 1, device_id=device, device_id_type=MESH)

    if between is not None:
        between()
    pl.semaphore_wait(barrier, n_seq + n_dp - 2 + jnp.where(relay.moves, 2, 0))


def turn(values, lanes_low):
    half = HEAD_DIM // 2
    width = values.shape[-1]
    return jnp.where(
        lanes_low, pltpu.roll(values, width - half, values.ndim - 1), pltpu.roll(values, half, values.ndim - 1)
    )


def low_lanes(shape):
    return lax.rem(lax.broadcasted_iota(jnp.int32, shape, len(shape) - 1), HEAD_DIM) < HEAD_DIM // 2


def head_lanes(kv, h, q_cols):
    wide = jnp.concatenate([kv] * (q_cols // (2 * HEAD_DIM)), axis=1).astype(F32)
    swapped = pltpu.roll(wide, HEAD_DIM, 1)
    here = lax.div(lax.broadcasted_iota(jnp.int32, wide.shape, 1), HEAD_DIM) == h
    key, value = (wide, swapped) if h % 2 == 0 else (swapped, wide)
    key = jnp.where(here, key * (1.0 / math.sqrt(HEAD_DIM)), 0.0).astype(BF16)
    return key, jnp.where(here, value, 0.0).astype(BF16)


def hidden_keys(first, second, prefix, query_axis):
    query, key = (first, second) if query_axis == 0 else (second, first)
    return jnp.where((key <= query) | (key < prefix), 0.0, NEGATIVE)


def bias_shape(length):
    return (length, length) if length <= 2 * QUERY_TILE else (8, 128)


def fill_bias(bias, prefix, query_axis, length):
    if bias.shape[0] != length:
        return
    tile = min(length, QUERY_TILE)

    @pl.loop(0, length // tile)
    def _(i):
        at = pl.ds(pl.multiple_of(i * tile, tile), tile)
        first = i * tile + lax.broadcasted_iota(jnp.int32, (tile, length), 0)
        second = lax.broadcasted_iota(jnp.int32, (tile, length), 1)
        bias[at, :] = hidden_keys(first, second, prefix, query_axis)


def bias_tile(bias, prefix, query_axis, length, tile, i):
    at = pl.ds(pl.multiple_of(i * tile, tile), tile)
    if bias.shape[0] == length:
        return bias[at, :] if query_axis == 0 else bias[:, at]
    shape = (tile, length) if query_axis == 0 else (length, tile)
    first = lax.broadcasted_iota(jnp.int32, shape, 0)
    second = lax.broadcasted_iota(jnp.int32, shape, 1)
    if query_axis == 0:
        first = first + i * tile
    else:
        second = second + i * tile
    return hidden_keys(first, second, prefix, query_axis)


def attention_kernel(
    n_seq, n_dp, prefix_ref, tok_ref, cot_ref, cos_ref, sin_ref, gains_ref,
    w_query_ref, w_key_ref, w_value_ref, w_gate_ref, w_up_ref, wo_own, wd_own,
    hidden_ref, nmlp_ref, q_ref, kv_ref, mixed_ref, normed_hbm, cot_hbm, wqkv_hbm, wo_hbm, wgu_hbm, wd_hbm,
    full, cot, wqkv, wo, acc, part, sib, rcv, qkvb, gub, bias, save_sem, *sems,
):
    n = Line(n_seq)
    rows, width = tok_ref.shape
    micro, length, q_cols = q_ref.shape
    span = rows // micro
    cols_all = wqkv.shape[3]
    pair = 2 * rows

    def prepare():
        tok = tok_ref[...].astype(F32)
        normed = (tok * lax.rsqrt(jnp.mean(tok * tok, axis=1, keepdims=True) + EPSILON)).astype(BF16)
        for m in range(micro):
            full[m, n.s] = normed[m * span : (m + 1) * span]
        cot[n.s] = cot_ref[...]
        for t in range(n_seq):
            head = slice(t // repeat * HEAD_DIM, (t // repeat + 1) * HEAD_DIM)
            qkvb[t, :, :q_cols] = (w_query_ref[:, t * q_cols : (t + 1) * q_cols].astype(F32) * gain_attn).astype(BF16)
            key_value = jnp.concatenate([w_key_ref[:, head], w_value_ref[:, head]], axis=1)
            qkvb[t, :, q_cols:] = (key_value.astype(F32) * gain_attn).astype(BF16)

    sems = list(sems)
    take = lambda count: [sems.pop(0) for _ in range(count)]
    gathers = [Gather(n, full, *take(3), m=m) for m in range(micro)]
    scatters = [Scatter(n, part, sib, rcv, *take(4), m=m) for m in range(micro)]
    gather_cot = Gather(n, cot, *take(3))
    qkv_w = Spread(n, n_dp, qkvb, wqkv, *take(4))
    gu_w = Spread(n, n_dp, gub, wgu_hbm, *take(4))
    out_w = OutRows(n, n_dp, wo_own, wo, *take(4))
    down_w = Copies(n_dp, wd_own, wd_hbm, *take(3))

    repeat = n_seq // KV_HEADS
    ff_block = wd_own.shape[0]
    gain_attn = gains_ref[:, :1]
    gain_mlp = gains_ref[:, 2 * HEAD_DIM : 2 * HEAD_DIM + 1]

    greet_all(n, n_dp, out_w, prepare)
    qkv_w.begin(n_seq)
    gathers[0].begin()
    out_w.begin()
    qkv_w.forward_own()
    for i, ref in enumerate((w_gate_ref, w_up_ref)):
        for owner in range(n_dp):
            for t in range(n_seq):
                cols = slice((owner * n_seq + t) * ff_block, (owner * n_seq + t + 1) * ff_block)
                first = (i * n_dp + owner) * ff_block
                gub[t, :, first : first + ff_block] = (ref[:, cols].astype(F32) * gain_mlp).astype(BF16)

    @pl.loop(1, n_seq)
    def _(j):
        qkv_w.forward_one(j, n_seq)

    out_w.forward()
    gathers[1].begin()
    down_w.begin()
    gu_w.forward_own()
    for j in range(n.n_line):
        gathers[0].visit(n.order(j))
    qkv_w.arrive()
    pltpu.make_async_copy(wqkv, wqkv_hbm, save_sem.at[1]).start()
    gu_w.begin(1 + AHEAD)

    low = low_lanes((span, cols_all))
    half_line = length // span // 2
    heads = q_cols // HEAD_DIM
    q_tile = min(length, QUERY_TILE)

    def project(m):
        @pl.loop(0, 2)
        def _(i):
            some = pl.ds(pl.multiple_of(i * half_line, half_line), half_line)
            value = nn(full[m, some].reshape(half_line * span, width), wqkv[...].reshape(width, cols_all))
            for k in range(half_line):
                at = pl.ds(pl.multiple_of((i * half_line + k) * span, span), span)
                block = value[k * span : (k + 1) * span]
                turned = (block * cos_ref[at, :] + turn(block, low) * sin_ref[at, :]).astype(BF16)
                q_ref[m, at, :] = turned[:, :q_cols]
                kv_ref[m, at, :] = turned[:, q_cols:]

    def attend(m, h):
        key, val = head_lanes(kv_ref[m], h, q_cols)

        @pl.loop(0, length // q_tile)
        def _(i):
            at = pl.ds(pl.multiple_of(i * q_tile, q_tile), q_tile)
            scores = nt(q_ref[m, at, :], key) + bias_tile(bias, prefix_ref[m], 0, length, q_tile, i)
            weights = jnp.exp(scores - jnp.max(scores, axis=1, keepdims=True))
            inverse = 1.0 / jnp.sum(weights, axis=1, keepdims=True)
            mixed = nn((weights * inverse).astype(BF16), val)
            if h == 0:
                acc[at, :] = mixed
            else:
                acc[at, :] += mixed

    sent = 0
    for m in range(micro):
        project(m)
        fill_bias(bias, prefix_ref[m], 0, length)
        for h in range(heads):
            if m + 1 < micro:
                for j in range(*spread_work(n.n_line, heads, h)):
                    gathers[m + 1].visit(n.order(j))
            if m == 1 and h == 0:
                down_w.pass_on()
            attend(m, h)
            done = m * heads + h
            for _ in range(*spread_work(n_seq - 1, micro * heads - 1, done - 1) if done else (0,)):
                sent += 1
                gu_w.forward_one(sent, AHEAD)
        mixed_ref[m] = acc[...].astype(BF16)
        if m == 0:
            out_w.arrive()
            pltpu.make_async_copy(wo, wo_hbm, save_sem.at[2]).start()

        @pl.loop(0, width // TILE)
        def _(w):
            cols = pl.ds(pl.multiple_of(w * TILE, TILE), TILE)
            value = nn(mixed_ref[m], wo[:, :, cols].reshape(q_cols, TILE))
            part[m, :, :, cols] = value.astype(BF16).reshape(n_seq, span, TILE)

        scatters[m].begin()
        if m == 0:
            gather_cot.begin()

    pltpu.make_async_copy(full, normed_hbm, save_sem.at[0]).start()
    gather_cot.visit(n.l)
    for time in range(n.last):
        for scatter in scatters:
            scatter.step(time)
        gather_cot.visit(n.order(time + 1))
    pltpu.make_async_copy(cot, cot_hbm, save_sem.at[3]).start()
    for m in range(micro):
        at = slice(m * span, (m + 1) * span)
        scatters[m].finish(hidden_ref.at[at])
    hidden = hidden_ref[...] + tok_ref[...].astype(F32)
    hidden_ref[...] = hidden
    nmlp_ref[...] = (hidden * lax.rsqrt(jnp.mean(hidden * hidden, axis=1, keepdims=True) + EPSILON)).astype(BF16)
    gu_w.arrive()
    down_w.end()
    pltpu.make_async_copy(full, normed_hbm, save_sem.at[0]).wait()
    pltpu.make_async_copy(wqkv, wqkv_hbm, save_sem.at[1]).wait()
    pltpu.make_async_copy(wo, wo_hbm, save_sem.at[2]).wait()
    pltpu.make_async_copy(cot, cot_hbm, save_sem.at[3]).wait()
    for gather in gathers:
        gather.end()
    gather_cot.end()
    qkv_w.end()
    gu_w.end()
    out_w.end()


def attention_call(prefix, tok, cot, cos, sin, gains, w_query, w_key, w_value, w_gate, w_up, wo_own, wd_own, n_seq, n_dp):
    rows, width = tok.shape
    micro = prefix.shape[0]
    length = cos.shape[0]
    shard = wo_own.shape[0]
    q_cols = width // n_seq
    qkv_cols = q_cols + 2 * HEAD_DIM
    ff_block = wd_own.shape[0]
    gu_cols = 2 * n_dp * ff_block
    every = n_seq * rows
    any_spec = pl.BlockSpec(memory_space=pl.ANY)
    vmem = pl.BlockSpec(memory_space=pltpu.VMEM)
    outs = [
        ((rows, width), F32, vmem),
        ((rows, width), BF16, vmem),
        ((micro, length, q_cols), BF16, vmem),
        ((micro, length, 2 * HEAD_DIM), BF16, vmem),
        ((micro, length, q_cols), BF16, vmem),
        ((micro, n_seq, rows // micro, width), BF16, any_spec),
        ((n_seq, rows, width), BF16, any_spec),
        ((n_dp, n_seq, shard, qkv_cols), BF16, any_spec),
        ((n_dp, shard, width), BF16, any_spec),
        ((n_dp, n_seq, shard, gu_cols), BF16, any_spec),
        ((n_dp, ff_block, width), BF16, any_spec),
    ]
    return pl.pallas_call(
        functools.partial(attention_kernel, n_seq, n_dp),
        out_shape=tuple(jax.ShapeDtypeStruct(s, t) for s, t, _ in outs),
        in_specs=[pl.BlockSpec(memory_space=pltpu.SMEM)] + [vmem] * 10 + [any_spec] * 2,
        out_specs=tuple(spec for _, _, spec in outs),
        scratch_shapes=[
            pltpu.VMEM((micro, n_seq, rows // micro, width), BF16),
            pltpu.VMEM((n_seq, rows, width), BF16),
            pltpu.VMEM((n_dp, n_seq, shard, qkv_cols), BF16),
            pltpu.VMEM((n_dp, shard, width), BF16),
            pltpu.VMEM((length, q_cols), F32),
            pltpu.VMEM((micro, n_seq, rows // micro, width), BF16),
            *Scatter.buffers(n_seq, rows // micro, width, micro),
            pltpu.VMEM((n_seq, shard, qkv_cols), BF16),
            pltpu.VMEM((n_seq, shard, gu_cols), BF16),
            pltpu.VMEM(bias_shape(length), F32),
            pltpu.SemaphoreType.DMA((4,)),
            *Gather.sems(n_seq) * micro,
            *Scatter.sems(n_seq) * micro,
            *Gather.sems(n_seq),
            *Spread.sems(n_seq, n_dp),
            *Spread.sems(n_seq, n_dp),
            *OutRows.sems(n_dp),
            *Copies.sems(n_dp),
        ],
        compiler_params=pltpu.CompilerParams(
            collective_id=2, has_side_effects=True, vmem_limit_bytes=VMEM_LIMIT
        ),
        cost_estimate=pl.CostEstimate(flops=10**10, bytes_accessed=40 << 20, transcendentals=0),
        name="attention",
    )(prefix, tok, cot, cos, sin, gains, w_query, w_key, w_value, w_gate, w_up, wo_own, wd_own)


def mlp_kernel(
    n_seq, n_dp, x_ref, hidden_ref, cot_hbm, wgu_hbm, wd_hbm,
    branch_ref, gh_ref, pout_hbm, dgu_hbm, dwd_ref,
    full, cot, wgu, wd, act, gg, gu, part, sib, rcv, dwd, land, total, stage_gu, stage_rows, load_sem, gu_sem, rows_sem, *sems,
):
    n = Line(n_seq)
    rows, width = x_ref.shape
    ff = wd.shape[0]
    pair = 2 * rows
    loads = [
        pltpu.make_async_copy(src, dst, load_sem.at[i])
        for i, (src, dst) in enumerate(
            [(wgu_hbm, wgu), (cot_hbm, cot), (wd_hbm, wd)]
        )
    ]

    def prepare():
        for load in loads:
            load.start()
        full[n.s] = x_ref[...]

    greet_all(n, n_dp, None, prepare)
    gather = Gather(n, full, *sems[:3])
    scatter = Scatter(n, part, sib, rcv, *sems[3:7])
    down = RowSum(n_dp, dwd, land, *sems[7:10])
    gather.begin()
    for load in loads:
        load.wait()

    @pl.loop(0, n.n_line)
    def _(j):
        chip = n.order(j)
        near = 2 * jnp.minimum(n.l, n.last - n.l)
        odd = lax.rem(j, 2) == 1
        pl.when((j == 0) | odd | (j > near))(lambda: gather.visit(chip))
        pl.when(odd & (j < near))(lambda: gather.visit(n.order(j + 1)))
        at = pl.ds(pl.multiple_of(chip * pair, pair), pair)
        two = pl.ds(pl.multiple_of(2 * chip, 2), 2)

        @pl.loop(0, ff // TILE)
        def _(f):
            cols = pl.ds(pl.multiple_of(f * TILE, TILE), TILE)
            x = full[two].reshape(pair, width)
            gate = nn(x, wgu[:, cols])
            up = nn(x, wgu[:, pl.ds(pl.multiple_of(ff + f * TILE, TILE), TILE)])
            grad = nt(cot[two].reshape(pair, width), wd[cols, :])
            sig = jax.nn.sigmoid(gate)
            silu = gate * sig
            act[at, cols] = (silu * up).astype(BF16)
            gg[at, cols] = (grad * up * (sig + silu * (1.0 - sig))).astype(BF16)
            gu[at, cols] = (grad * silu).astype(BF16)

        @pl.loop(0, width // TILE)
        def _(w):
            cols = pl.ds(pl.multiple_of(w * TILE, TILE), TILE)
            value = nt(gg[at, :], wgu[cols, :ff]) + nt(gu[at, :], wgu[cols, ff:])
            part[two, :, cols] = value.astype(BF16).reshape(2, rows, TILE)

    scatter.begin()
    scatter.step(0)
    owners = TILE // dwd.shape[1]

    def down_grad(f):
        cols = pl.ds(pl.multiple_of(f * TILE, TILE), TILE)
        at = pl.ds(f * owners, owners)
        for w in range(0, width, 2 * TILE):
            span = cot[:, :, w : w + 2 * TILE].reshape(n_seq * rows, 2 * TILE)
            value = tn(act[:, cols], span).astype(BF16)
            dwd[at, :, w : w + 2 * TILE] = value.reshape(owners, dwd.shape[1], 2 * TILE)

    if owners == 1:

        @pl.loop(1, n_dp + 1)
        def _(k):
            down_grad(lax.rem(down.d + k, n_dp))
            pl.when(k < n_dp)(lambda: down.copy(k, down.d).start())

        down.own().start()
    else:
        pl.loop(0, ff // TILE)(down_grad)
        down.begin()

    def gate_up_grads(first, end):
        @pl.loop(first, end)
        def _(w):
            slot = lax.rem(w, 2)
            cols = pl.ds(pl.multiple_of(w * TILE, TILE), TILE)
            x = full[:, :, cols].reshape(n_seq * rows, TILE)
            copy = pltpu.make_async_copy(stage_gu.at[slot], dgu_hbm.at[cols, :], gu_sem.at[slot])
            pl.when(w >= 2)(lambda: copy.wait())
            stage_gu[slot, :, :ff] = tn(x, gg[...]).astype(BF16)
            stage_gu[slot, :, ff:] = tn(x, gu[...]).astype(BF16)
            copy.start()

    def out_parts(first, end):
        @pl.loop(first, end)
        def _(chip):
            slot = lax.rem(chip, 2)
            at = pl.ds(pl.multiple_of(chip * pair, pair), pair)
            two = pl.ds(pl.multiple_of(2 * chip, 2), 2)
            copies = [
                pltpu.make_async_copy(
                    stage_rows.at[slot, pl.ds(i * rows, rows)], pout_hbm.at[2 * chip + i], rows_sem.at[slot + 2 * i]
                )
                for i in range(2)
            ]

            @pl.when(chip >= 2)
            def _():
                for copy in copies:
                    copy.wait()

            for w in range(0, width, 2 * TILE):
                stage_rows[slot, :pair, w : w + 2 * TILE] = nn(act[at, :], wd[:, w : w + 2 * TILE]).astype(BF16)
            for copy in copies:
                copy.start()

    def drain_out():
        for slot in range(2):
            for i in range(2):
                pltpu.make_async_copy(
                    stage_rows.at[slot, pl.ds(i * rows, rows)], pout_hbm.at[i], rows_sem.at[slot + 2 * i]
                ).wait()

    for time in range(n.last):
        if time > 0:
            scatter.step(time)
        if time == 0:
            out_parts(0, n.n_line)
        gate_up_grads(*spread_work(width // TILE, n.last, time))
    scatter.finish(total)
    grad_hidden = cot[n.s].astype(F32) + norm_back(hidden_ref[...], total[...])
    gh_ref[...] = grad_hidden
    branch_ref[...] = grad_hidden.astype(BF16)
    drain_out()
    for slot in range(2):
        pltpu.make_async_copy(stage_gu.at[slot], dgu_hbm.at[pl.ds(0, TILE), :], gu_sem.at[slot]).wait()
    down.finish(dwd_ref)
    gather.end()


def mlp_call(x, hidden, cot, wgu, wd, n_seq, n_dp):
    rows, width = x.shape
    ff = wd.shape[0]
    every = n_seq * rows
    any_spec = pl.BlockSpec(memory_space=pl.ANY)
    vmem = pl.BlockSpec(memory_space=pltpu.VMEM)
    return pl.pallas_call(
        functools.partial(mlp_kernel, n_seq, n_dp),
        out_shape=(
            jax.ShapeDtypeStruct((rows, width), BF16),
            jax.ShapeDtypeStruct((rows, width), F32),
            jax.ShapeDtypeStruct((n_seq, rows, width), BF16),
            jax.ShapeDtypeStruct((width, 2 * ff), BF16),
            jax.ShapeDtypeStruct((ff // n_dp, width), F32),
        ),
        in_specs=[vmem] * 2 + [any_spec] * 3,
        out_specs=(vmem, vmem, any_spec, any_spec, vmem),
        scratch_shapes=[
            pltpu.VMEM((n_seq, rows, width), BF16),
            pltpu.VMEM((n_seq, rows, width), BF16),
            pltpu.VMEM((width, 2 * ff), BF16),
            pltpu.VMEM((ff, width), BF16),
            pltpu.VMEM((every, ff), BF16),
            pltpu.VMEM((every, ff), BF16),
            pltpu.VMEM((every, ff), BF16),
            pltpu.VMEM((n_seq, rows, width), BF16),
            *Scatter.buffers(n_seq, rows, width),
            pltpu.VMEM((n_dp, ff // n_dp, width), BF16),
            pltpu.VMEM((n_dp, ff // n_dp, width), BF16),
            pltpu.VMEM((rows, width), F32),
            pltpu.VMEM((2, TILE, 2 * ff), BF16),
            pltpu.VMEM((2, TILE, width), BF16),
            pltpu.SemaphoreType.DMA((3,)),
            pltpu.SemaphoreType.DMA((2,)),
            pltpu.SemaphoreType.DMA((4,)),
            *Gather.sems(n_seq),
            *Scatter.sems(n_seq),
            *RowSum.sems(n_dp),
        ],
        compiler_params=pltpu.CompilerParams(
            collective_id=1, has_side_effects=True, vmem_limit_bytes=VMEM_LIMIT
        ),
        cost_estimate=pl.CostEstimate(flops=18 * every * width * ff, bytes_accessed=40 << 20, transcendentals=0),
        name="mlp",
    )(x, hidden, cot, wgu, wd)


def backward_kernel(
    n_seq, n_dp, prefix_ref, branch_ref, tok_ref, q_ref, kv_ref, mixed_ref, cos_ref, sin_ref, gains_ref,
    w_query_ref, w_key_ref, w_value_ref, gh_hbm, hidden_hbm, pout_hbm, normed_hbm, wqkv_hbm, wo_hbm, dgu_hbm,
    out_ref, in_ref, dgain_ref, dq_ref, dk_ref, dv_ref, dwo_out, dgate_ref, dup_ref,
    full, tiles, wqkv, wo, gm, acc_q, acc_k, acc_v, bias, gqkv, part, sib, rcv, sib_o, rcv_o,
    land_gu, final_gu, dqkv, land_qkv, final_qkv, dwo, land_o, final_o, total, load_sem, tile_sem, *sems,
):
    n = Line(n_seq)
    rows, width = branch_ref.shape
    micro, length, q_cols = q_ref.shape
    span = rows // micro
    pair = 2 * rows
    loads = [
        pltpu.make_async_copy(src, dst, load_sem.at[i])
        for i, (src, dst) in enumerate(
            [(pout_hbm, part), (wo_hbm, wo), (wqkv_hbm, wqkv), (hidden_hbm, total), (gh_hbm, in_ref)]
        )
    ]

    def prepare():
        for load in loads:
            load.start()
        for m in range(micro):
            full[m, n.s] = branch_ref[m * span : (m + 1) * span, :]

    sems = list(sems)
    take = lambda count: [sems.pop(0) for _ in range(count)]
    gathers = [Gather(n, full, *take(3), m=m) for m in range(micro)]
    scatter = Scatter(n, part, sib, rcv, *take(4))
    scatter_out = Scatter(n, part, sib_o, rcv_o, *take(4))
    gu_sum = Collect(n, n_dp, dgu_hbm, land_gu, final_gu, *take(5))
    qkv_sum = Collect(n, n_dp, dqkv, land_qkv, final_qkv, *take(5))
    out_sum = OutSum(n, n_dp, dwo, land_o, final_o, *take(5))
    greet_all(n, n_dp, out_sum, prepare)
    gathers[0].begin()
    gu_sum.begin(3)
    loads[0].wait()
    loads[1].wait()
    late = n_seq * 5 // 8
    scatter_out.begin()
    gathers[1].begin()
    for j in range(n.n_line):
        gathers[0].visit(n.order(j))
    loads[2].wait()

    heads = q_cols // HEAD_DIM
    scale = 1.0 / math.sqrt(HEAD_DIM)
    q_tile = min(length, QUERY_TILE)
    low = low_lanes((length, q_cols + 2 * HEAD_DIM))
    here = lax.div(lax.broadcasted_iota(jnp.int32, (length, q_cols), 1), HEAD_DIM)

    def attend_back(m, h):
        key, val = head_lanes(kv_ref[m], h, q_cols)

        @pl.loop(0, length // q_tile)
        def _(i):
            at = pl.ds(pl.multiple_of(i * q_tile, q_tile), q_tile)
            query, grad = q_ref[m, at, :], gm[m, at, :]
            scores = nt(key, query) + bias_tile(bias, prefix_ref[m], 1, length, q_tile, i)
            weights = jnp.exp(scores - jnp.max(scores, axis=0, keepdims=True))
            probs = weights * (1.0 / jnp.sum(weights, axis=0, keepdims=True))
            grad_probs = nt(val, grad)
            delta = jnp.sum(probs * grad_probs, axis=0, keepdims=True)
            grad_scores = (probs * (grad_probs - delta)).astype(BF16)
            acc_q[at, :] += tn(grad_scores, key)
            acc_k[...] += jnp.where(here == h, nn(grad_scores, query), 0.0)
            acc_v[...] += jnp.where(here == h, nn(probs.astype(BF16), grad), 0.0)

    shard = dwo.shape[1]

    def out_grads():

        @pl.loop(0, width // TILE)
        def _(w):
            cols = pl.ds(pl.multiple_of(w * TILE, TILE), TILE)
            d_out = jnp.zeros((q_cols, TILE), F32)
            for m in range(micro):
                d_out = d_out + tn(mixed_ref[m], full[m, :, :, cols].reshape(length, TILE))
            dwo[:, :, cols] = d_out.astype(BF16).reshape(n_dp, shard, TILE)

        out_sum.begin()

    for m in range(micro):
        gm[m] = nt(full[m].reshape(length, width), wo[...].reshape(q_cols, width)).astype(BF16)
        fill_bias(bias, prefix_ref[m], 1, length)
        for ref in (acc_q, acc_k, acc_v):
            ref[...] = jnp.zeros_like(ref)
        for h in range(heads):
            if m + 1 < micro:
                for j in range(*spread_work(n.n_line, heads, h)):
                    gathers[m + 1].visit(n.order(j))
            if m == 0:
                for time in range(*spread_work(n.last, heads, h)):
                    scatter_out.step(time)
            if m == 1 and h == 0:
                out_grads()
            for j in range(*spread_work(late, micro * heads, m * heads + h)):
                gu_sum.reduce(j, j + 1)
            attend_back(m, h)

        def fold(ref):
            total = ref[:, : 2 * HEAD_DIM]
            for w in range(2 * HEAD_DIM, q_cols, 2 * HEAD_DIM):
                total = total + ref[:, w : w + 2 * HEAD_DIM]
            return total + pltpu.roll(total, HEAD_DIM, 1)

        first = lax.broadcasted_iota(jnp.int32, (length, 2 * HEAD_DIM), 1) < HEAD_DIM
        grads = jnp.concatenate([acc_q[...], jnp.where(first, fold(acc_k) * scale, fold(acc_v))], axis=1)
        gqkv[m] = (grads * cos_ref[...] - turn(grads, low) * sin_ref[...]).astype(BF16)

    loads[3].wait()
    scatter_out.finish(total, True)
    out_ref[...] = total[...].astype(BF16)
    for m in range(micro):

        @pl.loop(0, width // TILE)
        def _(w):
            at = pl.ds(pl.multiple_of(w * TILE, TILE), TILE)
            value = nt(gqkv[m], wqkv[at, :])
            part[:, m * span : (m + 1) * span, at] = value.astype(BF16).reshape(n_seq, span, TILE)

    scatter.begin()
    scatter.step(0)

    half = n_seq // 2
    depth = half * shard

    def fetch(w):
        cols = pl.ds(pl.multiple_of(w * depth, depth), depth)
        slot = lax.rem(w, 2)
        return pltpu.make_async_copy(normed_hbm.at[:, :, :, cols], tiles.at[slot], tile_sem.at[slot])

    fetch(jnp.int32(0)).start()

    @pl.loop(0, n_dp * 2)
    def _(w):
        pl.when(w + 1 < n_dp * 2)(lambda: fetch(w + 1).start())
        fetch(w).wait()
        slot = lax.rem(w, 2)
        d_qkv = jnp.zeros((depth, q_cols + 2 * HEAD_DIM), F32)
        for m in range(micro):
            d_qkv = d_qkv + tn(tiles[slot, m].reshape(length, depth), gqkv[m])
        at = pl.ds(pl.multiple_of(lax.rem(w, 2) * half, half), half)
        dqkv[lax.div(w, 2), at] = d_qkv.astype(BF16).reshape(half, shard, q_cols + 2 * HEAD_DIM)

    qkv_sum.begin(n_seq)
    out_sum.reduce()
    for time in range(n.last):
        if time > 0:
            scatter.step(time)
        first, end = spread_work(n_seq - late, n.last, time)
        gu_sum.reduce(late + first, late + end)
    qkv_sum.reduce(0, n_seq)
    scatter.finish(total)
    loads[4].wait()
    in_ref[...] += norm_back(tok_ref[...].astype(F32), total[...])
    gu_sum.end()
    ff_block = dgate_ref.shape[1] // (n_dp * n_seq)
    gain_attn = gains_ref[:, :1]
    for i, ref in enumerate((dgate_ref, dup_ref)):
        for owner in range(n_dp):
            for t in range(n_seq):
                cols = slice((owner * n_seq + t) * ff_block, (owner * n_seq + t + 1) * ff_block)
                first = (i * n_dp + owner) * ff_block
                ref[:, cols] = final_gu[t, :, first : first + ff_block]
    qkv_sum.end()
    repeat = n_seq // KV_HEADS
    dots = jnp.zeros((shard, 1), F32)
    for t in range(n_seq):
        cols = slice(t * q_cols, (t + 1) * q_cols)
        value = final_qkv[t, :, :q_cols].astype(F32)
        dots = dots + jnp.sum(value * w_query_ref[:, cols].astype(F32), axis=1, keepdims=True)
        dq_ref[:, cols] = value * gain_attn
    for g in range(KV_HEADS):
        cols = slice(g * HEAD_DIM, (g + 1) * HEAD_DIM)
        for i, (ref, w_ref) in enumerate(((dk_ref, w_key_ref), (dv_ref, w_value_ref))):
            lanes = slice(q_cols + i * HEAD_DIM, q_cols + (i + 1) * HEAD_DIM)
            value = final_qkv[g * repeat, :, lanes].astype(F32)
            for t in range(g * repeat + 1, (g + 1) * repeat):
                value = value + final_qkv[t, :, lanes].astype(F32)
            dots = dots + jnp.sum(value * w_ref[:, cols].astype(F32), axis=1, keepdims=True)
            ref[:, cols] = value * gain_attn
    dgain_ref[...] = dots * jnp.ones((shard, 2 * HEAD_DIM), F32)
    out_sum.end()
    dwo_out[...] = final_o[...].astype(F32)
    for gather in gathers:
        gather.end()


def backward_call(
    prefix, branch, tok, q, kv, mixed, cos, sin, gains, w_query, w_key, w_value,
    gh, hidden, pout, normed, wqkv, wo, dgu,
):
    rows, width = branch.shape
    n_dp, n_seq, shard, gu_cols = dgu.shape
    ff = gu_cols // 2 * n_seq
    micro, length, q_cols = q.shape
    qkv_cols = q_cols + 2 * HEAD_DIM
    any_spec = pl.BlockSpec(memory_space=pl.ANY)
    vmem = pl.BlockSpec(memory_space=pltpu.VMEM)
    line_rows = pltpu.VMEM((n_seq, rows, width), BF16)
    return pl.pallas_call(
        functools.partial(backward_kernel, n_seq, n_dp),
        out_shape=(
            jax.ShapeDtypeStruct((rows, width), BF16),
            jax.ShapeDtypeStruct((rows, width), F32),
            jax.ShapeDtypeStruct((shard, 2 * HEAD_DIM), F32),
            *(jax.ShapeDtypeStruct(w.shape, F32) for w in (w_query, w_key, w_value)),
            jax.ShapeDtypeStruct((shard, width), F32),
            jax.ShapeDtypeStruct((shard, ff), BF16),
            jax.ShapeDtypeStruct((shard, ff), BF16),
        ),
        in_specs=[pl.BlockSpec(memory_space=pltpu.SMEM)] + [vmem] * 11 + [any_spec] * 7,
        out_specs=(vmem,) * 9,
        scratch_shapes=[
            pltpu.VMEM((micro, n_seq, rows // micro, width), BF16),
            pltpu.VMEM((2, micro, n_seq, rows // micro, n_seq // 2 * shard), BF16),
            pltpu.VMEM((width, qkv_cols), BF16),
            pltpu.VMEM(wo.shape, BF16),
            pltpu.VMEM((micro, length, q_cols), BF16),
            pltpu.VMEM((length, q_cols), F32),
            pltpu.VMEM((length, q_cols), F32),
            pltpu.VMEM((length, q_cols), F32),
            pltpu.VMEM(bias_shape(length), F32),
            pltpu.VMEM((micro, length, qkv_cols), BF16),
            line_rows,
            *Scatter.buffers(n_seq, rows, width),
            *Scatter.buffers(n_seq, rows, width),
            pltpu.VMEM((n_dp, n_seq, shard, gu_cols), BF16),
            pltpu.VMEM((n_seq, shard, gu_cols), BF16),
            pltpu.VMEM((n_dp, n_seq, shard, qkv_cols), BF16),
            pltpu.VMEM((n_dp, n_seq, shard, qkv_cols), BF16),
            pltpu.VMEM((n_seq, shard, qkv_cols), BF16),
            pltpu.VMEM((n_dp, shard, width), BF16),
            pltpu.VMEM((n_dp, shard, width), BF16),
            pltpu.VMEM((shard, width), BF16),
            pltpu.VMEM((rows, width), F32),
            pltpu.SemaphoreType.DMA((5,)),
            pltpu.SemaphoreType.DMA((2,)),
            *Gather.sems(n_seq) * micro,
            *Scatter.sems(n_seq),
            *Scatter.sems(n_seq),
            *Collect.sems(n_seq, n_dp),
            *Collect.sems(n_seq, n_dp),
            *OutSum.sems(n_dp),
        ],
        compiler_params=pltpu.CompilerParams(
            collective_id=3, has_side_effects=True, vmem_limit_bytes=VMEM_LIMIT
        ),
        cost_estimate=pl.CostEstimate(flops=10**10, bytes_accessed=40 << 20, transcendentals=0),
        name="backward",
    )(
        prefix, branch, tok, q, kv, mixed, cos, sin, gains, w_query, w_key, w_value,
        gh, hidden, pout, normed, wqkv, wo, dgu,
    )


def finish_kernel(count, gains_ref, *refs):
    moved, (d_gate, d_up, w_gate, w_up) = refs[:count], refs[count : count + 4]
    targets = refs[count + 4 : 2 * count + 4]
    gate_hbm, up_hbm, dots_ref = refs[2 * count + 4 : 2 * count + 7]
    held = refs[2 * count + 7 : 3 * count + 7]
    grads, weights, scaled, acc, move_sem, out_sem, load_sem, save_sem = refs[3 * count + 7 :]
    loads = [
        pltpu.make_async_copy(src, dst.at[i], load_sem.at[i, k])
        for i, pair in enumerate(((d_gate, w_gate), (d_up, w_up)))
        for k, (src, dst) in enumerate(zip(pair, (grads, weights)))
    ]
    moves = [
        pltpu.make_async_copy(src, mid, move_sem.at[i]) for i, (src, mid) in enumerate(zip(moved, held))
    ]
    outs = [
        pltpu.make_async_copy(mid, dst, out_sem.at[i]) for i, (mid, dst) in enumerate(zip(held, targets))
    ]
    for copy in loads + moves:
        copy.start()
    gain = gains_ref[:, 2 * HEAD_DIM : 2 * HEAD_DIM + 1]
    shard, ff = grads.shape[1:]
    acc[...] = jnp.zeros_like(acc)
    for move, out in zip(moves, outs):
        move.wait()
        out.start()
    saves = []
    for i, dst in enumerate((gate_hbm, up_hbm)):
        loads[2 * i].wait()
        loads[2 * i + 1].wait()

        @pl.loop(0, ff // (2 * TILE))
        def _(f):
            cols = pl.ds(pl.multiple_of(f * 2 * TILE, 2 * TILE), 2 * TILE)
            value = grads[i, :, cols].astype(F32)
            scaled[i, :, cols] = value * gain
            acc[...] += value * weights[i, :, cols].astype(F32)

        saves.append(pltpu.make_async_copy(scaled.at[i], dst, save_sem.at[i]))
        saves[-1].start()
    dots_ref[...] = jnp.sum(acc[...], axis=1, keepdims=True) * jnp.ones_like(dots_ref)
    for copy in outs + saves:
        copy.wait()


def finish_call(gains, moved, d_gate, d_up, w_gate, w_up):
    count = len(moved)
    any_spec = pl.BlockSpec(memory_space=pl.ANY)
    vmem = pl.BlockSpec(memory_space=pltpu.VMEM)
    shape = d_gate.shape
    return pl.pallas_call(
        functools.partial(finish_kernel, count),
        out_shape=(
            *(jax.ShapeDtypeStruct(v.shape, v.dtype) for v in moved),
            jax.ShapeDtypeStruct(shape, F32),
            jax.ShapeDtypeStruct(shape, F32),
            jax.ShapeDtypeStruct((shape[0], 2 * HEAD_DIM), F32),
        ),
        in_specs=[vmem] + [any_spec] * (count + 4),
        out_specs=(any_spec,) * (count + 2) + (vmem,),
        scratch_shapes=[
            *(pltpu.VMEM(v.shape, v.dtype) for v in moved),
            pltpu.VMEM((2, *shape), BF16),
            pltpu.VMEM((2, *shape), BF16),
            pltpu.VMEM((2, *shape), F32),
            pltpu.VMEM((shape[0], 2 * TILE), F32),
            pltpu.SemaphoreType.DMA((count,)),
            pltpu.SemaphoreType.DMA((count,)),
            pltpu.SemaphoreType.DMA((2, 2)),
            pltpu.SemaphoreType.DMA((2,)),
        ],
        compiler_params=pltpu.CompilerParams(vmem_limit_bytes=VMEM_LIMIT),
        name="results",
    )(gains, *moved, d_gate, d_up, w_gate, w_up)


def body(
    tokens, cotangent, prefix_len, attn_gain, w_query, w_key, w_value, w_out, mlp_gain, w_gate, w_up, w_down
):
    n_dp = lax.axis_size("dp")
    n_seq = lax.axis_size("seq")
    micro, span, width = tokens.shape
    shard = w_query.shape[0]
    rows = micro * span
    cos, sin = rope_tables(span * n_seq, HEADS // n_seq * HEAD_DIM)
    gains = jnp.concatenate(
        [jnp.broadcast_to(g.astype(F32)[:, None], (shard, 2 * HEAD_DIM)) for g in (attn_gain, mlp_gain)], axis=1
    )
    tok = tokens.reshape(rows, width)
    cot = cotangent.reshape(rows, width)
    hidden, normed_mlp, q, kv, mixed, normed, cot_all, wqkv, wo, wgu, wd = attention_call(
        prefix_len, tok, cot, cos, sin, gains, w_query, w_key, w_value, w_gate, w_up, w_out, w_down, n_seq, n_dp
    )
    branch, grad_hidden, out_part, dgu, w_down_grad = mlp_call(
        normed_mlp, hidden, cot_all, wgu.reshape(width, -1), wd.reshape(-1, width), n_seq, n_dp
    )
    block_out, input_grad, attn_gain_grad, *w_grads, w_out_grad, d_gate, d_up = backward_call(
        prefix_len, branch, tok, q, kv, mixed, cos, sin, gains, w_query, w_key, w_value,
        grad_hidden, hidden, out_part, normed, wqkv.reshape(width, -1), wo.reshape(-1, width), dgu.reshape(n_dp, n_seq, shard, -1),
    )
    moved = (block_out, input_grad, *w_grads, w_out_grad, w_down_grad)
    *moved, w_gate_grad, w_up_grad, mlp_gain_grad = finish_call(gains, moved, d_gate, d_up, w_gate, w_up)
    block_out, input_grad, *w_grads, w_out_grad, w_down_grad = moved
    return (
        block_out.reshape(micro, span, width),
        input_grad.reshape(micro, span, width),
        attn_gain_grad[:, 0],
        *w_grads,
        w_out_grad,
        mlp_gain_grad[:, 0],
        w_gate_grad,
        w_up_grad,
        w_down_grad,
    )


def solution(mesh):
    rows = P("dp", "seq", None)
    vec = P(("dp", "seq"))
    mat = P(("dp", "seq"), None)
    in_specs = (rows, rows, P("dp"), vec, mat, mat, mat, mat, vec, mat, mat, mat)
    out_specs = (rows, rows, vec, mat, mat, mat, mat, vec, mat, mat, mat)
    return jax.shard_map(body, mesh=mesh, in_specs=in_specs, out_specs=out_specs, check_vma=False)
```
